32 devices in a mesh: ctx: 8 (over z, y), fsdp: 4 (over x, core).
Axes of the slice: x: 2, y: 2, z: 4, core: 2. Of those that a mesh axis runs over, the one named last changes fastest.
Arguments:
- hidden_in: float32 [4, 2048, 1024], P('fsdp', 'ctx'), may hold values from -6 to 6
- starts: int32 [4, 8], P('fsdp'), may hold values from 0 to 2047, as said below
- w_query: float32 [1024, 1024], P('fsdp'), may hold values from -0.1875 to 0.1875
- w_key: float32 [1024, 1024], P('fsdp'), may hold values from -0.1875 to 0.1875
- w_value: float32 [1024, 1024], P('fsdp'), may hold values from -0.1875 to 0.1875
- w_output: float32 [1024, 1024], P('fsdp'), may hold values from -2 to 2
- w_expand: float32 [1024, 4096], P('fsdp'), may hold values from -0.1875 to 0.1875
- w_reduce: float32 [4096, 1024], P('fsdp'), may hold values from -0.09375 to 0.09375
- bias_query: float32 [1024], replicated, may hold values from -3 to 3
- bias_value: float32 [1024], replicated, may hold values from -0.12 to 0.12
- bias_output: float32 [1024], replicated, may hold values from -1.8 to 1.8
- bias_expand: float32 [4096], replicated, may hold values from -3 to 3
- bias_reduce: float32 [1024], replicated, may hold values from -1.8 to 1.8
- attention_gain: float32 [1024], replicated, may hold values from 0.5 to 1.5
- attention_shift: float32 [1024], replicated, may hold values from -1.8 to 1.8
- feedforward_gain: float32 [1024], replicated, may hold values from 0.5 to 1.5
- feedforward_shift: float32 [1024], replicated, may hold values from -1.8 to 1.8
- cotangent: float32 [4, 2048, 1024], P('fsdp', 'ctx'), may hold values from -6 to 6
Outputs:
- layer_out: float32 [4, 2048, 1024], P('fsdp', 'ctx')
- input_grad: float32 [4, 2048, 1024], P('fsdp', 'ctx')
- grad_w_query: float32 [1024, 1024], P('fsdp')
- grad_w_key: float32 [1024, 1024], P('fsdp')
- grad_w_value: float32 [1024, 1024], P('fsdp')
- grad_w_output: float32 [1024, 1024], P('fsdp')
- grad_w_expand: float32 [1024, 4096], P('fsdp')
- grad_w_reduce: float32 [4096, 1024], P('fsdp')
- grad_bias_query: float32 [1024], P('fsdp')
- grad_bias_value: float32 [1024], P('fsdp')
- grad_bias_output: float32 [1024], P('fsdp')
- grad_bias_expand: float32 [4096], P('fsdp')
- grad_bias_reduce: float32 [1024], P('fsdp')
- grad_attention_gain: float32 [1024], P('fsdp')
- grad_attention_shift: float32 [1024], P('fsdp')
- grad_feedforward_gain: float32 [1024], P('fsdp')
- grad_feedforward_shift: float32 [1024], P('fsdp')
The draws below stay inside these ranges and needn't reach their ends.
Inputs may be any that keep to these rules, and one draw needn't show every extreme that they name: Row s holds the first tokens of the documents of stream s, not decreasing, the first one 0; equal starts mark empty documents. One document of each stream has tokens among the first 256 and among the last 256 tokens of the stream.
All inputs are finite; a program needn't handle non-finite values.
Results may differ from the reference program's by a relative error of at most 0.023.
Values may be sent and summed in bfloat16 or wider, within the bound.
No kernel may reach another device: no remote copies, remote signals or barrier semaphores. Data moves between devices by JAX's collectives and lax.ppermute only.
A program may use at most 384 MiB of HBM per device.

```python
import math
import jax
import jax.numpy as jnp
from jax import lax

D = 1024
FF = 4096
HEADS = 16
TOK_DEV = 256
STREAMS = 4
LEN = 2048


def draw_starts(key, part):
    key = jax.random.fold_in(key, 7)
    subkeys = jax.random.split(key, 4)
    long_begin = jax.random.randint(subkeys[0], (STREAMS, 1), 1, TOK_DEV)
    long_end = LEN - jax.random.randint(subkeys[1], (STREAMS, 1), 1, TOK_DEV)
    early = jax.random.randint(subkeys[2], (STREAMS, 2), 0, 1 << 20) % long_begin + 1
    later = long_end + jax.random.randint(subkeys[3], (STREAMS, 2), 0, 1 << 20) % (LEN - long_end)
    final_column = jnp.full((STREAMS, 1), LEN - 1, jnp.int32)
    zeros_column = jnp.zeros((STREAMS, 1), jnp.int32)
    joined = jnp.concatenate((zeros_column, long_begin, long_end, early, later, final_column), axis=1)
    return jnp.sort(joined, axis=1).astype(jnp.int32)


def block_levels(own_key, extent, cuts, least, largest):
    def one(position, blocks):
        draws = jax.random.uniform(jax.random.fold_in(jax.random.fold_in(own_key, 6), position), (blocks,), jnp.float32, least / len(cuts), largest / len(cuts))
        return jnp.repeat(jnp.exp(draws), extent[position] // blocks).reshape((-1,) + (1,) * (len(extent) - position - 1))

    gain = one(*cuts[0])
    for cut in cuts[1:]:
        gain = gain * one(*cut)
    return gain


def gaussian(stream_key, extent, scale, limit, cuts=(), kind=jnp.bfloat16):
    entries = scale * jax.random.normal(stream_key, extent, jnp.float32)
    if cuts:
        entries = entries * block_levels(stream_key, extent, cuts, -0.22, 0.18)
    return jnp.clip(entries, -limit, limit).astype(kind)


def setup_inputs(seed: int = 0) -> dict:
    splits = jax.random.split(jax.random.key(seed), 19)
    hidden_in = gaussian(splits[0], (STREAMS, LEN, D), 1.0, 6.0, ((0, 4), (1, 8)), jnp.float32)
    starts = draw_starts(jax.random.fold_in(splits[18], 71), 0)
    w_query = gaussian(splits[2], (D, D), D ** -0.5, 0.1875, ((0, 4),), jnp.float32)
    w_key = gaussian(splits[3], (D, D), D ** -0.5, 0.1875, ((0, 4),), jnp.float32)
    w_value = gaussian(splits[4], (D, D), D ** -0.5, 0.1875, ((0, 4),), jnp.float32)
    w_output = gaussian(splits[5], (D, D), (max(1, D * 16 // LEN)) ** -0.5, 2.0, ((0, 4),), jnp.float32)
    w_expand = gaussian(splits[6], (D, FF), D ** -0.5, 0.1875, ((0, 4),), jnp.float32)
    w_reduce = gaussian(splits[7], (FF, D), FF ** -0.5, 0.09375, ((0, 4),), jnp.float32)
    bias_query = gaussian(splits[8], (D,), 0.5, 3.0, (), jnp.float32)
    bias_value = gaussian(splits[9], (D,), 0.02, 0.12, (), jnp.float32)
    bias_output = gaussian(splits[10], (D,), 0.3, 1.8, (), jnp.float32)
    bias_expand = gaussian(splits[11], (FF,), 0.5, 3.0, (), jnp.float32)
    bias_reduce = gaussian(splits[12], (D,), 0.3, 1.8, (), jnp.float32)
    attention_gain = jnp.clip(1.0 + 0.1 * jax.random.normal(splits[13], (D,), jnp.float32), 0.5, 1.5)
    attention_shift = gaussian(splits[14], (D,), 0.3, 1.8, (), jnp.float32)
    feedforward_gain = jnp.clip(1.0 + 0.1 * jax.random.normal(splits[15], (D,), jnp.float32), 0.5, 1.5)
    feedforward_shift = gaussian(splits[16], (D,), 0.3, 1.8, (), jnp.float32)
    cotangent = gaussian(splits[17], (STREAMS, LEN, D), 1.0, 6.0, ((0, 4), (1, 8)), jnp.float32)
    return dict(hidden_in=hidden_in, starts=starts, w_query=w_query, w_key=w_key, w_value=w_value, w_output=w_output, w_expand=w_expand, w_reduce=w_reduce, bias_query=bias_query, bias_value=bias_value, bias_output=bias_output, bias_expand=bias_expand, bias_reduce=bias_reduce, attention_gain=attention_gain, attention_shift=attention_shift, feedforward_gain=feedforward_gain, feedforward_shift=feedforward_shift, cotangent=cotangent)


@jax.custom_vjp
def low(v):
    return lax.optimization_barrier(v.astype(jnp.bfloat16)).astype(jnp.float32)

@jax.custom_vjp
def low_back(v):
    return v

def low_keep(v):
    return (low(v), None)

def low_pass(kept, grad):
    return (grad,)

def back_keep(v):
    return (v, None)

def back_low(kept, grad):
    return (low(grad),)
low.defvjp(low_keep, low_pass)
low_back.defvjp(back_keep, back_low)
epsilon = 1e-05
highest = lax.Precision.HIGHEST

def product(left, right):
    return jnp.dot(left, right, precision=highest, preferred_element_type=jnp.float32)

def layer_norm(values, gain_vector, shift_vector):
    average = lax.optimization_barrier(jnp.mean(values, axis=-1, keepdims=True))
    centered = values - average
    variance = lax.optimization_barrier(jnp.mean(centered * centered, axis=-1, keepdims=True))
    return centered * lax.rsqrt(variance + epsilon) * gain_vector + shift_vector

def attention_rows(query_block, doc_block, keys_all, values_all, docs_all):
    scores = low_back(jnp.einsum('qhd,khd->qhk', query_block, keys_all, precision=highest))
    allowed = (doc_block[:, None] == docs_all[None, :])[:, None, :]
    probabilities = jax.nn.softmax(jnp.where(allowed, scores, -1e+30), axis=-1)
    return jnp.einsum('qhk,khd->qhd', low(probabilities), values_all, precision=highest)

def stream_forward(inputs, starts_row, matrices, vectors):
    query_matrix, key_matrix, value_matrix, output_matrix, expand_matrix, reduce_matrix = matrices
    bias_query, bias_value, bias_output, bias_expand, bias_reduce, attention_gain, attention_shift, feedforward_gain, feedforward_shift = vectors
    length_all = inputs.shape[0]
    model_width = inputs.shape[1]
    head_size = model_width // HEADS
    positions = lax.iota(jnp.int32, length_all)
    docs_all = lax.optimization_barrier(jnp.sum((starts_row[None, :] <= positions[:, None]).astype(jnp.int32), axis=1)) - 1
    inputs_r = low(inputs)
    queries = low(low_back((product(inputs_r, query_matrix) + bias_query) * 0.125))
    keys_all = low(low_back(product(inputs_r, key_matrix)))
    values_all = low(low_back(product(inputs_r, value_matrix) + bias_value))
    block_rows = math.gcd(512, length_all)
    block_count = length_all // block_rows
    keys_heads = keys_all.reshape(length_all, HEADS, head_size)
    values_heads = values_all.reshape(length_all, HEADS, head_size)

    def one_block(pair):
        return attention_rows(pair[0], pair[1], keys_heads, values_heads, docs_all)
    attended = lax.map(jax.checkpoint(one_block), (queries.reshape(block_count, block_rows, HEADS, head_size), docs_all.reshape(block_count, block_rows)))
    attended = low(low_back(attended.reshape(length_all, model_width)))
    attention_out = low_back(product(attended, output_matrix) + bias_output)
    normed = layer_norm(inputs + attention_out, attention_gain, attention_shift)
    expanded = low_back(product(low(normed), expand_matrix) + bias_expand)
    activated = low(jax.nn.gelu(expanded, approximate=False))
    reduced = low_back(product(activated, reduce_matrix) + bias_reduce)
    return layer_norm(normed + reduced, feedforward_gain, feedforward_shift)

def reference(hidden_in, starts, w_query, w_key, w_value, w_output, w_expand, w_reduce, bias_query, bias_value, bias_output, bias_expand, bias_reduce, attention_gain, attention_shift, feedforward_gain, feedforward_shift, cotangent):

    def forward(inputs_all, matrices, vectors):
        rounded = tuple((low(matrix) for matrix in matrices))

        def one_stream(pair):
            return stream_forward(pair[0], pair[1], rounded, vectors)
        return lax.map(jax.checkpoint(one_stream), (inputs_all, starts))
    matrices = (w_query, w_key, w_value, w_output, w_expand, w_reduce)
    vectors = (bias_query, bias_value, bias_output, bias_expand, bias_reduce, attention_gain, attention_shift, feedforward_gain, feedforward_shift)
    layer_out, pullback = jax.vjp(forward, hidden_in, matrices, vectors)
    input_grad, matrix_grads, vector_grads = pullback(cotangent)
    return (layer_out, input_grad, matrix_grads[0], matrix_grads[1], matrix_grads[2], matrix_grads[3], matrix_grads[4], matrix_grads[5], vector_grads[0], vector_grads[1], vector_grads[2], vector_grads[3], vector_grads[4], vector_grads[5], vector_grads[6], vector_grads[7], vector_grads[8])
```

```python
import functools

import jax
import jax.numpy as jnp
from jax import lax
from jax.experimental import pallas as pl
from jax.experimental.pallas import tpu as pltpu
from jax.sharding import PartitionSpec as P

HEADS = 16
LANES = 128
epsilon = 1e-05
masked_value = -1e30
query_scale = 0.125
bf16 = jnp.bfloat16
f32 = jnp.float32
vmem_limit = 56 * 1024 * 1024


def matmul(left, right):
    return jnp.dot(left, right, preferred_element_type=f32)


def left_transposed(left, right):
    return lax.dot_general(left, right, (((0,), (0,)), ((), ())), preferred_element_type=f32)


def right_transposed(left, right):
    return lax.dot_general(left, right, (((1,), (1,)), ((), ())), preferred_element_type=f32)


def swap(array, axis, mask):
    size = lax.axis_size(axis)
    return lax.ppermute(array, axis, [(i, i ^ mask) for i in range(size)])


def shape(*sizes, dtype=f32):
    return jax.ShapeDtypeStruct(sizes, dtype)


def call(body, name, out_shape, operands, scalars=None, scratch=(), aliases=None, **grid):
    count = 0 if scalars is None else 1
    if not grid:
        whole = pl.BlockSpec(memory_space=pltpu.VMEM)
        several = isinstance(out_shape, (list, tuple))
        grid = dict(
            grid=(), in_specs=[whole] * len(operands), out_specs=[whole] * len(out_shape) if several else whole
        )
    return pl.pallas_call(
        body,
        out_shape=out_shape,
        grid_spec=pltpu.PrefetchScalarGridSpec(
            num_scalar_prefetch=count, scratch_shapes=list(scratch), **grid
        ),
        input_output_aliases=aliases or {},
        compiler_params=pltpu.CompilerParams(vmem_limit_bytes=vmem_limit),
        cost_estimate=pl.CostEstimate(flops=1, bytes_accessed=1, transcendentals=0),
        name=name,
    )(*([] if scalars is None else [scalars]), *operands)


def aligned(index, size):
    return pl.ds(pl.multiple_of(index * size, size), size)


def gather_ctx(own):
    size = lax.axis_size("ctx")
    masks = [1 << i for i in range(size.bit_length() - 1)]
    blocks = {0: own}
    for mask in masks[1:]:
        for index in list(blocks):
            blocks[index | mask] = swap(blocks[index], "ctx", mask)
    for index in list(blocks):
        blocks[index | 1] = swap(blocks[index], "ctx", 1)
    return [blocks[i] for i in range(len(blocks))]


def ctx_groups():
    bits = lax.axis_size("ctx").bit_length() - 1
    groups = [(0, 2)]
    first = 1
    while first < bits:
        count = min(2, bits - first)
        groups.append((first, 1 << count))
        first += count
    return groups


def sum_split(arrays, members, place):
    rows, width = arrays[0].shape
    size = rows // members
    number = len(arrays)

    def body(place_ref, *refs):
        ins, outs, total = refs[:number], refs[number:-1], refs[-1]
        value = ins[0][...].astype(f32)
        for ref in ins[1:]:
            value = value + ref[...].astype(f32)
        total[...] = value.astype(bf16)
        for m in range(members):
            outs[m][...] = total[aligned(place_ref[0] ^ m, size), :]

    return call(
        body,
        "sum_split",
        [shape(size, width, dtype=bf16)] * members,
        arrays,
        scalars=place.reshape(1),
        scratch=[pltpu.VMEM((rows, width), bf16)],
    )


def sum_all(arrays):
    def body(*refs):
        value = refs[0][...].astype(f32)
        for ref in refs[1:-1]:
            value = value + ref[...].astype(f32)
        refs[-1][...] = value.astype(bf16)

    return call(body, "sum_all", shape(*arrays[0].shape, dtype=bf16), arrays)


def join(arrays, place):
    size, width = arrays[0].shape

    def body(place_ref, *refs):
        for m in range(len(arrays)):
            refs[-1][aligned(place_ref[0] ^ m, size), :] = refs[m][...]

    return call(
        body,
        "join",
        shape(size * len(arrays), width, dtype=bf16),
        arrays,
        scalars=place.reshape(1),
    )


def sum_ctx(arrays):
    index = lax.axis_index("ctx").astype(jnp.int32)
    groups = ctx_groups()
    for first, members in groups:
        place = (index >> first) & (members - 1)
        pieces = sum_split(arrays, members, place)
        arrays = [pieces[0]] + [swap(pieces[m], "ctx", m << first) for m in range(1, members)]
    piece = sum_all(arrays)
    for first, members in reversed(groups):
        place = (index >> first) & (members - 1)
        pieces = [piece] + [swap(piece, "ctx", m << first) for m in range(1, members)]
        if first:
            piece = join(pieces, place)
    return pieces, place


def place_rows(chunks):
    pairs = [chunk for chunk, _ in chunks]
    place = chunks[0][1]
    size, width = pairs[0][0].shape
    number = len(pairs)

    def body(place_ref, *refs):
        for k in range(number):

            @pl.when(pl.program_id(0) == k)
            def _():
                for m in range(2):
                    where = aligned(place_ref[0] ^ m, size)
                    refs[-1][where, :] = refs[2 * k + m][...].astype(f32)

    return call(
        body,
        "place_rows",
        shape(number * 2 * size, width),
        [piece for pair in pairs for piece in pair],
        scalars=place.reshape(1),
        grid=(number,),
        in_specs=[pl.BlockSpec((size, width), lambda k, s: (0, 0))] * (2 * number),
        out_specs=pl.BlockSpec((2 * size, width), lambda k, s: (k, 0)),
    )


def place_expand(first, second, place, own, shard, model):
    sizes = [first[0].shape[0], second[0].shape[0]]

    def body(scalars, a0, a1, b0, b1, expand_ref, output_ref, first_all, second_all):
        for m, ref in enumerate((a0, a1)):
            first_all[aligned(scalars[0] ^ m, sizes[0]), :] = ref[...]
        for m, ref in enumerate((b0, b1)):
            second_all[aligned(scalars[0] ^ m, sizes[1]), :] = ref[...]
        for k, (source, unit) in {
            0: (first_all, 0),
            2: (first_all, 1),
            1: (second_all, 0),
            3: (second_all, 1),
        }.items():
            expand_ref[:, aligned(scalars[1] ^ k, expand_ref.shape[1] // 4)] = source[
                unit * shard : (unit + 1) * shard, :
            ].astype(f32)
        output_ref[...] = first_all[2 * shard : 3 * shard, :].astype(f32)

    columns = first[0].shape[1]
    return call(
        body,
        "place_expand",
        [shape(shard, 4 * columns), shape(shard, model)],
        [*first, *second],
        scalars=jnp.stack((place, own)),
        scratch=[pltpu.VMEM((2 * size, columns), bf16) for size in sizes],
    )


def place_projections(pieces, scalar, rows, width):
    count = len(pieces)
    if width % LANES:
        ordered = jnp.take(jnp.stack(pieces)[:, :rows], jnp.arange(count) ^ scalar, axis=0)
        ordered = jnp.transpose(ordered, (1, 0, 2)).astype(f32)
        return tuple(
            ordered[:, :, k * width : (k + 1) * width].reshape(rows, count * width)
            for k in range(3)
        )

    def body(scalar_ref, *refs):
        for i in range(count):
            where = aligned(scalar_ref[0] ^ i, width)
            for k in range(3):
                refs[count + k][:, where] = refs[i][:rows, k * width : (k + 1) * width].astype(f32)

    return call(
        body,
        "place_projections",
        [shape(rows, count * width)] * 3,
        pieces,
        scalars=scalar.reshape(1),
    )


def project(blocks, first, weights, bias, query_docs, key_docs, own, heads, head_size, length, before):
    tokens, model = blocks[0].shape
    width = heads * head_size
    shard = weights[0].shape[0]
    number = len(blocks)
    rows = number * tokens
    tile = 256
    per_block = tokens // tile
    start = first * per_block

    def body(own_ref, *refs):
        x_refs, w_refs = refs[:number], refs[number : number + 4]
        b_ref, qd_ref, kd_ref = refs[number + 4 : number + 7]
        q_ref, k_ref, v_ref, kt_ref, x_out = refs[-5:]
        for k in range(number):

            @pl.when(pl.program_id(0) // per_block == k)
            def _():
                x_out[...] = x_refs[k][...]

        product = b_ref[...]
        for k in range(4):
            product = product + matmul(x_out[:, aligned(own_ref[0] ^ k, shard)], w_refs[k][...])
        lane = lax.broadcasted_iota(jnp.int32, (tile, LANES - head_size), 1)
        ones = jnp.where(lane < 3, 1.0, 0.0).astype(f32)
        keys = product[:, width : 2 * width]
        for h in range(heads):
            cut = slice(h * head_size, (h + 1) * head_size)
            q_ref[h] = jnp.concatenate((product[:, :width][:, cut], qd_ref[...]), 1).astype(bf16)
            k_ref[h] = jnp.concatenate((keys[:, cut], kd_ref[...]), 1).astype(bf16)
            v_ref[h] = jnp.concatenate((product[:, 2 * width :][:, cut], ones), 1).astype(bf16)
        kt_ref[...] = jnp.transpose(keys).astype(bf16)

    out = shape(heads, length, LANES, dtype=bf16)
    out_spec = pl.BlockSpec((heads, tile, LANES), lambda i, s: (0, i + start, 0))
    extra_spec = pl.BlockSpec((tile, LANES - head_size), lambda i, s: (i + start, 0))
    old = list(before) if before is not None else []

    def block_map(k, i, s):
        return (jnp.clip(i - k * per_block, 0, per_block - 1), 0)

    operands = [*blocks, *weights, bias, query_docs, key_docs, *old]
    return call(
        body,
        "project",
        [out, out, out, shape(width, length, dtype=bf16), shape(length, model, dtype=bf16)],
        operands,
        scalars=own.reshape(1),
        aliases={1 + len(operands) - 5 + k: k for k in range(5)} if old else None,
        grid=(rows // tile,),
        in_specs=[pl.BlockSpec((tile, model), functools.partial(block_map, k)) for k in range(number)]
        + [pl.BlockSpec((shard, 3 * width), lambda i, s: (0, 0))] * 4
        + [pl.BlockSpec((1, 3 * width), lambda i, s: (0, 0)), extra_spec, extra_spec]
        + [pl.BlockSpec(memory_space=pl.ANY)] * len(old),
        out_specs=[
            out_spec,
            out_spec,
            out_spec,
            pl.BlockSpec((width, tile), lambda i, s: (0, i + start)),
            pl.BlockSpec((tile, model), lambda i, s: (i + start, 0)),
        ],
    )


def three_parts(value):
    high = value.astype(bf16).astype(f32)
    rest = value - high
    middle = rest.astype(bf16).astype(f32)
    return high, middle, rest - middle


def attend(queries, keys, values, first, number, tokens, head_size, docs, after):
    heads, length, _ = keys.shape
    width = heads * head_size
    tile = 256 if length <= 4096 else 128
    per_block = tokens // tile
    start = first * per_block
    rows = number * tokens

    def body(q_ref, k_ref, v_ref, after_ref, *outs):
        wide_ref, back_ref = outs[number:]
        lane = lax.broadcasted_iota(jnp.int32, (tile, LANES), 1)
        for h in range(heads):
            query = q_ref[h]
            scores = right_transposed(query, k_ref[h])
            largest = jnp.max(scores, axis=1, keepdims=True)
            weights = jnp.exp(scores - largest).astype(bf16)
            summed = matmul(weights, v_ref[h])
            total = summed[:, head_size : head_size + 1]
            cut = slice(h * head_size, (h + 1) * head_size)
            wide_ref[:, cut] = summed[:, :head_size] / total
            parts = three_parts(-(largest + jnp.log(total)))
            back = query.astype(f32)
            for k in range(3):
                back = jnp.where(lane == head_size + docs + k, parts[k], back)
            back_ref[h] = back.astype(bf16)
        for k in range(number):

            @pl.when(pl.program_id(0) // per_block == k)
            def _():
                outs[k][...] = wide_ref[...].astype(bf16)

    def block_map(k, i):
        return (jnp.clip(i - k * per_block, 0, per_block - 1), 0)

    result = call(
        body,
        "attend",
        [shape(tokens, width, dtype=bf16)] * number
        + [shape(rows, width), shape(heads, rows, LANES, dtype=bf16)],
        [queries, keys, values, after],
        grid=(rows // tile,),
        in_specs=[
            pl.BlockSpec((heads, tile, LANES), lambda i: (0, i + start, 0)),
            pl.BlockSpec((heads, length, LANES), lambda i: (0, 0, 0)),
            pl.BlockSpec((heads, length, LANES), lambda i: (0, 0, 0)),
            pl.BlockSpec(memory_space=pl.ANY),
        ],
        out_specs=[pl.BlockSpec((tile, width), functools.partial(block_map, k)) for k in range(number)]
        + [
            pl.BlockSpec((tile, width), lambda i: (i, 0)),
            pl.BlockSpec((heads, tile, LANES), lambda i: (0, i, 0)),
        ],
    )
    return result[:number], result[number], result[number + 1]


def attend_back(queries, douts, attended, keys, values, keys_t, before, head_size, after):
    heads, length, _ = keys.shape
    rows = attended.shape[0]
    block = douts[0].shape[0]
    width = heads * head_size
    tile = 256 if length <= 4096 else 128
    number = len(douts)
    per_block = block // tile

    def body(*refs):
        q_ref, a_ref, k_ref, v_ref, kt_ref, after_ref = refs[:6]
        d_refs = refs[6 : 6 + number]
        rest = refs[6 + number :]
        if before is not None:
            old_k, old_v = rest[:2]
            rest = rest[2:]
        dq_ref, dk_ref, dv_ref, d_scratch = rest
        step = pl.program_id(0)

        @pl.when(step == 0)
        def _():
            if before is None:
                dk_ref[...] = jnp.zeros_like(dk_ref)
                dv_ref[...] = jnp.zeros_like(dv_ref)
            else:
                dk_ref[...] = old_k[...]
                dv_ref[...] = old_v[...]

        for k in range(number):

            @pl.when(step // per_block == k)
            def _():
                d_scratch[...] = d_refs[k][...].astype(f32)

        lane = lax.broadcasted_iota(jnp.int32, (tile, LANES - head_size), 1)
        for h in range(heads):
            cut = slice(h * head_size, (h + 1) * head_size)
            dout = d_scratch[:, cut]
            parts = three_parts(-jnp.sum(dout * a_ref[:, cut], axis=1, keepdims=True))
            extra = jnp.zeros((tile, LANES - head_size), f32)
            for k in range(3):
                extra = jnp.where(lane == k, parts[k], extra)
            dout = jnp.concatenate((dout, extra), axis=1).astype(bf16)
            query = q_ref[h]
            probabilities = jnp.exp(right_transposed(k_ref[h], query))
            grads = right_transposed(v_ref[h], dout)
            d_scores = (probabilities * grads).astype(bf16)
            dk_ref[:, cut] += matmul(d_scores, query)[:, :head_size]
            dv_ref[:, cut] += matmul(probabilities.astype(bf16), dout)[:, :head_size]
            dq_t = matmul(kt_ref[cut, :], d_scores)
            dq_ref[:, cut] = jnp.transpose(dq_t).astype(bf16)

    whole = pl.BlockSpec((length, width), lambda i: (0, 0))
    resident = pl.BlockSpec((heads, length, LANES), lambda i: (0, 0, 0))

    def dout_map(k, i):
        return (jnp.clip(i - k * per_block, 0, per_block - 1), 0)

    in_specs = [
        pl.BlockSpec((heads, tile, LANES), lambda i: (0, i, 0)),
        pl.BlockSpec((tile, width), lambda i: (i, 0)),
        resident,
        resident,
        pl.BlockSpec((width, length), lambda i: (0, 0)),
        pl.BlockSpec(memory_space=pl.ANY),
    ] + [pl.BlockSpec((tile, width), functools.partial(dout_map, k)) for k in range(number)]
    operands = [queries, attended, keys, values, keys_t, after, *douts]
    if before is not None:
        in_specs += [whole, whole]
        operands += list(before)
    return call(
        body,
        "attend_back",
        [shape(rows, width, dtype=bf16), shape(length, width), shape(length, width)],
        operands,
        scratch=[pltpu.VMEM((tile, width), f32)],
        grid=(rows // tile,),
        in_specs=in_specs,
        out_specs=[pl.BlockSpec((tile, width), lambda i: (i, 0)), whole, whole],
    )


def head_grads(d_queries, d_key, d_value, tokens, number):
    width = d_key.shape[1]
    count = len(d_queries)
    rows = number * tokens

    def body(*refs):
        dk_ref, dv_ref = refs[count : count + 2]
        all_ref = refs[count + 2]
        first = 0
        for ref in refs[:count]:
            all_ref[first : first + ref.shape[0], :width] = ref[...]
            first += ref.shape[0]
        all_ref[:, width : 2 * width] = dk_ref[:rows, :].astype(bf16)
        all_ref[:, 2 * width :] = dv_ref[:rows, :].astype(bf16)
        for k in range(number):
            refs[count + 3 + k][...] = all_ref[k * tokens : (k + 1) * tokens, :]

    result = call(
        body,
        "head_grads",
        [shape(rows, 3 * width, dtype=bf16)] + [shape(tokens, 3 * width, dtype=bf16)] * number,
        [*d_queries, d_key, d_value],
    )
    return result[0], result[1:]


def lane_copy(value):
    return jnp.broadcast_to(value, (value.shape[0], LANES))


def attention_norm(parts, weights, inputs, vectors, scalars, width):
    number = len(parts)
    tokens, model = inputs.shape
    shard = weights[0].shape[0]

    def body(s_ref, *refs):
        p_refs, w_refs = refs[:number], refs[number : number + 4]
        x_ref, v_ref = refs[number + 4 : number + 6]
        normed_ref, rounded_ref, unit_ref, inverse_ref, all_ref, matrix = refs[number + 6 :]
        for k in range(4):
            matrix[aligned(s_ref[1] ^ k, shard), :] = w_refs[k][...]
        value = x_ref[...] + v_ref[0:1, :]
        for i in range(number):
            all_ref[:, i * width : (i + 1) * width] = p_refs[i][...]
            value = value + matmul(p_refs[i][...], matrix[aligned(s_ref[0] ^ i, width), :])
        average = jnp.mean(value, axis=-1, keepdims=True)
        centered = value - average
        inverse = lax.rsqrt(jnp.mean(centered * centered, axis=-1, keepdims=True) + epsilon)
        unit = centered * inverse
        normed = unit * v_ref[1:2, :] + v_ref[2:3, :]
        normed_ref[...] = normed
        rounded_ref[...] = normed.astype(bf16)
        unit_ref[...] = unit
        inverse_ref[...] = lane_copy(inverse)

    return call(
        body,
        "attention_norm",
        [
            shape(tokens, model),
            shape(tokens, model, dtype=bf16),
            shape(tokens, model),
            shape(tokens, LANES),
            shape(tokens, model, dtype=bf16),
        ],
        [*parts, *weights, inputs, vectors],
        scalars=scalars,
        scratch=[pltpu.VMEM((model, model), bf16)],
    )


def feed_forward(own, sibling, expand_parts, reduce_parts, bias, f):
    tokens, model = own.shape
    shard = expand_parts[0].shape[0]
    half = reduce_parts[0].shape[0]
    tile = 256
    steps = 2 * half // tile

    def body(f_ref, a_ref, b_ref, *refs):
        w_refs, r_refs, bias_ref = refs[:4], refs[4:6], refs[6]
        act_ref, slope_ref, own_ref, other_ref, x_all = refs[7:]
        step = pl.program_id(0)

        @pl.when(step == 0)
        def _():
            for k in range(4):
                chunk = aligned(f_ref[0] ^ k, shard)
                x_all[:tokens, k * shard : (k + 1) * shard] = a_ref[:, chunk]
                x_all[tokens:, k * shard : (k + 1) * shard] = b_ref[:, chunk]
            own_ref[...] = jnp.zeros_like(own_ref)
            other_ref[...] = jnp.zeros_like(other_ref)

        value = bias_ref[...]
        for k in range(4):
            value = value + matmul(x_all[:, k * shard : (k + 1) * shard], w_refs[k][...])
        below = 0.5 + 0.5 * lax.erf(value * 0.7071067811865476)
        density = 0.3989422804014327 * jnp.exp(-0.5 * value * value)
        activated = (value * below).astype(bf16)
        act_ref[...] = activated
        slope_ref[...] = (below + value * density).astype(bf16)
        for k in range(2):

            @pl.when(step // (half // tile) == k)
            def _():
                own_ref[...] += matmul(activated[:tokens], r_refs[k][...])
                other_ref[...] += matmul(activated[tokens:], r_refs[k][...])

    per = half // tile
    wide = shape(2 * tokens, 2 * half, dtype=bf16)
    whole = pl.BlockSpec((tokens, model), lambda t, s: (0, 0))
    return call(
        body,
        "feed_forward",
        [wide, wide, shape(tokens, model), shape(tokens, model)],
        [own, sibling, *expand_parts, *reduce_parts, bias],
        scalars=f.reshape(1),
        scratch=[pltpu.VMEM((2 * tokens, model), bf16)],
        grid=(steps,),
        in_specs=[whole, whole]
        + [pl.BlockSpec((shard, tile), lambda t, s: (0, t))] * 4
        + [
            pl.BlockSpec((tile, model), lambda t, s: (jnp.minimum(t, per - 1), 0)),
            pl.BlockSpec((tile, model), lambda t, s: (jnp.maximum(t - per, 0), 0)),
            pl.BlockSpec((1, tile), lambda t, s: (0, t)),
        ],
        out_specs=[pl.BlockSpec((2 * tokens, tile), lambda t, s: (0, t))] * 2 + [whole, whole],
    )


def second_norm(normed, own, received, vectors, cotangent):
    tokens, model = normed.shape
    tile = 64

    def body(n_ref, p_ref, r_ref, v_ref, c_ref, out_ref, d_ref, rounded_ref, sums_ref):
        value = n_ref[...] + p_ref[...] + r_ref[...] + v_ref[0:1, :]
        average = jnp.mean(value, axis=-1, keepdims=True)
        centered = value - average
        inverse = lax.rsqrt(jnp.mean(centered * centered, axis=-1, keepdims=True) + epsilon)
        unit = centered * inverse
        out_ref[...] = unit * v_ref[1:2, :] + v_ref[2:3, :]
        dy = c_ref[...]
        dz = dy * v_ref[1:2, :]
        mean_dz = jnp.mean(dz, axis=-1, keepdims=True)
        mean_dzz = jnp.mean(dz * unit, axis=-1, keepdims=True)
        result = inverse * (dz - mean_dz - unit * mean_dzz)
        d_ref[...] = result
        rounded = result.astype(bf16)
        rounded_ref[...] = rounded

        @pl.when(pl.program_id(0) == 0)
        def _():
            sums_ref[...] = jnp.zeros_like(sums_ref)

        sums_ref[0:1, :] += jnp.sum(dy * unit, axis=0, keepdims=True)
        sums_ref[1:2, :] += jnp.sum(dy, axis=0, keepdims=True)
        sums_ref[2:3, :] += jnp.sum(rounded.astype(f32), axis=0, keepdims=True)

    rows = pl.BlockSpec((tile, model), lambda i: (i, 0))
    fixed = pl.BlockSpec((8, model), lambda i: (0, 0))
    return call(
        body,
        "second_norm",
        [shape(tokens, model), shape(tokens, model), shape(tokens, model, dtype=bf16), shape(8, model)],
        [normed, own, received, vectors, cotangent],
        grid=(tokens // tile,),
        in_specs=[rows, rows, rows, fixed, rows],
        out_specs=[rows, rows, rows, fixed],
    )


def feed_back(own, sibling, slope, expand_parts, reduce_parts, f):
    tokens, model = own.shape
    shard = expand_parts[0].shape[0]
    half = reduce_parts[0].shape[0]
    tile = 256
    per = half // tile
    steps = 2 * per

    def body(f_ref, a_ref, b_ref, slope_ref, *refs):
        w_refs, r_refs = refs[:4], refs[4:6]
        de_ref, sums_ref, own_ref, other_ref, d_all, dact, total = refs[6:]
        step = pl.program_id(0)

        @pl.when(step == 0)
        def _():
            d_all[:tokens, :] = a_ref[...]
            d_all[tokens:, :] = b_ref[...]
            total[...] = jnp.zeros_like(total)

        for k in range(2):

            @pl.when(step // per == k)
            def _():
                dact[...] = right_transposed(d_all[...], r_refs[k][...])

        rounded = (dact[...] * slope_ref[...].astype(f32)).astype(bf16)
        de_ref[...] = rounded
        sums_ref[...] = jnp.sum(rounded.astype(f32), axis=0, keepdims=True)
        for k in range(4):
            total[:, k * shard : (k + 1) * shard] += right_transposed(rounded, w_refs[k][...])

        @pl.when(step == steps - 1)
        def _():
            for k in range(4):
                chunk = aligned(f_ref[0] ^ k, shard)
                own_ref[:, chunk] = total[:tokens, k * shard : (k + 1) * shard]
                other_ref[:, chunk] = total[tokens:, k * shard : (k + 1) * shard]

    whole = pl.BlockSpec((tokens, model), lambda t, s: (0, 0))
    wide = pl.BlockSpec((2 * tokens, tile), lambda t, s: (0, t))
    return call(
        body,
        "feed_back",
        [
            shape(2 * tokens, 2 * half, dtype=bf16),
            shape(1, 2 * half),
            shape(tokens, model),
            shape(tokens, model),
        ],
        [own, sibling, slope, *expand_parts, *reduce_parts],
        scalars=f.reshape(1),
        scratch=[
            pltpu.VMEM((2 * tokens, model), bf16),
            pltpu.VMEM((2 * tokens, tile), f32),
            pltpu.VMEM((2 * tokens, model), f32),
        ],
        grid=(steps,),
        in_specs=[whole, whole, wide]
        + [pl.BlockSpec((shard, tile), lambda t, s: (0, t))] * 4
        + [
            pl.BlockSpec((tile, model), lambda t, s: (jnp.minimum(t, per - 1), 0)),
            pl.BlockSpec((tile, model), lambda t, s: (jnp.maximum(t - per, 0), 0)),
        ],
        out_specs=[wide, pl.BlockSpec((1, tile), lambda t, s: (0, t)), whole, whole],
    )


def first_norm_back(d_second, own, received, unit, inverse, vectors, weights, scalars, width, number):
    tokens, model = d_second.shape
    shard = weights[0].shape[0]

    def body(s_ref, d_ref, p_ref, r_ref, u_ref, i_ref, v_ref, *refs):
        w_refs = refs[:4]
        first_ref, rounded_ref, sums_ref = refs[4:7]
        outs, matrix = refs[7:-1], refs[-1]
        for k in range(4):
            matrix[aligned(s_ref[1] ^ k, shard), :] = w_refs[k][...]
        dy = d_ref[...] + p_ref[...] + r_ref[...]
        unit_value = u_ref[...]
        dz = dy * v_ref[1:2, :]
        mean_dz = jnp.mean(dz, axis=-1, keepdims=True)
        mean_dzz = jnp.mean(dz * unit_value, axis=-1, keepdims=True)
        result = i_ref[:, 0:1] * (dz - mean_dz - unit_value * mean_dzz)
        first_ref[...] = result
        rounded = result.astype(bf16)
        rounded_ref[...] = rounded
        sums_ref[...] = jnp.zeros_like(sums_ref)
        sums_ref[0:1, :] = jnp.sum(dy * unit_value, axis=0, keepdims=True)
        sums_ref[1:2, :] = jnp.sum(dy, axis=0, keepdims=True)
        sums_ref[2:3, :] = jnp.sum(rounded.astype(f32), axis=0, keepdims=True)
        for i in range(number):
            rows = matrix[aligned(s_ref[0] ^ i, width), :]
            outs[i][...] = right_transposed(rounded, rows).astype(bf16)

    result = call(
        body,
        "first_norm_back",
        [shape(tokens, model), shape(tokens, model, dtype=bf16), shape(8, model)]
        + [shape(tokens, width, dtype=bf16)] * number,
        [d_second, own, received, unit, inverse, vectors, *weights],
        scalars=scalars,
        scratch=[pltpu.VMEM((model, model), bf16)],
    )
    return result[:3], result[3:]


def input_gradient(d_first, blocks, matrix, scalar, width):
    number = len(blocks)
    tokens, model = d_first.shape
    if width % LANES:
        columns = [
            lax.dynamic_slice_in_dim(matrix, k * model + (scalar ^ i) * width, width, 1)
            for i in range(number)
            for k in range(3)
        ]
        return d_first + right_transposed(
            jnp.concatenate(blocks, axis=1), jnp.concatenate(columns, axis=1)
        )

    def body(s_ref, d_ref, m_ref, *refs):
        value = d_ref[...]
        for i in range(number):
            for k in range(3):
                where = pl.ds(pl.multiple_of(k * model + (s_ref[0] ^ i) * width, width), width)
                value = value + right_transposed(
                    refs[i][:, k * width : (k + 1) * width], m_ref[:, where]
                )
        refs[-1][...] = value

    return call(
        body,
        "input_gradient",
        shape(tokens, model),
        [d_first, matrix, *blocks],
        scalars=scalar.reshape(1),
    )


def cast_projections(matrices, after):
    rows, model = matrices[0].shape

    def body(q_ref, k_ref, v_ref, after_ref, out_ref):
        out_ref[:, :model] = (q_ref[...] * query_scale).astype(bf16)
        out_ref[:, model : 2 * model] = k_ref[...].astype(bf16)
        out_ref[:, 2 * model :] = v_ref[...].astype(bf16)

    whole = pl.BlockSpec((rows, model), lambda: (0, 0))
    return call(
        body,
        "cast_projections",
        shape(rows, 3 * model, dtype=bf16),
        [*matrices, after],
        grid=(),
        in_specs=[whole] * 3 + [pl.BlockSpec(memory_space=pl.ANY)],
        out_specs=pl.BlockSpec((rows, 3 * model), lambda: (0, 0)),
    )


def padded(vectors):
    return jnp.concatenate((jnp.stack(vectors), jnp.zeros((8 - len(vectors), vectors[0].shape[0]), f32)))


def per_device(
    hidden_in,
    starts,
    w_query,
    w_key,
    w_value,
    w_output,
    w_expand,
    w_reduce,
    bias_query,
    bias_value,
    bias_output,
    bias_expand,
    bias_reduce,
    attention_gain,
    attention_shift,
    feedforward_gain,
    feedforward_shift,
    cotangent,
):
    tokens, model = hidden_in.shape[1:]
    head_size = model // HEADS
    ctx_size = lax.axis_size("ctx")
    length = tokens * ctx_size
    near = min(ctx_size, HEADS)
    copies = ctx_size // near
    heads = HEADS // near
    width = heads * head_size
    shard = w_query.shape[0]
    ff_block = w_reduce.shape[0]
    documents = starts.shape[1]
    c = lax.axis_index("ctx").astype(jnp.int32)
    f = lax.axis_index("fsdp").astype(jnp.int32)
    group = c & (near - 1)
    both = jnp.stack((group, f))

    inputs = hidden_in[0]
    blocks = gather_ctx(inputs.astype(bf16))

    own_columns = jnp.concatenate(
        [
            lax.dynamic_slice_in_dim(m, group * width, width, 1) * scale
            for m, scale in ((w_query, query_scale), (w_key, 1.0), (w_value, 1.0))
        ],
        axis=1,
    ).astype(bf16)

    def gather_rows(own):
        rows = own.shape[0]
        across = swap(own, "fsdp", 2)
        others = swap(jnp.concatenate((own, across), axis=0), "fsdp", 1)
        return [own, others[:rows], across, others[rows:]]

    projection_parts = gather_rows(own_columns)
    output_parts = gather_rows(w_output.astype(bf16))

    def expand_columns(order):
        return jnp.concatenate(
            [lax.dynamic_slice_in_dim(w_expand, (f ^ k) * ff_block, ff_block, 1) for k in order],
            axis=1,
        ).astype(bf16)

    expand_own = expand_columns((0, 2))
    expand_flipped = expand_columns((2, 0))
    sibling_flipped = swap(expand_columns((3, 1)), "fsdp", 1)
    expand_sibling = jnp.concatenate(
        (sibling_flipped[:, ff_block:], sibling_flipped[:, :ff_block]), axis=1
    )
    expand_parts = [
        expand_own,
        expand_sibling,
        swap(expand_flipped, "fsdp", 2),
        swap(sibling_flipped, "fsdp", 2),
    ]
    reduce_r = w_reduce.astype(bf16)
    reduce_parts = [reduce_r, swap(reduce_r, "fsdp", 2)]
    expand_bias = jnp.concatenate(
        [lax.dynamic_slice_in_dim(bias_expand, (f ^ k) * ff_block, ff_block, 0) for k in (0, 2)]
    ).reshape(1, -1)

    order = c ^ lax.iota(jnp.int32, ctx_size)
    positions = (order[:, None] * tokens + lax.iota(jnp.int32, tokens)[None, :]).reshape(-1)
    docs = jnp.sum((starts[0][None, :] <= positions[:, None]).astype(jnp.int32), axis=1) - 1
    lane = lax.iota(jnp.int32, LANES - head_size)[None, :]
    same = docs[:, None] == lane
    query_docs = jnp.where((lane < documents) & ~same, masked_value, 0.0).astype(f32)
    key_docs = jnp.where(same | ((lane >= documents) & (lane < documents + 3)), 1.0, 0.0).astype(f32)
    own_bias = jnp.concatenate(
        (
            lax.dynamic_slice_in_dim(bias_query * query_scale, group * width, width, 0),
            jnp.zeros((width,), f32),
            lax.dynamic_slice_in_dim(bias_value, group * width, width, 0),
        )
    ).reshape(1, -1)
    attention_vectors = padded((bias_output, attention_gain, attention_shift))
    feed_vectors = padded((bias_reduce, feedforward_gain, feedforward_shift))

    state = None
    for first in range(0, ctx_size, 2):
        state = project(
            blocks[first : first + 2],
            first,
            projection_parts,
            own_bias,
            query_docs,
            key_docs,
            f,
            heads,
            head_size,
            length,
            state,
        )
    queries, keys, values, keys_t, stream = state
    all_projection = lax.all_gather(
        cast_projections((w_query, w_key, w_value), queries), "fsdp", axis=0, tiled=True
    )

    half = near // 2
    parts = [None] * near
    kept = [None, None]
    after = queries
    for part in (1, 0):
        outs, wide, back = attend(
            queries, keys, values, part * half, half, tokens, head_size, documents, after
        )
        after = wide
        kept[part] = (wide, back)
        for k in range(half):
            index = part * half + k
            parts[index] = outs[k] if index == 0 else swap(outs[k], "ctx", index)
    normed, normed_r, first_unit, first_inverse, attended_r = attention_norm(
        parts, output_parts, inputs, attention_vectors, both, width
    )

    sibling_normed = swap(normed_r, "fsdp", 1)
    activated_r, slope, partial, other = feed_forward(
        normed_r, sibling_normed, expand_parts, reduce_parts, expand_bias, f
    )
    layer_out, d_second, d_reduced_r, second_sums = second_norm(
        normed, partial, swap(other, "fsdp", 1), feed_vectors, cotangent[0]
    )
    sibling_reduced = swap(d_reduced_r, "fsdp", 1)
    pair_reduced = jnp.concatenate((d_reduced_r, sibling_reduced), axis=0)
    pair_normed = jnp.concatenate((normed_r, sibling_normed), axis=0)

    cut = ff_block // 2

    def reduce_rows(first):
        return left_transposed(activated_r[:, first : first + cut], pair_reduced).astype(bf16)

    reduce_received = [swap(reduce_rows(ff_block + k * cut), "fsdp", 2) for k in range(2)]
    d_expanded_r, bias_expand_sum, partial, other = feed_back(
        d_reduced_r, sibling_reduced, slope, expand_parts, reduce_parts, f
    )
    (d_first, d_attention_r, first_sums), d_attended = first_norm_back(
        d_second,
        partial,
        swap(other, "fsdp", 1),
        first_unit,
        first_inverse,
        attention_vectors,
        output_parts,
        both,
        width,
        near,
    )
    douts = [d_attended[0]] + [swap(d_attended[i], "ctx", i) for i in range(1, near)]

    def expand_unit(row_block, column_block):
        rows = lax.dynamic_slice_in_dim(pair_normed, (f ^ row_block) * shard, shard, 1)
        columns = d_expanded_r[:, column_block * ff_block : (column_block + 1) * ff_block]
        return left_transposed(rows, columns).astype(bf16)

    def expand_units(row_block, flip):
        return jnp.concatenate([expand_unit(row_block, k ^ flip) for k in range(2)], axis=0)

    expand_received = [swap(expand_units(k, 1), "fsdp", 2) for k in (2, 3)]
    expand_other = sum_all([expand_units(1, 0), expand_received[1]])
    expand_mine = expand_units(0, 0)

    grad_output = left_transposed(attended_r, d_attention_r).astype(bf16)
    per_shard = shard // width

    def output_rows(index):
        return [
            lax.dynamic_slice_in_dim(
                grad_output, ((index * per_shard + e) ^ group) * width, width, 0
            )
            for e in range(per_shard)
        ]

    received = swap(jnp.concatenate(output_rows(f ^ 1) + output_rows(f ^ 3), axis=0), "fsdp", 1)
    output_sum = sum_all([jnp.concatenate(output_rows(f) + output_rows(f ^ 2), axis=0), received])
    output_received = swap(output_sum[shard:], "fsdp", 2)

    unit = 16 * ctx_size

    def pad_rows(arrays):
        rows = sum(a.shape[0] for a in arrays)
        missing = -rows % unit
        if missing:
            arrays = [*arrays, jnp.zeros((missing, arrays[0].shape[1]), bf16)]
        return jnp.concatenate(arrays, axis=0) if len(arrays) > 1 else arrays[0]

    chunk_terms = [
        [reduce_rows(0), reduce_received[0]],
        [reduce_rows(cut), reduce_received[1]],
        [pad_rows([expand_mine, output_sum[:shard]]), pad_rows([expand_received[0], output_received])],
        [swap(expand_other, "fsdp", 1)],
    ]
    chunks = [sum_ctx(terms) for terms in chunk_terms]
    grad_w_reduce = place_rows(chunks[:2])
    grad_w_expand, grad_w_output = place_expand(
        chunks[2][0], chunks[3][0], chunks[3][1], f, shard, model
    )

    bias_expand_all = jnp.zeros((4 * ff_block,), f32)
    for k in range(2):
        bias_expand_all = lax.dynamic_update_slice_in_dim(
            bias_expand_all,
            bias_expand_sum[0, k * ff_block : (k + 1) * ff_block],
            (f ^ (2 * k)) * ff_block,
            0,
        )
    vectors = jnp.concatenate(
        (first_sums[:3].reshape(-1), second_sums[:3].reshape(-1), bias_expand_all)
    ).reshape(-1, LANES)
    masks = [1 << i for i in range(ctx_size.bit_length() - 1)]
    for axis, mask in [("fsdp", 1), ("fsdp", 2)] + [("ctx", mask) for mask in masks]:
        vectors = vectors + swap(vectors, axis, mask)
    vectors = vectors.reshape(-1)
    grad_att_gain, grad_att_shift, grad_bias_output, grad_ff_gain, grad_ff_shift, grad_bias_reduce = [
        lax.dynamic_slice_in_dim(vectors[k * model : (k + 1) * model], f * shard, shard, 0)
        for k in range(6)
    ]
    grad_bias_expand = lax.dynamic_slice_in_dim(vectors[6 * model :], f * ff_block, ff_block, 0)

    before = None
    d_queries = []
    after = d_attended[0]
    for part in (0, 1):
        wide, back = kept[part]
        d_query, d_key, d_value = attend_back(
            back,
            douts[part * half : (part + 1) * half],
            wide,
            keys,
            values,
            keys_t,
            before,
            head_size,
            after,
        )
        before = (d_key, d_value)
        after = d_query
        d_queries.append(d_query)
    count = ctx_size
    while count > near:
        count //= 2
        received = [
            swap(d[count * tokens :].astype(bf16), "ctx", count).astype(f32) for d in (d_key, d_value)
        ]
        d_key = d_key[: count * tokens] + received[0]
        d_value = d_value[: count * tokens] + received[1]
    d_all, d_blocks = head_grads(d_queries, d_key, d_value, tokens, near)

    scales = jnp.concatenate((jnp.full((width,), query_scale, f32), jnp.ones((2 * width,), f32)))
    grad_projection = (left_transposed(stream[: near * tokens], d_all) * scales).astype(bf16)
    bias_rows = jnp.broadcast_to(jnp.sum(d_all.astype(f32), axis=0) * scales, (16, 3 * width)).astype(
        bf16
    )

    def projection_rows(index):
        return lax.dynamic_slice_in_dim(grad_projection, index * shard, shard, 0)

    received = swap(
        jnp.concatenate((projection_rows(f ^ 3), projection_rows(f ^ 1), bias_rows), axis=0),
        "fsdp",
        1,
    )
    mine = jnp.concatenate((projection_rows(f ^ 2), projection_rows(f), bias_rows), axis=0)
    mine = sum_all([mine, received])
    received = swap(jnp.concatenate((mine[:shard], mine[2 * shard :]), axis=0), "fsdp", 2)
    mine = sum_all([mine[shard:], received])
    count = ctx_size
    while count > near:
        count //= 2
        mine = sum_all([mine, swap(mine, "ctx", count)])
    pieces = gather_ctx(mine)[:near]
    grad_query, grad_key, grad_value = place_projections(pieces, group, shard, width)
    bias_all = jnp.stack([piece[shard] for piece in pieces]).astype(f32)
    bias_all = jnp.take(bias_all, group ^ lax.iota(jnp.int32, near), axis=0)
    grad_bias_query = lax.dynamic_slice_in_dim(bias_all[:, :width].reshape(-1), f * shard, shard, 0)
    grad_bias_value = lax.dynamic_slice_in_dim(
        bias_all[:, 2 * width :].reshape(-1), f * shard, shard, 0
    )

    mine = [d_blocks[0]] + [swap(d_blocks[i], "ctx", i) for i in range(1, near)]
    input_grad = input_gradient(d_first, mine, all_projection, group, width)

    return (
        layer_out[None],
        input_grad[None],
        grad_query,
        grad_key,
        grad_value,
        grad_w_output,
        grad_w_expand,
        grad_w_reduce,
        grad_bias_query,
        grad_bias_value,
        grad_bias_output,
        grad_bias_expand,
        grad_bias_reduce,
        grad_att_gain,
        grad_att_shift,
        grad_ff_gain,
        grad_ff_shift,
    )


def solution(mesh):
    rows = P("fsdp", None)
    activations = P("fsdp", "ctx", None)
    return jax.shard_map(
        per_device,
        mesh=mesh,
        in_specs=(activations,) + (rows,) * 7 + (P(),) * 9 + (activations,),
        out_specs=(activations, activations) + (rows,) * 6 + (P("fsdp"),) * 9,
        check_vma=False,
    )
```

```python
import functools

import jax
import jax.numpy as jnp
from jax import lax
from jax.experimental import pallas as pl
from jax.experimental.pallas import tpu as pltpu
from jax.sharding import PartitionSpec as P

HEADS = 16
LANES = 128
epsilon = 1e-05
masked_value = -1e30
query_scale = 0.125
bf16 = jnp.bfloat16
f32 = jnp.float32
vmem_limit = 28 * 1024 * 1024


def matmul(left, right):
    return jnp.dot(left, right, preferred_element_type=f32)


def left_transposed(left, right):
    return lax.dot_general(left, right, (((0,), (0,)), ((), ())), preferred_element_type=f32)


def right_transposed(left, right):
    return lax.dot_general(left, right, (((1,), (1,)), ((), ())), preferred_element_type=f32)


def swap(array, axis, mask):
    size = lax.axis_size(axis)
    return lax.ppermute(array, axis, [(i, i ^ mask) for i in range(size)])


def shape(*sizes, dtype=f32):
    return jax.ShapeDtypeStruct(sizes, dtype)


class Order:
    last = ()


def call(
    body, name, out_shape, operands, scalars=None, scratch=(), aliases=None, deps=(), limit=vmem_limit, **grid
):
    count = 0 if scalars is None else 1
    several = isinstance(out_shape, (list, tuple))
    if not grid:
        whole = pl.BlockSpec(memory_space=pltpu.VMEM)
        grid = dict(
            grid=(),
            in_specs=[whole] * len(operands),
            out_specs=[whole] * len(out_shape) if several else whole,
        )
    extra = [*Order.last, *deps]
    first = count + len(operands)
    grid["in_specs"] = list(grid["in_specs"]) + [pl.BlockSpec(memory_space=pl.ANY)] * len(extra)

    def ordered(*refs):
        body(*refs[:first], *refs[first + len(extra) :])

    result = pl.pallas_call(
        ordered,
        out_shape=out_shape,
        grid_spec=pltpu.PrefetchScalarGridSpec(
            num_scalar_prefetch=count, scratch_shapes=list(scratch), **grid
        ),
        input_output_aliases=aliases or {},
        compiler_params=pltpu.CompilerParams(vmem_limit_bytes=limit),
        cost_estimate=pl.CostEstimate(flops=1, bytes_accessed=1, transcendentals=0),
        name=name,
    )(*([] if scalars is None else [scalars]), *operands, *extra)
    Order.last = (result[0] if several else result,)
    return result


def aligned(index, size):
    return pl.ds(pl.multiple_of(index * size, size), size)


def gather_ctx(own):
    size = lax.axis_size("ctx")
    masks = [1 << i for i in range(size.bit_length() - 1)]
    blocks = {0: own}
    for mask in reversed(masks[1:]):
        for index in list(blocks):
            blocks[index | mask] = swap(blocks[index], "ctx", mask)
    for index in list(blocks):
        if index != 2:
            blocks[index | 1] = swap(blocks[index], "ctx", 1)
    blocks[3] = swap(blocks[1], "ctx", 2)
    return [blocks[i] for i in range(len(blocks))]


def exchange(array, number):
    size = lax.axis_size("ctx")
    if number == size:
        return lax.all_to_all(array, "ctx", 0, 0, tiled=True)
    rows = array.shape[0] // number
    own = lax.axis_index("ctx").astype(jnp.int32) & (number - 1)
    result = jnp.zeros_like(array)
    for i in range(number):
        block = lax.dynamic_slice_in_dim(array, (own ^ i) * rows, rows, 0)
        block = block if i == 0 else swap(block, "ctx", i)
        result = lax.dynamic_update_slice_in_dim(result, block, (own ^ i) * rows, 0)
    return result


def ctx_groups():
    return [(bit, 2) for bit in range(lax.axis_size("ctx").bit_length() - 1)]


def piece_of(index, size):
    bits = size.bit_length() - 1
    piece = 0
    for bit in range(bits):
        piece = piece | (((index >> bit) & 1) << (bits - 1 - bit))
    return piece


def sum_split(segments, members, place, rows, deps):
    width = segments[0][0][0].shape[1]
    size = rows // members
    number = sum(len(arrays) for arrays, _, _ in segments)

    def body(place_ref, *refs):
        ins, outs, total = refs[:number], refs[number:-1], refs[-1]
        first = at = 0
        for arrays, begin, end in segments:
            value = ins[at][begin:end, :].astype(f32)
            for ref in ins[at + 1 : at + len(arrays)]:
                value = value + ref[begin:end, :].astype(f32)
            total[first : first + end - begin, :] = value.astype(bf16)
            first += end - begin
            at += len(arrays)
        if first < rows:
            total[first:, :] = jnp.zeros((rows - first, width), bf16)
        for m in range(members):
            outs[m][...] = total[aligned(place_ref[0] ^ m, size), :]

    return call(
        body,
        "sum_split",
        [shape(size, width, dtype=bf16)] * members,
        [array for arrays, _, _ in segments for array in arrays],
        deps=deps,
        scalars=place.reshape(1),
        scratch=[pltpu.VMEM((rows, width), bf16)],
    )


def sum_all(arrays, dtype=bf16):
    def body(*refs):
        value = refs[0][...].astype(f32)
        for ref in refs[1:-1]:
            value = value + ref[...].astype(f32)
        refs[-1][...] = value.astype(dtype)

    return call(body, "sum_all", shape(*arrays[0].shape, dtype=dtype), arrays)


class CtxSum:
    def __init__(self, groups, *segments):
        self.index = lax.axis_index("ctx").astype(jnp.int32)
        self.groups = list(groups)
        self.segments = segments
        unit = 16
        for _, members in groups:
            unit *= members
        self.rows = -(-sum(end - begin for _, begin, end in segments) // unit) * unit

    def step(self, deps=()):
        if not self.groups:
            return
        first, members = self.groups.pop(0)
        place = (self.index >> first) & (members - 1)
        pieces = sum_split(self.segments, members, place, self.rows, deps)
        self.rows //= members
        arrays = [pieces[0]] + [swap(pieces[m], "ctx", m << first) for m in range(1, members)]
        self.segments = [(arrays, 0, self.rows)]

    def finish(self):
        while self.groups:
            self.step()
        return self.segments[0][0]


def place_rows(gathered, size):
    rows, width = gathered.shape

    def body(in_ref, out_ref):
        out_ref[...] = in_ref[...].astype(f32)

    return call(
        body,
        "place_rows",
        shape(rows, width),
        [gathered],
        grid=(size,),
        in_specs=[pl.BlockSpec((rows // size, width), lambda p: (piece_of(p, size), 0))],
        out_specs=pl.BlockSpec((rows // size, width), lambda p: (p, 0)),
    )


def place_expand(gathered, f, shard, size):
    rows, columns = gathered.shape
    piece = rows // size

    def body(f_ref, in_ref, expand_ref, output_ref, *refs):
        outs, ordered, small = refs[:-2], refs[-2], refs[-1]
        for j in range(size):
            at = piece_of(j, size) * piece
            ordered[at : at + piece, :] = in_ref[j * piece : (j + 1) * piece, :]
        for unit, k in enumerate((0, 2, 1, 3)):
            expand_ref[:, aligned(f_ref[0] ^ k, columns)] = ordered[
                unit * shard : (unit + 1) * shard, :
            ].astype(f32)
        output_ref[...] = ordered[4 * shard : 5 * shard, :].astype(f32)
        small[...] = ordered[5 * shard : 5 * shard + 16, :].astype(f32)
        for k in range(6):
            outs[k][...] = small[k : k + 1, aligned(f_ref[0], shard)]
        outs[6][...] = small[pl.ds(8 + f_ref[0], 1), :]

    return call(
        body,
        "place_expand",
        [shape(shard, 4 * columns), shape(shard, columns)]
        + [shape(1, shard)] * 6
        + [shape(1, columns)],
        [gathered],
        scalars=f.reshape(1),
        scratch=[pltpu.VMEM((rows, columns), bf16), pltpu.VMEM((16, columns), f32)],
    )


def cast_feed(expand, reduce):
    shard, columns = expand.shape
    block = columns // 4

    def body(e_ref, r_ref, out_ref):
        at = pl.program_id(0)

        @pl.when(at < 4)
        def _():
            out_ref[...] = e_ref[...].astype(bf16)

        @pl.when(at >= 4)
        def _():
            out_ref[...] = r_ref[...].astype(bf16)

    return call(
        body,
        "cast_feed",
        shape(4 * shard + reduce.shape[0], block, dtype=bf16),
        [expand, reduce],
        grid=(8,),
        in_specs=[
            pl.BlockSpec((shard, block), lambda i: (0, jnp.minimum(i, 3))),
            pl.BlockSpec((reduce.shape[0] // 4, block), lambda i: (jnp.maximum(i - 4, 0), 0)),
        ],
        out_specs=pl.BlockSpec((shard, block), lambda i: (i, 0)),
    )


def cast_all(matrix, deps=()):
    rows, columns = matrix.shape
    tile = min(rows, 256)

    def body(in_ref, out_ref):
        out_ref[...] = in_ref[...].astype(bf16)

    spec = pl.BlockSpec((tile, columns), lambda i: (i, 0))
    return call(
        body,
        "cast_all",
        shape(rows, columns, dtype=bf16),
        [matrix],
        deps=deps,
        grid=(rows // tile,),
        in_specs=[spec],
        out_specs=spec,
    )


def reduce_gradient(activated, own, sibling, half, deps=()):
    rows, columns = activated.shape
    tokens, model = own.shape
    tile = columns // 4

    def body(h_ref, a_ref, d_ref, s_ref, out_ref):
        value = left_transposed(a_ref[:tokens, :], d_ref[...])
        out_ref[...] = (value + left_transposed(a_ref[tokens:, :], s_ref[...])).astype(bf16)

    whole = pl.BlockSpec((tokens, model), lambda i, s: (0, 0))
    return call(
        body,
        "reduce_gradient",
        shape(columns // 2, model, dtype=bf16),
        [activated, own, sibling],
        deps=deps,
        scalars=half.reshape(1),
        grid=(2,),
        in_specs=[pl.BlockSpec((rows, tile), lambda i, s: (0, 2 * i + s[0])), whole, whole],
        out_specs=pl.BlockSpec((tile, model), lambda i, s: (i, 0)),
    )


def expand_gradients(own, sibling, d_expanded, f, row_blocks, flip, shard):
    tokens, model = own.shape
    columns = d_expanded.shape[1] // 2

    def body(f_ref, a_ref, b_ref, d_ref, out_ref):
        value = left_transposed(a_ref[...], d_ref[:tokens, :])
        out_ref[...] = (value + left_transposed(b_ref[...], d_ref[tokens:, :])).astype(bf16)

    def rows_map(i, s):
        return (0, s[0] ^ jnp.where(i < 2, row_blocks[0], row_blocks[1]))

    left = pl.BlockSpec((tokens, shard), rows_map)
    return call(
        body,
        "expand_gradients",
        shape(4 * shard, columns, dtype=bf16),
        [own, sibling, d_expanded],
        scalars=f.reshape(1),
        grid=(4,),
        in_specs=[left, left, pl.BlockSpec((2 * tokens, columns), lambda i, s: (0, (i % 2) ^ flip))],
        out_specs=pl.BlockSpec((shard, columns), lambda i, s: (i, 0)),
    )


def output_gradient(attended, d_attention, first_sums, second_sums, bias_sums, f, shard):
    model = d_attention.shape[1]
    tile = 256
    steps = model // tile

    def body(s_ref, a_ref, d_ref, first_ref, second_ref, bias_ref, keep_ref, send_ref, rows, small):
        step = pl.program_id(0)
        rows[aligned(step, tile), :] = left_transposed(a_ref[...], d_ref[...]).astype(bf16)

        @pl.when(step == steps - 1)
        def _():
            small[...] = jnp.zeros_like(small)
            small[0:3, :] = first_ref[0:3, :]
            small[3:6, :] = second_ref[0:3, :]
            for k in range(2):
                small[pl.ds(8 + (s_ref[0] ^ (2 * k)), 1), :] = bias_ref[
                    :, k * model : (k + 1) * model
                ]
            for out_ref, blocks in ((keep_ref, (0, 2)), (send_ref, (1, 3))):
                for k, block in enumerate(blocks):
                    out_ref[k * shard : (k + 1) * shard, :] = rows[
                        aligned(s_ref[0] ^ block, shard), :
                    ]
                out_ref[2 * shard :, :] = small[...].astype(bf16)

    total = 2 * shard + 16
    whole = pl.BlockSpec((total, model), lambda i, s: (0, 0))
    return call(
        body,
        "output_gradient",
        [shape(total, model, dtype=bf16)] * 2,
        [attended, d_attention, first_sums, second_sums, bias_sums],
        scalars=f.reshape(1),
        scratch=[pltpu.VMEM((model, model), bf16), pltpu.VMEM((16, model), f32)],
        grid=(steps,),
        in_specs=[pl.BlockSpec((attended.shape[0], tile), lambda i, s: (0, i))]
        + [
            pl.BlockSpec(array.shape, lambda i, s: (0, 0))
            for array in (d_attention, first_sums, second_sums, bias_sums)
        ],
        out_specs=[whole, whole],
    )


def add_parts(first, second, parts):
    width = first.shape[1]

    def body(a_ref, b_ref, *outs):
        for out_ref, ranges in zip(outs, parts):
            at = 0
            for begin, end in ranges:
                value = a_ref[begin:end, :].astype(f32) + b_ref[begin:end, :].astype(f32)
                out_ref[at : at + end - begin, :] = value.astype(bf16)
                at += end - begin

    return call(
        body,
        "add_parts",
        [shape(sum(e - b for b, e in ranges), width, dtype=bf16) for ranges in parts],
        [first, second],
    )


def projection_gradients(stream, d_all, f, shard):
    rows, width = d_all.shape
    model = stream.shape[1]
    tile = 512
    steps = rows // tile

    def body(f_ref, x_ref, d_ref, send_ref, keep_ref, total, sums, rounded):
        step = pl.program_id(0)

        @pl.when(step == 0)
        def _():
            total[...] = jnp.zeros_like(total)
            sums[...] = jnp.zeros_like(sums)

        d_value = d_ref[...]
        total[...] += left_transposed(x_ref[...], d_value)
        sums[...] += jnp.sum(d_value.astype(f32), axis=0, keepdims=True)

        @pl.when(step == steps - 1)
        def _():
            lane = lax.broadcasted_iota(jnp.int32, (1, width), 1)
            scale = jnp.where(lane < width // 3, query_scale, 1.0)
            rounded[...] = (total[...] * scale).astype(bf16)
            bias = jnp.broadcast_to(sums[...] * scale, (16, width)).astype(bf16)
            for out_ref, blocks in ((send_ref, (3, 1)), (keep_ref, (2, 0))):
                for k, block in enumerate(blocks):
                    out_ref[k * shard : (k + 1) * shard, :] = rounded[
                        aligned(f_ref[0] ^ block, shard), :
                    ]
                out_ref[2 * shard :, :] = bias

    out = shape(2 * shard + 16, width, dtype=bf16)
    whole = pl.BlockSpec((2 * shard + 16, width), lambda i, s: (0, 0))
    return call(
        body,
        "projection_gradients",
        [out, out],
        [stream, d_all],
        scalars=f.reshape(1),
        scratch=[
            pltpu.VMEM((model, width), f32),
            pltpu.VMEM((1, width), f32),
            pltpu.VMEM((model, width), bf16),
        ],
        grid=(steps,),
        in_specs=[
            pl.BlockSpec((tile, model), lambda i, s: (i, 0)),
            pl.BlockSpec((tile, width), lambda i, s: (i, 0)),
        ],
        out_specs=[whole, whole],
    )


def place_projections(gathered, f, count, width, shard):
    rows = gathered.shape[0] // count

    def body(f_ref, in_ref, *refs):
        outs, sums = refs[:-1], refs[-1]
        for j in range(count):
            where = slice(j * width, (j + 1) * width)
            for k in range(3):
                cut = slice(k * width, (k + 1) * width)
                outs[k][:, where] = in_ref[j * rows : j * rows + shard, cut].astype(f32)
                sums[k : k + 1, where] = in_ref[j * rows + shard : (j + 1) * rows, cut].astype(f32)[
                    0:1, :
                ]
        for k, row in ((3, 0), (4, 2)):
            outs[k][...] = sums[row : row + 1, aligned(f_ref[0], shard)]

    return call(
        body,
        "place_projections",
        [shape(shard, count * width)] * 3 + [shape(1, shard)] * 2,
        [gathered],
        scalars=f.reshape(1),
        scratch=[pltpu.VMEM((8, count * width), f32)],
    )


def project(blocks, first, weights, bias, query_docs, key_docs, own, heads, head_size, length, before, deps):
    tokens, model = blocks[0].shape
    width = heads * head_size
    shard = weights[0].shape[0]
    number = len(blocks)
    rows = number * tokens
    tile = 256
    per_block = tokens // tile
    start = first * per_block

    def body(own_ref, *refs):
        x_refs, w_refs = refs[:number], refs[number : number + 4]
        b_ref, qd_ref, kd_ref = refs[number + 4 : number + 7]
        q_ref, k_ref, v_ref, kt_ref, x_out = refs[-5:]
        for k in range(number):

            @pl.when(pl.program_id(0) // per_block == k)
            def _():
                x_out[...] = x_refs[k][...]

        product = b_ref[...]
        for k in range(4):
            product = product + matmul(x_out[:, aligned(own_ref[0] ^ k, shard)], w_refs[k][...])
        lane = lax.broadcasted_iota(jnp.int32, (tile, LANES - head_size), 1)
        ones = jnp.where(lane < 3, 1.0, 0.0).astype(f32)
        keys = product[:, width : 2 * width]
        for h in range(heads):
            cut = slice(h * head_size, (h + 1) * head_size)
            q_ref[h] = jnp.concatenate((product[:, :width][:, cut], qd_ref[...]), 1).astype(bf16)
            k_ref[h] = jnp.concatenate((keys[:, cut], kd_ref[...]), 1).astype(bf16)
            v_ref[h] = jnp.concatenate((product[:, 2 * width :][:, cut], ones), 1).astype(bf16)
        kt_ref[...] = jnp.transpose(keys).astype(bf16)

    out = shape(heads, length, LANES, dtype=bf16)
    out_spec = pl.BlockSpec((heads, tile, LANES), lambda i, s: (0, i + start, 0))
    extra_spec = pl.BlockSpec((tile, LANES - head_size), lambda i, s: (i + start, 0))
    old = list(before) if before is not None else []

    def block_map(k, i, s):
        return (jnp.clip(i - k * per_block, 0, per_block - 1), 0)

    operands = [*blocks, *weights, bias, query_docs, key_docs, *old]
    return call(
        body,
        "project",
        [out, out, out, shape(width, length, dtype=bf16), shape(length, model, dtype=bf16)],
        operands,
        scalars=own.reshape(1),
        deps=deps,
        aliases={1 + len(operands) - 5 + k: k for k in range(5)} if old else None,
        grid=(rows // tile,),
        in_specs=[pl.BlockSpec((tile, model), functools.partial(block_map, k)) for k in range(number)]
        + [pl.BlockSpec((shard, 3 * width), lambda i, s: (0, 0))] * 4
        + [pl.BlockSpec((1, 3 * width), lambda i, s: (0, 0)), extra_spec, extra_spec]
        + [pl.BlockSpec(memory_space=pl.ANY)] * len(old),
        out_specs=[
            out_spec,
            out_spec,
            out_spec,
            pl.BlockSpec((width, tile), lambda i, s: (0, i + start)),
            pl.BlockSpec((tile, model), lambda i, s: (i + start, 0)),
        ],
    )


def three_parts(value):
    high = value.astype(bf16).astype(f32)
    rest = value - high
    middle = rest.astype(bf16).astype(f32)
    return high, middle, rest - middle


def attend(queries, keys, values, group, number, tokens, head_size, docs, deps):
    heads, length, _ = keys.shape
    width = heads * head_size
    tile = 256 if length <= 4096 else 128
    per = tokens // tile
    rows = number * tokens

    def body(s_ref, q_ref, k_ref, v_ref, out_ref, wide_ref, back_ref):
        lane = lax.broadcasted_iota(jnp.int32, (tile, LANES), 1)
        for h in range(heads):
            query = q_ref[h]
            scores = right_transposed(query, k_ref[h])
            largest = jnp.max(scores, axis=1, keepdims=True)
            weights = jnp.exp(scores - largest).astype(bf16)
            summed = matmul(weights, v_ref[h])
            total = summed[:, head_size : head_size + 1]
            cut = slice(h * head_size, (h + 1) * head_size)
            attended = summed[:, :head_size] / total
            wide_ref[:, cut] = attended
            out_ref[:, cut] = attended.astype(bf16)
            parts = three_parts(-(largest + jnp.log(total)))
            back = query.astype(f32)
            for k in range(3):
                back = jnp.where(lane == head_size + docs + k, parts[k], back)
            back_ref[h] = back.astype(bf16)

    return call(
        body,
        "attend",
        [
            shape(rows, width, dtype=bf16),
            shape(rows, width),
            shape(heads, rows, LANES, dtype=bf16),
        ],
        [queries, keys, values],
        deps=deps,
        scalars=group.reshape(1),
        grid=(rows // tile,),
        in_specs=[
            pl.BlockSpec((heads, tile, LANES), lambda i, s: (0, i, 0)),
            pl.BlockSpec((heads, length, LANES), lambda i, s: (0, 0, 0)),
            pl.BlockSpec((heads, length, LANES), lambda i, s: (0, 0, 0)),
        ],
        out_specs=[
            pl.BlockSpec((tile, width), lambda i, s: (((i // per) ^ s[0]) * per + i % per, 0)),
            pl.BlockSpec((tile, width), lambda i, s: (i, 0)),
            pl.BlockSpec((heads, tile, LANES), lambda i, s: (0, i, 0)),
        ],
    )


def attend_back(queries, douts, attended, keys, values, keys_t, head_size, tokens, group):
    heads, length, _ = keys.shape
    rows = attended.shape[0]
    width = heads * head_size
    tile = 256 if length <= 4096 else 128
    per = tokens // tile

    def body(s_ref, q_ref, d_ref, a_ref, k_ref, v_ref, kt_ref, dq_ref, dk_ref, dv_ref):
        @pl.when(pl.program_id(0) == 0)
        def _():
            dk_ref[...] = jnp.zeros_like(dk_ref)
            dv_ref[...] = jnp.zeros_like(dv_ref)

        lane = lax.broadcasted_iota(jnp.int32, (tile, LANES - head_size), 1)
        for h in range(heads):
            cut = slice(h * head_size, (h + 1) * head_size)
            dout = d_ref[:, cut].astype(f32)
            parts = three_parts(-jnp.sum(dout * a_ref[:, cut], axis=1, keepdims=True))
            extra = jnp.zeros((tile, LANES - head_size), f32)
            for k in range(3):
                extra = jnp.where(lane == k, parts[k], extra)
            dout = jnp.concatenate((dout, extra), axis=1).astype(bf16)
            query = q_ref[h]
            probabilities = jnp.exp(right_transposed(k_ref[h], query))
            grads = right_transposed(v_ref[h], dout)
            d_scores = (probabilities * grads).astype(bf16)
            dk_ref[:, cut] += matmul(d_scores, query)[:, :head_size]
            dv_ref[:, cut] += matmul(probabilities.astype(bf16), dout)[:, :head_size]
            dq_t = matmul(kt_ref[cut, :], d_scores)
            dq_ref[:, cut] = jnp.transpose(dq_t).astype(bf16)

    whole = pl.BlockSpec((length, width), lambda i, s: (0, 0))
    resident = pl.BlockSpec((heads, length, LANES), lambda i, s: (0, 0, 0))

    def dout_map(i, s):
        return (((i // per) ^ s[0]) * per + i % per, 0)

    in_specs = [
        pl.BlockSpec((heads, tile, LANES), lambda i, s: (0, i, 0)),
        pl.BlockSpec((tile, width), dout_map),
        pl.BlockSpec((tile, width), lambda i, s: (i, 0)),
        resident,
        resident,
        pl.BlockSpec((width, length), lambda i, s: (0, 0)),
    ]
    operands = [queries, douts, attended, keys, values, keys_t]
    return call(
        body,
        "attend_back",
        [shape(rows, width, dtype=bf16), shape(length, width), shape(length, width)],
        operands,
        scalars=group.reshape(1),
        limit=vmem_limit if length <= 4096 else 2 * vmem_limit,
        grid=(rows // tile,),
        in_specs=in_specs,
        out_specs=[pl.BlockSpec((tile, width), lambda i, s: (i, 0)), whole, whole],
    )


def head_grads(d_queries, d_key, d_value, tokens, number, group):
    width = d_key.shape[1]
    count = len(d_queries)
    rows = number * tokens

    def body(s_ref, *refs):
        dk_ref, dv_ref, all_ref, send_ref = refs[count:]
        first = 0
        for ref in refs[:count]:
            all_ref[first : first + ref.shape[0], :width] = ref[...]
            first += ref.shape[0]
        all_ref[:, width : 2 * width] = dk_ref[:rows, :].astype(bf16)
        all_ref[:, 2 * width :] = dv_ref[:rows, :].astype(bf16)
        for k in range(number):
            send_ref[aligned(s_ref[0] ^ k, tokens), :] = all_ref[k * tokens : (k + 1) * tokens, :]

    return call(
        body,
        "head_grads",
        [shape(rows, 3 * width, dtype=bf16)] * 2,
        [*d_queries, d_key, d_value],
        scalars=group.reshape(1),
    )


def lane_copy(value):
    return jnp.broadcast_to(value, (value.shape[0], LANES))


def attention_norm(received, weights, inputs, vectors, f, number):
    tokens, model = inputs.shape
    shard = weights[0].shape[0]
    width = received.shape[1]

    def body(f_ref, p_ref, *refs):
        w_refs = refs[:4]
        x_ref, v_ref = refs[4:6]
        normed_ref, rounded_ref, unit_ref, inverse_ref, all_ref, matrix = refs[6:]
        for k in range(4):
            matrix[aligned(f_ref[0] ^ k, shard), :] = w_refs[k][...]
        for j in range(number):
            all_ref[:, j * width : (j + 1) * width] = p_ref[j * tokens : (j + 1) * tokens, :]
        value = x_ref[...] + v_ref[0:1, :] + matmul(all_ref[...], matrix[...])
        average = jnp.mean(value, axis=-1, keepdims=True)
        centered = value - average
        inverse = lax.rsqrt(jnp.mean(centered * centered, axis=-1, keepdims=True) + epsilon)
        unit = centered * inverse
        normed = unit * v_ref[1:2, :] + v_ref[2:3, :]
        normed_ref[...] = normed
        rounded_ref[...] = normed.astype(bf16)
        unit_ref[...] = unit
        inverse_ref[...] = lane_copy(inverse)

    return call(
        body,
        "attention_norm",
        [
            shape(tokens, model),
            shape(tokens, model, dtype=bf16),
            shape(tokens, model),
            shape(tokens, LANES),
            shape(tokens, model, dtype=bf16),
        ],
        [received, *weights, inputs, vectors],
        scalars=f.reshape(1),
        scratch=[pltpu.VMEM((model, model), bf16)],
    )


def feed_specs(shard, model):
    tile = 2 * shard

    def block(t, s):
        return s[0] ^ (2 * (t // 2))

    specs = [
        pl.BlockSpec((shard, tile), lambda t, s, k=k: (8 * k + block(t, s), t % 2)) for k in range(4)
    ]
    specs.append(pl.BlockSpec((tile, model), lambda t, s: (4 * block(t, s) + 2 + t % 2, 0)))
    return specs, lambda t, s: 2 * block(t, s) + t % 2


def feed_forward(own, sibling, matrix, bias, f):
    tokens, model = own.shape
    shard = model // 4
    tile = 2 * shard

    def body(f_ref, a_ref, b_ref, *refs):
        w_refs, r_ref, bias_ref = refs[:4], refs[4], refs[5]
        act_ref, slope_ref, own_ref, other_ref, x_all = refs[6:]

        @pl.when(pl.program_id(0) == 0)
        def _():
            x_all[:tokens, :] = a_ref[...]
            x_all[tokens:, :] = b_ref[...]
            own_ref[...] = jnp.zeros_like(own_ref)
            other_ref[...] = jnp.zeros_like(other_ref)

        value = bias_ref[...]
        for k in range(4):
            value = value + matmul(x_all[:, k * shard : (k + 1) * shard], w_refs[k][...])
        below = 0.5 + 0.5 * lax.erf(value * 0.7071067811865476)
        density = 0.3989422804014327 * jnp.exp(-0.5 * value * value)
        activated = (value * below).astype(bf16)
        act_ref[...] = activated
        slope_ref[...] = (below + value * density).astype(bf16)
        own_ref[...] += matmul(activated[:tokens], r_ref[...])
        other_ref[...] += matmul(activated[tokens:], r_ref[...])

    specs, column = feed_specs(shard, model)
    wide = shape(2 * tokens, 4 * tile, dtype=bf16)
    whole = pl.BlockSpec((tokens, model), lambda t, s: (0, 0))
    return call(
        body,
        "feed_forward",
        [wide, wide, shape(tokens, model), shape(tokens, model)],
        [own, sibling, *[matrix] * 5, bias],
        scalars=f.reshape(1),
        limit=2 * vmem_limit,
        scratch=[pltpu.VMEM((2 * tokens, model), bf16)],
        grid=(4,),
        in_specs=[whole, whole, *specs, pl.BlockSpec((1, tile), lambda t, s: (0, column(t, s)))],
        out_specs=[pl.BlockSpec((2 * tokens, tile), lambda t, s: (0, t))] * 2 + [whole, whole],
    )


def second_norm(normed, own, received, vectors, cotangent):
    tokens, model = normed.shape
    tile = 64

    def body(n_ref, p_ref, r_ref, v_ref, c_ref, out_ref, d_ref, rounded_ref, sums_ref):
        value = n_ref[...] + p_ref[...] + r_ref[...] + v_ref[0:1, :]
        average = jnp.mean(value, axis=-1, keepdims=True)
        centered = value - average
        inverse = lax.rsqrt(jnp.mean(centered * centered, axis=-1, keepdims=True) + epsilon)
        unit = centered * inverse
        out_ref[...] = unit * v_ref[1:2, :] + v_ref[2:3, :]
        dy = c_ref[...]
        dz = dy * v_ref[1:2, :]
        mean_dz = jnp.mean(dz, axis=-1, keepdims=True)
        mean_dzz = jnp.mean(dz * unit, axis=-1, keepdims=True)
        result = inverse * (dz - mean_dz - unit * mean_dzz)
        d_ref[...] = result
        rounded = result.astype(bf16)
        rounded_ref[...] = rounded

        @pl.when(pl.program_id(0) == 0)
        def _():
            sums_ref[...] = jnp.zeros_like(sums_ref)

        sums_ref[0:1, :] += jnp.sum(dy * unit, axis=0, keepdims=True)
        sums_ref[1:2, :] += jnp.sum(dy, axis=0, keepdims=True)
        sums_ref[2:3, :] += jnp.sum(rounded.astype(f32), axis=0, keepdims=True)

    rows = pl.BlockSpec((tile, model), lambda i: (i, 0))
    fixed = pl.BlockSpec((8, model), lambda i: (0, 0))
    return call(
        body,
        "second_norm",
        [shape(tokens, model), shape(tokens, model), shape(tokens, model, dtype=bf16), shape(8, model)],
        [normed, own, received, vectors, cotangent],
        grid=(tokens // tile,),
        in_specs=[rows, rows, rows, fixed, rows],
        out_specs=[rows, rows, rows, fixed],
    )


def feed_back(own, sibling, slope, matrix, f):
    tokens, model = own.shape
    shard = model // 4
    tile = 2 * shard

    def body(f_ref, a_ref, b_ref, slope_ref, *refs):
        w_refs, r_ref = refs[:4], refs[4]
        de_ref, sums_ref, own_ref, other_ref, d_all = refs[5:]

        @pl.when(pl.program_id(0) == 0)
        def _():
            d_all[:tokens, :] = a_ref[...]
            d_all[tokens:, :] = b_ref[...]
            own_ref[...] = jnp.zeros_like(own_ref)
            other_ref[...] = jnp.zeros_like(other_ref)

        value = right_transposed(d_all[...], r_ref[...])
        rounded = (value * slope_ref[...].astype(f32)).astype(bf16)
        de_ref[...] = rounded
        sums_ref[...] = jnp.sum(rounded.astype(f32), axis=0, keepdims=True)
        for k in range(4):
            cut = slice(k * shard, (k + 1) * shard)
            own_ref[:, cut] += right_transposed(rounded[:tokens], w_refs[k][...])
            other_ref[:, cut] += right_transposed(rounded[tokens:], w_refs[k][...])

    specs, _ = feed_specs(shard, model)
    whole = pl.BlockSpec((tokens, model), lambda t, s: (0, 0))
    wide = pl.BlockSpec((2 * tokens, tile), lambda t, s: (0, t))
    return call(
        body,
        "feed_back",
        [
            shape(2 * tokens, 4 * tile, dtype=bf16),
            shape(1, 4 * tile),
            shape(tokens, model),
            shape(tokens, model),
        ],
        [own, sibling, slope, *[matrix] * 5],
        scalars=f.reshape(1),
        limit=2 * vmem_limit,
        scratch=[pltpu.VMEM((2 * tokens, model), bf16)],
        grid=(4,),
        in_specs=[whole, whole, wide, *specs],
        out_specs=[wide, pl.BlockSpec((1, tile), lambda t, s: (0, t)), whole, whole],
    )


def first_norm_back(d_second, own, received, unit, inverse, vectors, weights, f, number):
    tokens, model = d_second.shape
    shard = weights[0].shape[0]
    width = model // number

    def body(f_ref, d_ref, p_ref, r_ref, u_ref, i_ref, v_ref, *refs):
        w_refs = refs[:4]
        first_ref, rounded_ref, sums_ref, out_ref, matrix = refs[4:]
        for k in range(4):
            matrix[aligned(f_ref[0] ^ k, shard), :] = w_refs[k][...]
        dy = d_ref[...] + p_ref[...] + r_ref[...]
        unit_value = u_ref[...]
        dz = dy * v_ref[1:2, :]
        mean_dz = jnp.mean(dz, axis=-1, keepdims=True)
        mean_dzz = jnp.mean(dz * unit_value, axis=-1, keepdims=True)
        result = i_ref[:, 0:1] * (dz - mean_dz - unit_value * mean_dzz)
        first_ref[...] = result
        rounded = result.astype(bf16)
        rounded_ref[...] = rounded
        sums_ref[...] = jnp.zeros_like(sums_ref)
        sums_ref[0:1, :] = jnp.sum(dy * unit_value, axis=0, keepdims=True)
        sums_ref[1:2, :] = jnp.sum(dy, axis=0, keepdims=True)
        sums_ref[2:3, :] = jnp.sum(rounded.astype(f32), axis=0, keepdims=True)
        d_attended = right_transposed(rounded, matrix[...]).astype(bf16)
        for j in range(number):
            out_ref[j * tokens : (j + 1) * tokens, :] = d_attended[:, j * width : (j + 1) * width]

    return call(
        body,
        "first_norm_back",
        [
            shape(tokens, model),
            shape(tokens, model, dtype=bf16),
            shape(8, model),
            shape(number * tokens, width, dtype=bf16),
        ],
        [d_second, own, received, unit, inverse, vectors, *weights],
        scalars=f.reshape(1),
        scratch=[pltpu.VMEM((model, model), bf16)],
    )


def input_gradient(d_first, received, matrix, number):
    tokens, model = d_first.shape
    width = received.shape[1] // 3

    def body(d_ref, m_ref, r_ref, out_ref, ordered):
        for j in range(number):
            for k in range(3):
                ordered[:, k * model + j * width : k * model + (j + 1) * width] = r_ref[
                    j * tokens : (j + 1) * tokens, k * width : (k + 1) * width
                ]
        out_ref[...] = d_ref[...] + right_transposed(ordered[...], m_ref[...])

    return call(
        body,
        "input_gradient",
        shape(tokens, model),
        [d_first, matrix, received],
        scratch=[pltpu.VMEM((tokens, 3 * model), bf16)],
    )


def cast_projections(matrices, deps):
    rows, model = matrices[0].shape

    def body(q_ref, k_ref, v_ref, out_ref):
        out_ref[:, :model] = (q_ref[...] * query_scale).astype(bf16)
        out_ref[:, model : 2 * model] = k_ref[...].astype(bf16)
        out_ref[:, 2 * model :] = v_ref[...].astype(bf16)

    whole = pl.BlockSpec((rows, model), lambda: (0, 0))
    return call(
        body,
        "cast_projections",
        shape(rows, 3 * model, dtype=bf16),
        [*matrices],
        deps=deps,
        grid=(),
        in_specs=[whole] * 3,
        out_specs=pl.BlockSpec((rows, 3 * model), lambda: (0, 0)),
    )


def padded(vectors):
    return jnp.concatenate((jnp.stack(vectors), jnp.zeros((8 - len(vectors), vectors[0].shape[0]), f32)))


def per_device(
    hidden_in,
    starts,
    w_query,
    w_key,
    w_value,
    w_output,
    w_expand,
    w_reduce,
    bias_query,
    bias_value,
    bias_output,
    bias_expand,
    bias_reduce,
    attention_gain,
    attention_shift,
    feedforward_gain,
    feedforward_shift,
    cotangent,
):
    Order.last = ()
    tokens, model = hidden_in.shape[1:]
    head_size = model // HEADS
    ctx_size = lax.axis_size("ctx")
    length = tokens * ctx_size
    near = min(ctx_size, HEADS)
    copies = ctx_size // near
    heads = HEADS // near
    width = heads * head_size
    shard = w_query.shape[0]
    ff_block = w_reduce.shape[0]
    documents = starts.shape[1]
    c = lax.axis_index("ctx").astype(jnp.int32)
    f = lax.axis_index("fsdp").astype(jnp.int32)
    group = c & (near - 1)

    inputs = hidden_in[0]
    feed_matrix = lax.all_gather(cast_feed(w_expand, w_reduce), "fsdp", axis=0, tiled=True)
    blocks = gather_ctx(cast_all(inputs))

    own_columns = jnp.concatenate(
        [
            lax.dynamic_slice_in_dim(m, group * width, width, 1) * scale
            for m, scale in ((w_query, query_scale), (w_key, 1.0), (w_value, 1.0))
        ],
        axis=1,
    ).astype(bf16)

    def gather_rows(own):
        across = swap(own, "fsdp", 2)
        return [own, swap(own, "fsdp", 1), across, swap(across, "fsdp", 1)]

    projection_parts = gather_rows(own_columns)

    output_parts = gather_rows(cast_all(w_output, [blocks[1], blocks[2], blocks[4]]))

    all_projection = lax.all_gather(
        cast_projections((w_query, w_key, w_value), ()), "fsdp", axis=0, tiled=True
    )

    order = c ^ lax.iota(jnp.int32, ctx_size)
    positions = (order[:, None] * tokens + lax.iota(jnp.int32, tokens)[None, :]).reshape(-1)
    docs = jnp.sum((starts[0][None, :] <= positions[:, None]).astype(jnp.int32), axis=1) - 1
    lane = lax.iota(jnp.int32, LANES - head_size)[None, :]
    same = docs[:, None] == lane
    query_docs = jnp.where((lane < documents) & ~same, masked_value, 0.0).astype(f32)
    key_docs = jnp.where(same | ((lane >= documents) & (lane < documents + 3)), 1.0, 0.0).astype(f32)
    own_bias = jnp.concatenate(
        (
            lax.dynamic_slice_in_dim(bias_query * query_scale, group * width, width, 0),
            jnp.zeros((width,), f32),
            lax.dynamic_slice_in_dim(bias_value, group * width, width, 0),
        )
    ).reshape(1, -1)
    attention_vectors = padded((bias_output, attention_gain, attention_shift))
    feed_vectors = padded((bias_reduce, feedforward_gain, feedforward_shift))

    queries, keys, values, keys_t, stream = project(
        blocks,
        0,
        projection_parts,
        own_bias,
        query_docs,
        key_docs,
        f,
        heads,
        head_size,
        length,
        None,
        (),
    )

    out, wide, back = attend(
        queries, keys, values, group, near, tokens, head_size, documents, output_parts[1:]
    )
    received = exchange(out, near)
    normed, normed_r, first_unit, first_inverse, attended_r = attention_norm(
        received, output_parts, inputs, attention_vectors, f, near
    )

    sibling_normed = swap(normed_r, "fsdp", 1)
    activated_r, slope, partial, other = feed_forward(
        normed_r, sibling_normed, feed_matrix, bias_expand.reshape(1, -1), f
    )
    layer_out, d_second, d_reduced_r, second_sums = second_norm(
        normed, partial, swap(other, "fsdp", 1), feed_vectors, cotangent[0]
    )
    sibling_reduced = swap(d_reduced_r, "fsdp", 1)

    d_expanded_r, bias_expand_sum, partial, other = feed_back(
        d_reduced_r, sibling_reduced, slope, feed_matrix, f
    )
    other = swap(other, "fsdp", 1)

    expand_send = expand_gradients(normed_r, sibling_normed, d_expanded_r, f, (2, 3), 1, shard)
    expand_received = swap(expand_send, "fsdp", 2)
    d_first, d_attention_r, first_sums, d_attended = first_norm_back(
        d_second,
        partial,
        other,
        first_unit,
        first_inverse,
        attention_vectors,
        output_parts,
        f,
        near,
    )
    douts = exchange(d_attended, near)
    output_keep, output_send = output_gradient(
        attended_r, d_attention_r, first_sums, second_sums, bias_expand_sum, f, shard
    )
    output_received = swap(output_send, "fsdp", 1)
    low = c & 1
    reduce_keep = reduce_gradient(activated_r, d_reduced_r, sibling_reduced, low)
    expand_keep = expand_gradients(normed_r, sibling_normed, d_expanded_r, f, (0, 1), 0, shard)
    reduce_send = reduce_gradient(activated_r, d_reduced_r, sibling_reduced, 1 - low, [douts])
    reduce_received = swap(reduce_send, "ctx", 1)

    rest = (2 * shard, 2 * shard + 16)
    d_query, d_key, d_value = attend_back(
        back, douts, wide, keys, values, keys_t, head_size, tokens, group
    )
    output_keep, output_send = add_parts(
        output_keep, output_received, [[(0, shard), rest], [(shard, 2 * shard), rest]]
    )
    output_received = swap(output_send, "fsdp", 2)
    count = ctx_size
    while count > near:
        count //= 2
        received = [
            swap(d[count * tokens :].astype(bf16), "ctx", count).astype(f32) for d in (d_key, d_value)
        ]
        d_key = d_key[: count * tokens] + received[0]
        d_value = d_value[: count * tokens] + received[1]
    d_all, d_send = head_grads([d_query], d_key, d_value, tokens, near, group)
    d_mine = exchange(d_send, near)

    send, keep = projection_gradients(stream, d_all, f, shard)
    received = swap(send, "fsdp", 1)
    (expand_send,) = add_parts(expand_keep, expand_received, [[(2 * shard, 4 * shard)]])
    expand_other = swap(expand_send, "fsdp", 1)
    send, keep = add_parts(keep, received, [[(0, shard), rest], [(shard, 2 * shard), rest]])
    received = swap(send, "fsdp", 2)
    cut = ff_block // 2
    reduce_keep, reduce_send = add_parts(
        reduce_keep, reduce_received, [[(0, cut)], [(cut, 2 * cut)]]
    )
    reduce_received = swap(reduce_send, "fsdp", 2)
    groups = ctx_groups()
    expander = CtxSum(
        groups,
        ([expand_keep, expand_received], 0, 2 * shard),
        ([expand_other], 0, 2 * shard),
        ([output_keep, output_received], 0, shard + 16),
    )
    mine = sum_all([keep, received])
    count = ctx_size
    while count > near:
        count //= 2
        mine = sum_all([mine, swap(mine, "ctx", count)])
    projections = lax.all_gather(mine, "ctx", axis=0, tiled=True)
    expander.step([d_mine])
    reducer = CtxSum(groups[1:], ([reduce_keep, reduce_received], 0, cut))
    input_grad = input_gradient(d_first, d_mine, all_projection, near)
    reducer.step()
    reducer.step()
    expander.step()
    reduced = lax.all_gather(sum_all(reducer.finish()), "ctx", axis=0, tiled=True)
    expander.step()
    expanded = lax.all_gather(sum_all(expander.finish()), "ctx", axis=0, tiled=True)
    grad_query, grad_key, grad_value, grad_bias_query, grad_bias_value = place_projections(
        projections[: near * (shard + 16)], f, near, width, shard
    )
    grad_w_reduce = place_rows(reduced, ctx_size)
    grad_w_expand, grad_w_output, *small = place_expand(expanded, f, shard, ctx_size)
    (
        grad_bias_query,
        grad_bias_value,
        grad_att_gain,
        grad_att_shift,
        grad_bias_output,
        grad_ff_gain,
        grad_ff_shift,
        grad_bias_reduce,
        grad_bias_expand,
    ) = [v.reshape(-1) for v in (grad_bias_query, grad_bias_value, *small)]

    return (
        layer_out[None],
        input_grad[None],
        grad_query,
        grad_key,
        grad_value,
        grad_w_output,
        grad_w_expand,
        grad_w_reduce,
        grad_bias_query,
        grad_bias_value,
        grad_bias_output,
        grad_bias_expand,
        grad_bias_reduce,
        grad_att_gain,
        grad_att_shift,
        grad_ff_gain,
        grad_ff_shift,
    )


def solution(mesh):
    rows = P("fsdp", None)
    activations = P("fsdp", "ctx", None)
    return jax.shard_map(
        per_device,
        mesh=mesh,
        in_specs=(activations,) + (rows,) * 7 + (P(),) * 9 + (activations,),
        out_specs=(activations, activations) + (rows,) * 6 + (P("fsdp"),) * 9,
        check_vma=False,
    )
```

```python
import functools

import jax
import jax.numpy as jnp
from jax import lax
from jax.experimental import pallas as pl
from jax.experimental.pallas import tpu as pltpu
from jax.sharding import PartitionSpec as P

HEADS = 16
LANES = 128
epsilon = 1e-05
masked_value = -1e30
query_scale = 0.125
bf16 = jnp.bfloat16
f32 = jnp.float32
vmem_limit = 28 * 1024 * 1024


def matmul(left, right):
    return jnp.dot(left, right, preferred_element_type=f32)


def left_transposed(left, right):
    return lax.dot_general(left, right, (((0,), (0,)), ((), ())), preferred_element_type=f32)


def right_transposed(left, right):
    return lax.dot_general(left, right, (((1,), (1,)), ((), ())), preferred_element_type=f32)


def swap(array, axis, mask):
    size = lax.axis_size(axis)
    return lax.ppermute(array, axis, [(i, i ^ mask) for i in range(size)])


def shape(*sizes, dtype=f32):
    return jax.ShapeDtypeStruct(sizes, dtype)


class Order:
    last = ()


def call(
    body, name, out_shape, operands, scalars=None, scratch=(), aliases=None, deps=(), limit=vmem_limit, **grid
):
    count = 0 if scalars is None else 1
    several = isinstance(out_shape, (list, tuple))
    if not grid:
        whole = pl.BlockSpec(memory_space=pltpu.VMEM)
        grid = dict(
            grid=(),
            in_specs=[whole] * len(operands),
            out_specs=[whole] * len(out_shape) if several else whole,
        )
    extra = [*Order.last, *deps]
    first = count + len(operands)
    grid["in_specs"] = list(grid["in_specs"]) + [pl.BlockSpec(memory_space=pl.ANY)] * len(extra)

    def ordered(*refs):
        body(*refs[:first], *refs[first + len(extra) :])

    result = pl.pallas_call(
        ordered,
        out_shape=out_shape,
        grid_spec=pltpu.PrefetchScalarGridSpec(
            num_scalar_prefetch=count, scratch_shapes=list(scratch), **grid
        ),
        input_output_aliases=aliases or {},
        compiler_params=pltpu.CompilerParams(vmem_limit_bytes=limit),
        cost_estimate=pl.CostEstimate(flops=1, bytes_accessed=1, transcendentals=0),
        name=name,
    )(*([] if scalars is None else [scalars]), *operands, *extra)
    Order.last = (result[0] if several else result,)
    return result


def aligned(index, size):
    return pl.ds(pl.multiple_of(index * size, size), size)


def gather_ctx(own):
    size = lax.axis_size("ctx")
    masks = [1 << i for i in range(size.bit_length() - 1)]
    blocks = {0: own}
    for mask in reversed(masks[1:]):
        for index in list(blocks):
            blocks[index | mask] = swap(blocks[index], "ctx", mask)
    for index in list(blocks):
        if index != 2:
            blocks[index | 1] = swap(blocks[index], "ctx", 1)
    blocks[3] = swap(blocks[1], "ctx", 2)
    return [blocks[i] for i in range(len(blocks))]


def gather_small(own, number):
    blocks = {0: own}
    for index in range(2, number, 2):
        blocks[index] = swap(own, "ctx", index)
    for index in list(blocks):
        blocks[index | 1] = swap(blocks[index], "ctx", 1)
    return [blocks[i] for i in range(number)]


def exchange(array, number):
    size = lax.axis_size("ctx")
    if number == size:
        return lax.all_to_all(array, "ctx", 0, 0, tiled=True)
    rows = array.shape[0] // number
    own = lax.axis_index("ctx").astype(jnp.int32) & (number - 1)
    result = jnp.zeros_like(array)
    for i in range(number):
        block = lax.dynamic_slice_in_dim(array, (own ^ i) * rows, rows, 0)
        block = block if i == 0 else swap(block, "ctx", i)
        result = lax.dynamic_update_slice_in_dim(result, block, (own ^ i) * rows, 0)
    return result


def ctx_groups(together=1):
    bits = lax.axis_size("ctx").bit_length() - 1
    groups, first = [(0, 2)], 1
    while first < bits:
        count = min(together, bits - first)
        groups.append((first, 1 << count))
        first += count
    return groups


def piece_of(index, size, together=1):
    bits = size.bit_length() - 1
    piece, first, count = 0, 0, 1
    while first < bits:
        piece = (piece << count) | ((index >> first) & ((1 << count) - 1))
        first += count
        count = min(together, bits - first)
    return piece


def sum_split(segments, members, place, rows, deps):
    width = segments[0][0][0].shape[1]
    size = rows // members
    number = sum(len(arrays) for arrays, _, _ in segments)

    def body(place_ref, *refs):
        ins, outs, total = refs[:number], refs[number:-1], refs[-1]
        first = at = 0
        for arrays, begin, end in segments:
            value = ins[at][begin:end, :].astype(f32)
            for ref in ins[at + 1 : at + len(arrays)]:
                value = value + ref[begin:end, :].astype(f32)
            total[first : first + end - begin, :] = value.astype(bf16)
            first += end - begin
            at += len(arrays)
        if first < rows:
            total[first:, :] = jnp.zeros((rows - first, width), bf16)
        for m in range(members):
            outs[m][...] = total[aligned(place_ref[0] ^ m, size), :]

    return call(
        body,
        "sum_split",
        [shape(size, width, dtype=bf16)] * members,
        [array for arrays, _, _ in segments for array in arrays],
        deps=deps,
        scalars=place.reshape(1),
        scratch=[pltpu.VMEM((rows, width), bf16)],
    )


def sum_all(arrays, dtype=bf16):
    def body(*refs):
        value = refs[0][...].astype(f32)
        for ref in refs[1:-1]:
            value = value + ref[...].astype(f32)
        refs[-1][...] = value.astype(dtype)

    return call(body, "sum_all", shape(*arrays[0].shape, dtype=dtype), arrays)


class CtxSum:
    def __init__(self, groups, *segments):
        self.index = lax.axis_index("ctx").astype(jnp.int32)
        self.groups = list(groups)
        self.segments = segments
        unit = 16
        for _, members in groups:
            unit *= members
        self.rows = -(-sum(end - begin for _, begin, end in segments) // unit) * unit

    def step(self, deps=()):
        if not self.groups:
            return
        first, members = self.groups.pop(0)
        place = (self.index >> first) & (members - 1)
        pieces = sum_split(self.segments, members, place, self.rows, deps)
        self.rows //= members
        arrays = [pieces[0]] + [swap(pieces[m], "ctx", m << first) for m in range(1, members)]
        self.segments = [(arrays, 0, self.rows)]

    def finish(self):
        while self.groups:
            self.step()
        return self.segments[0][0]


def stack_sums(first, second):
    sizes = [first[0].shape[0], second[0].shape[0]]

    def body(*refs):
        for begin, refs_of in ((0, refs[: len(first)]), (sizes[0], refs[len(first) : -1])):
            value = refs_of[0][...].astype(f32)
            for ref in refs_of[1:]:
                value = value + ref[...].astype(f32)
            refs[-1][begin : begin + value.shape[0], :] = value.astype(bf16)

    return call(
        body, "stack_sums", shape(sum(sizes), first[0].shape[1], dtype=bf16), [*first, *second]
    )


def place_gradients(gathered, f, shard, rows, size):
    piece = gathered.shape[0] // size
    columns = gathered.shape[1]
    below = piece - rows

    def body(f_ref, in_ref, reduce_ref, expand_ref, output_ref, *refs):
        outs, ordered, small = refs[:-2], refs[-2], refs[-1]
        at = pl.program_id(0)
        reduce_ref[...] = in_ref[0, :rows, :].astype(f32)
        ordered[aligned(piece_of(at, size, 2), below), :] = in_ref[0, rows:, :]

        @pl.when(at == size - 1)
        def _():
            for unit, k in enumerate((0, 2, 1, 3)):
                expand_ref[:, aligned(f_ref[0] ^ k, columns)] = ordered[
                    unit * shard : (unit + 1) * shard, :
                ].astype(f32)
            output_ref[...] = ordered[4 * shard : 5 * shard, :].astype(f32)
            small[...] = ordered[5 * shard : 5 * shard + 16, :].astype(f32)
            for k in range(6):
                outs[k][...] = small[k : k + 1, aligned(f_ref[0], shard)]
            outs[6][...] = small[pl.ds(8 + f_ref[0], 1), :]

    def whole(*sizes):
        return pl.BlockSpec(sizes, lambda p, s: (0, 0))

    return call(
        body,
        "place_gradients",
        [shape(size * rows, columns), shape(shard, 4 * columns), shape(shard, columns)]
        + [shape(1, shard)] * 6
        + [shape(1, columns)],
        [gathered.reshape(size, piece, columns)],
        scalars=f.reshape(1),
        scratch=[pltpu.VMEM((size * below, columns), bf16), pltpu.VMEM((16, columns), f32)],
        limit=2 * vmem_limit,
        grid=(size,),
        in_specs=[pl.BlockSpec((1, piece, columns), lambda j, s: (j, 0, 0))],
        out_specs=[
            pl.BlockSpec((rows, columns), lambda j, s: (piece_of(j, size), 0)),
            whole(shard, 4 * columns),
            whole(shard, columns),
        ]
        + [whole(1, shard)] * 6
        + [whole(1, columns)],
    )


def cast_feed(expand, reduce):
    shard, columns = expand.shape
    block = columns // 4

    def body(e_ref, r_ref, out_ref):
        at = pl.program_id(0)

        @pl.when(at < 4)
        def _():
            out_ref[...] = e_ref[...].astype(bf16)

        @pl.when(at >= 4)
        def _():
            out_ref[...] = r_ref[...].astype(bf16)

    return call(
        body,
        "cast_feed",
        shape(4 * shard + reduce.shape[0], block, dtype=bf16),
        [expand, reduce],
        grid=(8,),
        in_specs=[
            pl.BlockSpec((shard, block), lambda i: (0, jnp.minimum(i, 3))),
            pl.BlockSpec((reduce.shape[0] // 4, block), lambda i: (jnp.maximum(i - 4, 0), 0)),
        ],
        out_specs=pl.BlockSpec((shard, block), lambda i: (i, 0)),
    )


def cast_all(matrix, deps=()):
    rows, columns = matrix.shape
    tile = min(rows, 256)

    def body(in_ref, out_ref):
        out_ref[...] = in_ref[...].astype(bf16)

    spec = pl.BlockSpec((tile, columns), lambda i: (i, 0))
    return call(
        body,
        "cast_all",
        shape(rows, columns, dtype=bf16),
        [matrix],
        deps=deps,
        grid=(rows // tile,),
        in_specs=[spec],
        out_specs=spec,
    )


def reduce_gradient(activated, own, sibling, half, deps=()):
    rows, columns = activated.shape
    tokens, model = own.shape
    tile = columns // 4

    def body(h_ref, a_ref, d_ref, s_ref, out_ref):
        value = left_transposed(a_ref[:tokens, :], d_ref[...])
        out_ref[...] = (value + left_transposed(a_ref[tokens:, :], s_ref[...])).astype(bf16)

    whole = pl.BlockSpec((tokens, model), lambda i, s: (0, 0))
    return call(
        body,
        "reduce_gradient",
        shape(columns // 2, model, dtype=bf16),
        [activated, own, sibling],
        deps=deps,
        scalars=half.reshape(1),
        grid=(2,),
        in_specs=[pl.BlockSpec((rows, tile), lambda i, s: (0, 2 * i + s[0])), whole, whole],
        out_specs=pl.BlockSpec((tile, model), lambda i, s: (i, 0)),
    )


def expand_gradients(own, sibling, d_expanded, f, row_blocks, flip, shard, deps=()):
    tokens, model = own.shape
    columns = d_expanded.shape[1] // 2

    def body(f_ref, a_ref, b_ref, d_ref, out_ref):
        value = left_transposed(a_ref[...], d_ref[:tokens, :])
        out_ref[...] = (value + left_transposed(b_ref[...], d_ref[tokens:, :])).astype(bf16)

    def rows_map(i, s):
        return (0, s[0] ^ jnp.where(i < 2, row_blocks[0], row_blocks[1]))

    left = pl.BlockSpec((tokens, shard), rows_map)
    return call(
        body,
        "expand_gradients",
        shape(4 * shard, columns, dtype=bf16),
        [own, sibling, d_expanded],
        deps=deps,
        scalars=f.reshape(1),
        grid=(4,),
        in_specs=[left, left, pl.BlockSpec((2 * tokens, columns), lambda i, s: (0, (i % 2) ^ flip))],
        out_specs=pl.BlockSpec((shard, columns), lambda i, s: (i, 0)),
    )


def output_gradient(attended, d_attention, first_sums, second_sums, bias_sums, f, shard):
    model = d_attention.shape[1]
    tile = 256
    steps = model // tile

    def body(s_ref, a_ref, d_ref, first_ref, second_ref, bias_ref, keep_ref, send_ref, rows, small):
        step = pl.program_id(0)
        rows[aligned(step, tile), :] = left_transposed(a_ref[...], d_ref[...]).astype(bf16)

        @pl.when(step == steps - 1)
        def _():
            small[...] = jnp.zeros_like(small)
            small[0:3, :] = first_ref[0:3, :]
            small[3:6, :] = second_ref[0:3, :]
            for k in range(2):
                small[pl.ds(8 + (s_ref[0] ^ (2 * k)), 1), :] = bias_ref[
                    :, k * model : (k + 1) * model
                ]
            for out_ref, blocks in ((keep_ref, (0, 2)), (send_ref, (1, 3))):
                for k, block in enumerate(blocks):
                    out_ref[k * shard : (k + 1) * shard, :] = rows[
                        aligned(s_ref[0] ^ block, shard), :
                    ]
                out_ref[2 * shard :, :] = small[...].astype(bf16)

    total = 2 * shard + 16
    whole = pl.BlockSpec((total, model), lambda i, s: (0, 0))
    return call(
        body,
        "output_gradient",
        [shape(total, model, dtype=bf16)] * 2,
        [attended, d_attention, first_sums, second_sums, bias_sums],
        scalars=f.reshape(1),
        scratch=[pltpu.VMEM((model, model), bf16), pltpu.VMEM((16, model), f32)],
        grid=(steps,),
        in_specs=[pl.BlockSpec((attended.shape[0], tile), lambda i, s: (0, i))]
        + [
            pl.BlockSpec(array.shape, lambda i, s: (0, 0))
            for array in (d_attention, first_sums, second_sums, bias_sums)
        ],
        out_specs=[whole, whole],
    )


def add_parts(first, second, parts):
    width = first.shape[1]

    def body(a_ref, b_ref, *outs):
        for out_ref, ranges in zip(outs, parts):
            at = 0
            for begin, end in ranges:
                value = a_ref[begin:end, :].astype(f32) + b_ref[begin:end, :].astype(f32)
                out_ref[at : at + end - begin, :] = value.astype(bf16)
                at += end - begin

    return call(
        body,
        "add_parts",
        [shape(sum(e - b for b, e in ranges), width, dtype=bf16) for ranges in parts],
        [first, second],
    )


def projection_gradients(stream, d_all, f, shard):
    rows, width = d_all.shape
    model = stream.shape[1]
    tile = 512
    steps = rows // tile

    def body(f_ref, x_ref, d_ref, send_ref, keep_ref, total, sums, rounded):
        step = pl.program_id(0)

        @pl.when(step == 0)
        def _():
            total[...] = jnp.zeros_like(total)
            sums[...] = jnp.zeros_like(sums)

        d_value = d_ref[...]
        total[...] += left_transposed(x_ref[...], d_value)
        sums[...] += jnp.sum(d_value.astype(f32), axis=0, keepdims=True)

        @pl.when(step == steps - 1)
        def _():
            lane = lax.broadcasted_iota(jnp.int32, (1, width), 1)
            scale = jnp.where(lane < width // 3, query_scale, 1.0)
            rounded[...] = (total[...] * scale).astype(bf16)
            bias = jnp.broadcast_to(sums[...] * scale, (16, width)).astype(bf16)
            for out_ref, blocks in ((send_ref, (3, 1)), (keep_ref, (2, 0))):
                for k, block in enumerate(blocks):
                    out_ref[k * shard : (k + 1) * shard, :] = rounded[
                        aligned(f_ref[0] ^ block, shard), :
                    ]
                out_ref[2 * shard :, :] = bias

    out = shape(2 * shard + 16, width, dtype=bf16)
    whole = pl.BlockSpec((2 * shard + 16, width), lambda i, s: (0, 0))
    return call(
        body,
        "projection_gradients",
        [out, out],
        [stream, d_all],
        scalars=f.reshape(1),
        scratch=[
            pltpu.VMEM((model, width), f32),
            pltpu.VMEM((1, width), f32),
            pltpu.VMEM((model, width), bf16),
        ],
        grid=(steps,),
        in_specs=[
            pl.BlockSpec((tile, model), lambda i, s: (i, 0)),
            pl.BlockSpec((tile, width), lambda i, s: (i, 0)),
        ],
        out_specs=[whole, whole],
    )


def place_projections(pieces, scalars, rows, width, shard):
    count = len(pieces)
    if width % LANES:
        order = jnp.arange(count) ^ scalars[0]
        ordered = jnp.take(jnp.stack(pieces), order, axis=0)
        weights = jnp.transpose(ordered[:, :rows], (1, 0, 2)).astype(f32)
        biases = ordered[:, rows].astype(f32)
        return [
            weights[:, :, k * width : (k + 1) * width].reshape(rows, count * width)
            for k in range(3)
        ] + [
            lax.dynamic_slice_in_dim(
                biases[:, k * width : (k + 1) * width].reshape(1, -1), scalars[1] * shard, shard, 1
            )
            for k in (0, 2)
        ]

    def body(s_ref, *refs):
        outs, sums = refs[count:-1], refs[-1]
        for i in range(count):
            where = aligned(s_ref[0] ^ i, width)
            for k in range(3):
                cut = slice(k * width, (k + 1) * width)
                outs[k][:, where] = refs[i][:rows, cut].astype(f32)
                sums[k : k + 1, where] = refs[i][rows : rows + 16, cut].astype(f32)[0:1, :]
        for k, row in ((3, 0), (4, 2)):
            outs[k][...] = sums[row : row + 1, aligned(s_ref[1], shard)]

    return call(
        body,
        "place_projections",
        [shape(rows, count * width)] * 3 + [shape(1, shard)] * 2,
        pieces,
        scalars=scalars,
        scratch=[pltpu.VMEM((8, count * width), f32)],
    )


def project(blocks, first, weights, bias, query_docs, key_docs, own, heads, head_size, length, before, deps):
    tokens, model = blocks[0].shape
    width = heads * head_size
    shard = weights[0].shape[0]
    number = len(blocks)
    rows = number * tokens
    tile = 256
    per_block = tokens // tile
    start = first * per_block

    def body(own_ref, *refs):
        x_refs, w_refs = refs[:number], refs[number : number + 4]
        b_ref, qd_ref, kd_ref = refs[number + 4 : number + 7]
        q_ref, k_ref, v_ref, kt_ref, x_out = refs[-5:]
        for k in range(number):

            @pl.when(pl.program_id(0) // per_block == k)
            def _():
                x_out[...] = x_refs[k][...]

        product = b_ref[...]
        for k in range(4):
            product = product + matmul(x_out[:, aligned(own_ref[0] ^ k, shard)], w_refs[k][...])
        lane = lax.broadcasted_iota(jnp.int32, (tile, LANES - head_size), 1)
        ones = jnp.where(lane < 3, 1.0, 0.0).astype(f32)
        keys = product[:, width : 2 * width]
        for h in range(heads):
            cut = slice(h * head_size, (h + 1) * head_size)
            q_ref[h] = jnp.concatenate((product[:, :width][:, cut], qd_ref[...]), 1).astype(bf16)
            k_ref[h] = jnp.concatenate((keys[:, cut], kd_ref[...]), 1).astype(bf16)
            v_ref[h] = jnp.concatenate((product[:, 2 * width :][:, cut], ones), 1).astype(bf16)
        kt_ref[...] = jnp.transpose(keys).astype(bf16)

    out = shape(heads, length, LANES, dtype=bf16)
    out_spec = pl.BlockSpec((heads, tile, LANES), lambda i, s: (0, i + start, 0))
    extra_spec = pl.BlockSpec((tile, LANES - head_size), lambda i, s: (i + start, 0))
    old = list(before) if before is not None else []

    def block_map(k, i, s):
        return (jnp.clip(i - k * per_block, 0, per_block - 1), 0)

    operands = [*blocks, *weights, bias, query_docs, key_docs, *old]
    return call(
        body,
        "project",
        [out, out, out, shape(width, length, dtype=bf16), shape(length, model, dtype=bf16)],
        operands,
        scalars=own.reshape(1),
        deps=deps,
        aliases={1 + len(operands) - 5 + k: k for k in range(5)} if old else None,
        grid=(rows // tile,),
        in_specs=[pl.BlockSpec((tile, model), functools.partial(block_map, k)) for k in range(number)]
        + [pl.BlockSpec((shard, 3 * width), lambda i, s: (0, 0))] * 4
        + [pl.BlockSpec((1, 3 * width), lambda i, s: (0, 0)), extra_spec, extra_spec]
        + [pl.BlockSpec(memory_space=pl.ANY)] * len(old),
        out_specs=[
            out_spec,
            out_spec,
            out_spec,
            pl.BlockSpec((width, tile), lambda i, s: (0, i + start)),
            pl.BlockSpec((tile, model), lambda i, s: (i + start, 0)),
        ],
    )


def three_parts(value):
    high = value.astype(bf16).astype(f32)
    rest = value - high
    middle = rest.astype(bf16).astype(f32)
    return high, middle, rest - middle


def attend(queries, keys, values, group, number, tokens, head_size, docs, deps):
    heads, length, _ = keys.shape
    width = heads * head_size
    tile = 2 * tokens if length <= 4096 else 128
    per, span = max(1, tokens // tile), max(1, tile // tokens)
    rows = number * tokens
    chunk = min(length, 1024)

    def body(s_ref, q_ref, k_ref, v_ref, out_ref, wide_ref, back_ref):
        lane = lax.broadcasted_iota(jnp.int32, (tile, LANES), 1)
        for h in range(heads):
            query = q_ref[h]
            largest = summed = None
            for first in range(0, length, chunk):
                scores = right_transposed(query, k_ref[h, first : first + chunk, :])
                before = largest
                largest = jnp.max(scores, axis=1, keepdims=True)
                if before is not None:
                    largest = jnp.maximum(before, largest)
                    summed = summed * jnp.exp(before - largest)
                weights = jnp.exp(scores - largest).astype(bf16)
                part = matmul(weights, v_ref[h, first : first + chunk, :])
                summed = part if before is None else summed + part
            total = summed[:, head_size : head_size + 1]
            cut = slice(h * head_size, (h + 1) * head_size)
            attended = summed[:, :head_size] / total
            wide_ref[:, cut] = attended
            for b in range(span):
                where = aligned((b ^ s_ref[0]) & (span - 1), tile // span)
                out_ref[where, cut] = attended[b * tokens : (b + 1) * tokens].astype(bf16)
            parts = three_parts(-(largest + jnp.log(total)))
            back = query.astype(f32)
            for k in range(3):
                back = jnp.where(lane == head_size + docs + k, parts[k], back)
            back_ref[h] = back.astype(bf16)

    return call(
        body,
        "attend",
        [
            shape(rows, width, dtype=bf16),
            shape(rows, width),
            shape(heads, rows, LANES, dtype=bf16),
        ],
        [queries, keys, values],
        deps=deps,
        limit=40 * 1024 * 1024,
        scalars=group.reshape(1),
        grid=(rows // tile,),
        in_specs=[
            pl.BlockSpec((heads, tile, LANES), lambda i, s: (0, i, 0)),
            pl.BlockSpec((heads, length, LANES), lambda i, s: (0, 0, 0)),
            pl.BlockSpec((heads, length, LANES), lambda i, s: (0, 0, 0)),
        ],
        out_specs=[
            pl.BlockSpec((tile, width), lambda i, s: (((i // per) ^ (s[0] // span)) * per + i % per, 0)),
            pl.BlockSpec((tile, width), lambda i, s: (i, 0)),
            pl.BlockSpec((heads, tile, LANES), lambda i, s: (0, i, 0)),
        ],
    )


def attend_back(queries, douts, attended, keys, values, keys_t, head_size, tokens, group):
    heads, length, _ = keys.shape
    rows = attended.shape[0]
    width = heads * head_size
    tile = 2 * tokens if length <= 4096 else 128
    per, span = max(1, tokens // tile), max(1, tile // tokens)

    def body(s_ref, q_ref, d_ref, a_ref, k_ref, v_ref, kt_ref, dq_ref, dk_ref, dv_ref):
        @pl.when(pl.program_id(0) == 0)
        def _():
            dk_ref[...] = jnp.zeros_like(dk_ref)
            dv_ref[...] = jnp.zeros_like(dv_ref)

        lane = lax.broadcasted_iota(jnp.int32, (tile, LANES - head_size), 1)
        for h in range(heads):
            cut = slice(h * head_size, (h + 1) * head_size)
            dout = jnp.concatenate(
                [
                    d_ref[aligned((b ^ s_ref[0]) & (span - 1), tile // span), cut]
                    for b in range(span)
                ],
                axis=0,
            ).astype(f32)
            parts = three_parts(-jnp.sum(dout * a_ref[:, cut], axis=1, keepdims=True))
            extra = jnp.zeros((tile, LANES - head_size), f32)
            for k in range(3):
                extra = jnp.where(lane == k, parts[k], extra)
            dout = jnp.concatenate((dout, extra), axis=1).astype(bf16)
            query = q_ref[h]
            probabilities = jnp.exp(right_transposed(k_ref[h], query))
            grads = right_transposed(v_ref[h], dout)
            d_scores = (probabilities * grads).astype(bf16)
            dk_ref[:, cut] += matmul(d_scores, query)[:, :head_size]
            dv_ref[:, cut] += matmul(probabilities.astype(bf16), dout)[:, :head_size]
            dq_t = matmul(kt_ref[cut, :], d_scores)
            dq_ref[:, cut] = jnp.transpose(dq_t).astype(bf16)

    whole = pl.BlockSpec((length, width), lambda i, s: (0, 0))
    resident = pl.BlockSpec((heads, length, LANES), lambda i, s: (0, 0, 0))

    def dout_map(i, s):
        return (((i // per) ^ (s[0] // span)) * per + i % per, 0)

    in_specs = [
        pl.BlockSpec((heads, tile, LANES), lambda i, s: (0, i, 0)),
        pl.BlockSpec((tile, width), dout_map),
        pl.BlockSpec((tile, width), lambda i, s: (i, 0)),
        resident,
        resident,
        pl.BlockSpec((width, length), lambda i, s: (0, 0)),
    ]
    operands = [queries, douts, attended, keys, values, keys_t]
    return call(
        body,
        "attend_back",
        [shape(rows, width, dtype=bf16), shape(length, width), shape(length, width)],
        operands,
        scalars=group.reshape(1),
        limit=40 * 1024 * 1024 if length <= 4096 else 2 * vmem_limit,
        grid=(rows // tile,),
        in_specs=in_specs,
        out_specs=[pl.BlockSpec((tile, width), lambda i, s: (i, 0)), whole, whole],
    )


def head_grads(d_queries, d_key, d_value, tokens, number, group):
    width = d_key.shape[1]
    count = len(d_queries)
    rows = number * tokens

    def body(s_ref, *refs):
        dk_ref, dv_ref, all_ref, send_ref = refs[count:]
        first = 0
        for ref in refs[:count]:
            all_ref[first : first + ref.shape[0], :width] = ref[...]
            first += ref.shape[0]
        all_ref[:, width : 2 * width] = dk_ref[:rows, :].astype(bf16)
        all_ref[:, 2 * width :] = dv_ref[:rows, :].astype(bf16)
        for k in range(number):
            send_ref[aligned(s_ref[0] ^ k, tokens), :] = all_ref[k * tokens : (k + 1) * tokens, :]

    return call(
        body,
        "head_grads",
        [shape(rows, 3 * width, dtype=bf16)] * 2,
        [*d_queries, d_key, d_value],
        scalars=group.reshape(1),
    )


def lane_copy(value):
    return jnp.broadcast_to(value, (value.shape[0], LANES))


def attention_norm(received, weights, inputs, vectors, f, number):
    tokens, model = inputs.shape
    shard = weights[0].shape[0]
    width = received.shape[1]

    def body(f_ref, p_ref, *refs):
        w_refs = refs[:4]
        x_ref, v_ref = refs[4:6]
        normed_ref, rounded_ref, unit_ref, inverse_ref, all_ref, matrix = refs[6:]
        for k in range(4):
            matrix[aligned(f_ref[0] ^ k, shard), :] = w_refs[k][...]
        for j in range(number):
            all_ref[:, j * width : (j + 1) * width] = p_ref[j * tokens : (j + 1) * tokens, :]
        value = x_ref[...] + v_ref[0:1, :] + matmul(all_ref[...], matrix[...])
        average = jnp.mean(value, axis=-1, keepdims=True)
        centered = value - average
        inverse = lax.rsqrt(jnp.mean(centered * centered, axis=-1, keepdims=True) + epsilon)
        unit = centered * inverse
        normed = unit * v_ref[1:2, :] + v_ref[2:3, :]
        normed_ref[...] = normed
        rounded_ref[...] = normed.astype(bf16)
        unit_ref[...] = unit
        inverse_ref[...] = lane_copy(inverse)

    return call(
        body,
        "attention_norm",
        [
            shape(tokens, model),
            shape(tokens, model, dtype=bf16),
            shape(tokens, model),
            shape(tokens, LANES),
            shape(tokens, model, dtype=bf16),
        ],
        [received, *weights, inputs, vectors],
        scalars=f.reshape(1),
        scratch=[pltpu.VMEM((model, model), bf16)],
    )


def feed_specs(shard, model):
    tile = 2 * shard

    def block(t, s):
        return s[0] ^ (2 * (t // 2))

    specs = [
        pl.BlockSpec((shard, tile), lambda t, s, k=k: (8 * k + block(t, s), t % 2)) for k in range(4)
    ]
    specs.append(pl.BlockSpec((tile, model), lambda t, s: (4 * block(t, s) + 2 + t % 2, 0)))
    return specs, lambda t, s: 2 * block(t, s) + t % 2


def feed_forward(own, sibling, matrix, bias, f):
    tokens, model = own.shape
    shard = model // 4
    tile = 2 * shard

    def body(f_ref, a_ref, b_ref, *refs):
        w_refs, r_ref, bias_ref = refs[:4], refs[4], refs[5]
        act_ref, slope_ref, own_ref, other_ref, x_all = refs[6:]

        @pl.when(pl.program_id(0) == 0)
        def _():
            x_all[:tokens, :] = a_ref[...]
            x_all[tokens:, :] = b_ref[...]
            own_ref[...] = jnp.zeros_like(own_ref)
            other_ref[...] = jnp.zeros_like(other_ref)

        value = bias_ref[...]
        for k in range(4):
            value = value + matmul(x_all[:, k * shard : (k + 1) * shard], w_refs[k][...])
        below = 0.5 + 0.5 * lax.erf(value * 0.7071067811865476)
        density = 0.3989422804014327 * jnp.exp(-0.5 * value * value)
        activated = (value * below).astype(bf16)
        act_ref[...] = activated
        slope_ref[...] = (below + value * density).astype(bf16)
        own_ref[...] += matmul(activated[:tokens], r_ref[...])
        other_ref[...] += matmul(activated[tokens:], r_ref[...])

    specs, column = feed_specs(shard, model)
    wide = shape(2 * tokens, 4 * tile, dtype=bf16)
    whole = pl.BlockSpec((tokens, model), lambda t, s: (0, 0))
    return call(
        body,
        "feed_forward",
        [wide, wide, shape(tokens, model), shape(tokens, model)],
        [own, sibling, *[matrix] * 5, bias],
        scalars=f.reshape(1),
        limit=50 * 1024 * 1024,
        scratch=[pltpu.VMEM((2 * tokens, model), bf16)],
        grid=(4,),
        in_specs=[whole, whole, *specs, pl.BlockSpec((1, tile), lambda t, s: (0, column(t, s)))],
        out_specs=[pl.BlockSpec((2 * tokens, tile), lambda t, s: (0, t))] * 2 + [whole, whole],
    )


def second_norm(normed, own, received, vectors, cotangent):
    tokens, model = normed.shape
    tile = 64

    def body(n_ref, p_ref, r_ref, v_ref, c_ref, out_ref, d_ref, rounded_ref, sums_ref):
        value = n_ref[...] + p_ref[...] + r_ref[...] + v_ref[0:1, :]
        average = jnp.mean(value, axis=-1, keepdims=True)
        centered = value - average
        inverse = lax.rsqrt(jnp.mean(centered * centered, axis=-1, keepdims=True) + epsilon)
        unit = centered * inverse
        out_ref[...] = unit * v_ref[1:2, :] + v_ref[2:3, :]
        dy = c_ref[...]
        dz = dy * v_ref[1:2, :]
        mean_dz = jnp.mean(dz, axis=-1, keepdims=True)
        mean_dzz = jnp.mean(dz * unit, axis=-1, keepdims=True)
        result = inverse * (dz - mean_dz - unit * mean_dzz)
        d_ref[...] = result
        rounded = result.astype(bf16)
        rounded_ref[...] = rounded

        @pl.when(pl.program_id(0) == 0)
        def _():
            sums_ref[...] = jnp.zeros_like(sums_ref)

        sums_ref[0:1, :] += jnp.sum(dy * unit, axis=0, keepdims=True)
        sums_ref[1:2, :] += jnp.sum(dy, axis=0, keepdims=True)
        sums_ref[2:3, :] += jnp.sum(rounded.astype(f32), axis=0, keepdims=True)

    rows = pl.BlockSpec((tile, model), lambda i: (i, 0))
    fixed = pl.BlockSpec((8, model), lambda i: (0, 0))
    return call(
        body,
        "second_norm",
        [shape(tokens, model), shape(tokens, model), shape(tokens, model, dtype=bf16), shape(8, model)],
        [normed, own, received, vectors, cotangent],
        grid=(tokens // tile,),
        in_specs=[rows, rows, rows, fixed, rows],
        out_specs=[rows, rows, rows, fixed],
    )


def feed_back(own, sibling, slope, matrix, f):
    tokens, model = own.shape
    shard = model // 4
    tile = 2 * shard

    def body(f_ref, a_ref, b_ref, slope_ref, *refs):
        w_refs, r_ref = refs[:4], refs[4]
        de_ref, sums_ref, own_ref, other_ref, d_all = refs[5:]

        @pl.when(pl.program_id(0) == 0)
        def _():
            d_all[:tokens, :] = a_ref[...]
            d_all[tokens:, :] = b_ref[...]
            own_ref[...] = jnp.zeros_like(own_ref)
            other_ref[...] = jnp.zeros_like(other_ref)

        value = right_transposed(d_all[...], r_ref[...])
        rounded = (value * slope_ref[...].astype(f32)).astype(bf16)
        de_ref[...] = rounded
        sums_ref[...] = jnp.sum(rounded.astype(f32), axis=0, keepdims=True)
        for k in range(4):
            cut = slice(k * shard, (k + 1) * shard)
            own_ref[:, cut] += right_transposed(rounded[:tokens], w_refs[k][...])
            other_ref[:, cut] += right_transposed(rounded[tokens:], w_refs[k][...])

    specs, _ = feed_specs(shard, model)
    whole = pl.BlockSpec((tokens, model), lambda t, s: (0, 0))
    wide = pl.BlockSpec((2 * tokens, tile), lambda t, s: (0, t))
    return call(
        body,
        "feed_back",
        [
            shape(2 * tokens, 4 * tile, dtype=bf16),
            shape(1, 4 * tile),
            shape(tokens, model),
            shape(tokens, model),
        ],
        [own, sibling, slope, *[matrix] * 5],
        scalars=f.reshape(1),
        limit=50 * 1024 * 1024,
        scratch=[pltpu.VMEM((2 * tokens, model), bf16)],
        grid=(4,),
        in_specs=[whole, whole, wide, *specs],
        out_specs=[wide, pl.BlockSpec((1, tile), lambda t, s: (0, t)), whole, whole],
    )


def first_norm_back(d_second, own, received, unit, inverse, vectors, weights, f, number):
    tokens, model = d_second.shape
    shard = weights[0].shape[0]
    width = model // number

    def body(f_ref, d_ref, p_ref, r_ref, u_ref, i_ref, v_ref, *refs):
        w_refs = refs[:4]
        first_ref, rounded_ref, sums_ref, out_ref, matrix = refs[4:]
        for k in range(4):
            matrix[aligned(f_ref[0] ^ k, shard), :] = w_refs[k][...]
        dy = d_ref[...] + p_ref[...] + r_ref[...]
        unit_value = u_ref[...]
        dz = dy * v_ref[1:2, :]
        mean_dz = jnp.mean(dz, axis=-1, keepdims=True)
        mean_dzz = jnp.mean(dz * unit_value, axis=-1, keepdims=True)
        result = i_ref[:, 0:1] * (dz - mean_dz - unit_value * mean_dzz)
        first_ref[...] = result
        rounded = result.astype(bf16)
        rounded_ref[...] = rounded
        sums_ref[...] = jnp.zeros_like(sums_ref)
        sums_ref[0:1, :] = jnp.sum(dy * unit_value, axis=0, keepdims=True)
        sums_ref[1:2, :] = jnp.sum(dy, axis=0, keepdims=True)
        sums_ref[2:3, :] = jnp.sum(rounded.astype(f32), axis=0, keepdims=True)
        d_attended = right_transposed(rounded, matrix[...]).astype(bf16)
        for j in range(number):
            out_ref[j * tokens : (j + 1) * tokens, :] = d_attended[:, j * width : (j + 1) * width]

    return call(
        body,
        "first_norm_back",
        [
            shape(tokens, model),
            shape(tokens, model, dtype=bf16),
            shape(8, model),
            shape(number * tokens, width, dtype=bf16),
        ],
        [d_second, own, received, unit, inverse, vectors, *weights],
        scalars=f.reshape(1),
        scratch=[pltpu.VMEM((model, model), bf16)],
    )


def input_gradient(d_first, received, matrix, number):
    tokens, model = d_first.shape
    width = received.shape[1] // 3

    def body(d_ref, m_ref, r_ref, out_ref, ordered):
        for j in range(number):
            for k in range(3):
                ordered[:, k * model + j * width : k * model + (j + 1) * width] = r_ref[
                    j * tokens : (j + 1) * tokens, k * width : (k + 1) * width
                ]
        out_ref[...] = d_ref[...] + right_transposed(ordered[...], m_ref[...])

    return call(
        body,
        "input_gradient",
        shape(tokens, model),
        [d_first, matrix, received],
        scratch=[pltpu.VMEM((tokens, 3 * model), bf16)],
    )


def cast_projections(matrices, deps):
    rows, model = matrices[0].shape

    def body(q_ref, k_ref, v_ref, out_ref):
        out_ref[:, :model] = (q_ref[...] * query_scale).astype(bf16)
        out_ref[:, model : 2 * model] = k_ref[...].astype(bf16)
        out_ref[:, 2 * model :] = v_ref[...].astype(bf16)

    whole = pl.BlockSpec((rows, model), lambda: (0, 0))
    return call(
        body,
        "cast_projections",
        shape(rows, 3 * model, dtype=bf16),
        [*matrices],
        deps=deps,
        grid=(),
        in_specs=[whole] * 3,
        out_specs=pl.BlockSpec((rows, 3 * model), lambda: (0, 0)),
    )


def padded(vectors):
    return jnp.concatenate((jnp.stack(vectors), jnp.zeros((8 - len(vectors), vectors[0].shape[0]), f32)))


def per_device(
    hidden_in,
    starts,
    w_query,
    w_key,
    w_value,
    w_output,
    w_expand,
    w_reduce,
    bias_query,
    bias_value,
    bias_output,
    bias_expand,
    bias_reduce,
    attention_gain,
    attention_shift,
    feedforward_gain,
    feedforward_shift,
    cotangent,
):
    Order.last = ()
    tokens, model = hidden_in.shape[1:]
    head_size = model // HEADS
    ctx_size = lax.axis_size("ctx")
    length = tokens * ctx_size
    near = min(ctx_size, HEADS)
    copies = ctx_size // near
    heads = HEADS // near
    width = heads * head_size
    shard = w_query.shape[0]
    ff_block = w_reduce.shape[0]
    documents = starts.shape[1]
    c = lax.axis_index("ctx").astype(jnp.int32)
    f = lax.axis_index("fsdp").astype(jnp.int32)
    group = c & (near - 1)

    inputs = hidden_in[0]
    feed_matrix = lax.all_gather(cast_feed(w_expand, w_reduce), "fsdp", axis=0, tiled=True)
    blocks = gather_ctx(cast_all(inputs))

    own_columns = jnp.concatenate(
        [
            lax.dynamic_slice_in_dim(m, group * width, width, 1) * scale
            for m, scale in ((w_query, query_scale), (w_key, 1.0), (w_value, 1.0))
        ],
        axis=1,
    ).astype(bf16)

    def gather_rows(own):
        across = swap(own, "fsdp", 2)
        return [own, swap(own, "fsdp", 1), across, swap(across, "fsdp", 1)]

    projection_parts = gather_rows(own_columns)

    output_parts = gather_rows(cast_all(w_output, [blocks[1], blocks[2], blocks[4]]))

    all_projection = lax.all_gather(
        cast_projections((w_query, w_key, w_value), ()), "fsdp", axis=0, tiled=True
    )

    order = c ^ lax.iota(jnp.int32, ctx_size)
    positions = (order[:, None] * tokens + lax.iota(jnp.int32, tokens)[None, :]).reshape(-1)
    docs = jnp.sum((starts[0][None, :] <= positions[:, None]).astype(jnp.int32), axis=1) - 1
    lane = lax.iota(jnp.int32, LANES - head_size)[None, :]
    same = docs[:, None] == lane
    query_docs = jnp.where((lane < documents) & ~same, masked_value, 0.0).astype(f32)
    key_docs = jnp.where(same | ((lane >= documents) & (lane < documents + 3)), 1.0, 0.0).astype(f32)
    own_bias = jnp.concatenate(
        (
            lax.dynamic_slice_in_dim(bias_query * query_scale, group * width, width, 0),
            jnp.zeros((width,), f32),
            lax.dynamic_slice_in_dim(bias_value, group * width, width, 0),
        )
    ).reshape(1, -1)
    attention_vectors = padded((bias_output, attention_gain, attention_shift))
    feed_vectors = padded((bias_reduce, feedforward_gain, feedforward_shift))

    queries, keys, values, keys_t, stream = project(
        blocks,
        0,
        projection_parts,
        own_bias,
        query_docs,
        key_docs,
        f,
        heads,
        head_size,
        length,
        None,
        (),
    )

    out, wide, back = attend(
        queries, keys, values, group, near, tokens, head_size, documents, output_parts[1:]
    )
    received = exchange(out, near)
    normed, normed_r, first_unit, first_inverse, attended_r = attention_norm(
        received, output_parts, inputs, attention_vectors, f, near
    )

    sibling_normed = swap(normed_r, "fsdp", 1)
    activated_r, slope, partial, other = feed_forward(
        normed_r, sibling_normed, feed_matrix, bias_expand.reshape(1, -1), f
    )
    layer_out, d_second, d_reduced_r, second_sums = second_norm(
        normed, partial, swap(other, "fsdp", 1), feed_vectors, cotangent[0]
    )
    sibling_reduced = swap(d_reduced_r, "fsdp", 1)

    d_expanded_r, bias_expand_sum, partial, other = feed_back(
        d_reduced_r, sibling_reduced, slope, feed_matrix, f
    )
    other = swap(other, "fsdp", 1)

    expand_send = expand_gradients(normed_r, sibling_normed, d_expanded_r, f, (2, 3), 1, shard)
    expand_received = swap(expand_send, "fsdp", 2)
    d_first, d_attention_r, first_sums, d_attended = first_norm_back(
        d_second,
        partial,
        other,
        first_unit,
        first_inverse,
        attention_vectors,
        output_parts,
        f,
        near,
    )
    douts = exchange(d_attended, near)
    output_keep, output_send = output_gradient(
        attended_r, d_attention_r, first_sums, second_sums, bias_expand_sum, f, shard
    )
    output_received = swap(output_send, "fsdp", 1)
    low = c & 1
    reduce_send = reduce_gradient(activated_r, d_reduced_r, sibling_reduced, 1 - low, [douts])
    reduce_received = swap(reduce_send, "ctx", 1)

    rest = (2 * shard, 2 * shard + 16)
    d_query, d_key, d_value = attend_back(
        back, douts, wide, keys, values, keys_t, head_size, tokens, group
    )
    output_keep, output_send = add_parts(
        output_keep, output_received, [[(0, shard), rest], [(shard, 2 * shard), rest]]
    )
    output_received = swap(output_send, "fsdp", 2)
    expand_keep = expand_gradients(
        normed_r, sibling_normed, d_expanded_r, f, (0, 1), 0, shard
    )
    (expand_send,) = add_parts(expand_keep, expand_received, [[(2 * shard, 4 * shard)]])
    expand_other = swap(expand_send, "fsdp", 1)
    count = ctx_size
    while count > near:
        count //= 2
        received = [
            swap(d[count * tokens :].astype(bf16), "ctx", count).astype(f32) for d in (d_key, d_value)
        ]
        d_key = d_key[: count * tokens] + received[0]
        d_value = d_value[: count * tokens] + received[1]
    d_all, d_send = head_grads([d_query], d_key, d_value, tokens, near, group)
    d_mine = exchange(d_send, near)

    send, keep = projection_gradients(stream, d_all, f, shard)
    received = swap(send, "fsdp", 1)
    cut = ff_block // 2
    reduce_keep = reduce_gradient(activated_r, d_reduced_r, sibling_reduced, low)
    reduce_keep, reduce_send = add_parts(
        reduce_keep, reduce_received, [[(0, cut)], [(cut, 2 * cut)]]
    )
    reduce_received = swap(reduce_send, "fsdp", 2)
    send, keep = add_parts(keep, received, [[(0, shard), rest], [(shard, 2 * shard), rest]])
    received = swap(send, "fsdp", 2)
    expander = CtxSum(
        ctx_groups(2),
        ([expand_keep, expand_received], 0, 2 * shard),
        ([expand_other], 0, 2 * shard),
        ([output_keep, output_received], 0, shard + 16),
    )
    expander.step()
    mine = sum_all([keep, received])
    count = ctx_size
    while count > near:
        count //= 2
        mine = sum_all([mine, swap(mine, "ctx", count)])
    reducer = CtxSum(ctx_groups()[1:], ([reduce_keep, reduce_received], 0, cut))
    reducer.step([d_mine])
    expander.step()
    reducer.step()
    input_grad = input_gradient(d_first, d_mine, all_projection, near)
    reduced, expanded = reducer.finish(), expander.finish()
    gathered = lax.all_gather(stack_sums(reduced, expanded), "ctx", axis=0, tiled=True)
    grad_query, grad_key, grad_value, grad_bias_query, grad_bias_value = place_projections(
        gather_small(mine, near), jnp.stack((group, f)), shard, width, shard
    )
    grad_w_reduce, grad_w_expand, grad_w_output, *small = place_gradients(
        gathered, f, shard, reduced[0].shape[0], ctx_size
    )
    (
        grad_bias_query,
        grad_bias_value,
        grad_att_gain,
        grad_att_shift,
        grad_bias_output,
        grad_ff_gain,
        grad_ff_shift,
        grad_bias_reduce,
        grad_bias_expand,
    ) = [v.reshape(-1) for v in (grad_bias_query, grad_bias_value, *small)]

    return (
        layer_out[None],
        input_grad[None],
        grad_query,
        grad_key,
        grad_value,
        grad_w_output,
        grad_w_expand,
        grad_w_reduce,
        grad_bias_query,
        grad_bias_value,
        grad_bias_output,
        grad_bias_expand,
        grad_bias_reduce,
        grad_att_gain,
        grad_att_shift,
        grad_ff_gain,
        grad_ff_shift,
    )


def solution(mesh):
    rows = P("fsdp", None)
    activations = P("fsdp", "ctx", None)
    return jax.shard_map(
        per_device,
        mesh=mesh,
        in_specs=(activations,) + (rows,) * 7 + (P(),) * 9 + (activations,),
        out_specs=(activations, activations) + (rows,) * 6 + (P("fsdp"),) * 9,
        check_vma=False,
    )
```

```python
import functools

import jax
import jax.numpy as jnp
from jax import lax
from jax.experimental import pallas as pl
from jax.experimental.pallas import tpu as pltpu
from jax.sharding import PartitionSpec as P

HEADS = 16
LANES = 128
epsilon = 1e-05
masked_value = -1e30
query_scale = 0.125
bf16 = jnp.bfloat16
f32 = jnp.float32
vmem_limit = 28 * 1024 * 1024


def matmul(left, right):
    return jnp.dot(left, right, preferred_element_type=f32)


def left_transposed(left, right):
    return lax.dot_general(left, right, (((0,), (0,)), ((), ())), preferred_element_type=f32)


def right_transposed(left, right):
    return lax.dot_general(left, right, (((1,), (1,)), ((), ())), preferred_element_type=f32)


def swap(array, axis, mask):
    size = lax.axis_size(axis)
    return lax.ppermute(array, axis, [(i, i ^ mask) for i in range(size)])


def shape(*sizes, dtype=f32):
    return jax.ShapeDtypeStruct(sizes, dtype)


class Order:
    last = ()


def call(
    body, name, out_shape, operands, scalars=None, scratch=(), aliases=None, deps=(), limit=vmem_limit, **grid
):
    count = 0 if scalars is None else 1
    several = isinstance(out_shape, (list, tuple))
    if not grid:
        whole = pl.BlockSpec(memory_space=pltpu.VMEM)
        grid = dict(
            grid=(),
            in_specs=[whole] * len(operands),
            out_specs=[whole] * len(out_shape) if several else whole,
        )
    extra = [*Order.last, *deps]
    first = count + len(operands)
    grid["in_specs"] = list(grid["in_specs"]) + [pl.BlockSpec(memory_space=pl.ANY)] * len(extra)

    def ordered(*refs):
        body(*refs[:first], *refs[first + len(extra) :])

    result = pl.pallas_call(
        ordered,
        out_shape=out_shape,
        grid_spec=pltpu.PrefetchScalarGridSpec(
            num_scalar_prefetch=count, scratch_shapes=list(scratch), **grid
        ),
        input_output_aliases=aliases or {},
        compiler_params=pltpu.CompilerParams(vmem_limit_bytes=limit),
        cost_estimate=pl.CostEstimate(flops=1, bytes_accessed=1, transcendentals=0),
        name=name,
    )(*([] if scalars is None else [scalars]), *operands, *extra)
    Order.last = (result[0] if several else result,)
    return result


def aligned(index, size):
    return pl.ds(pl.multiple_of(index * size, size), size)


def gather_ctx(own):
    size = lax.axis_size("ctx")
    masks = [1 << i for i in range(size.bit_length() - 1)]
    blocks = {0: own}
    for mask in reversed(masks[1:]):
        for index in list(blocks):
            blocks[index | mask] = swap(blocks[index], "ctx", mask)
    for index in list(blocks):
        if index != 2:
            blocks[index | 1] = swap(blocks[index], "ctx", 1)
    blocks[3] = swap(blocks[1], "ctx", 2)
    return [blocks[i] for i in range(len(blocks))]


def gather_small(own, number):
    blocks = {0: own}
    for index in range(2, number, 2):
        blocks[index] = swap(own, "ctx", index)
    for index in list(blocks):
        blocks[index | 1] = swap(blocks[index], "ctx", 1)
    return [blocks[i] for i in range(number)]


def exchange(array, number):
    size = lax.axis_size("ctx")
    if number == size:
        return lax.all_to_all(array, "ctx", 0, 0, tiled=True)
    rows = array.shape[0] // number
    own = lax.axis_index("ctx").astype(jnp.int32) & (number - 1)
    result = jnp.zeros_like(array)
    for i in range(number):
        block = lax.dynamic_slice_in_dim(array, (own ^ i) * rows, rows, 0)
        block = block if i == 0 else swap(block, "ctx", i)
        result = lax.dynamic_update_slice_in_dim(result, block, (own ^ i) * rows, 0)
    return result


def ctx_groups(together=1):
    bits = lax.axis_size("ctx").bit_length() - 1
    groups, first = [(0, 2)], 1
    while first < bits:
        count = min(together, bits - first)
        groups.append((first, 1 << count))
        first += count
    return groups


def piece_of(index, size, together=1):
    bits = size.bit_length() - 1
    piece, first, count = 0, 0, 1
    while first < bits:
        piece = (piece << count) | ((index >> first) & ((1 << count) - 1))
        first += count
        count = min(together, bits - first)
    return piece


def sum_split(segments, members, place, rows, deps):
    width = segments[0][0][0].shape[1]
    size = rows // members
    number = sum(len(arrays) for arrays, _, _ in segments)

    def body(place_ref, *refs):
        ins, outs, total = refs[:number], refs[number:-1], refs[-1]
        first = at = 0
        for arrays, begin, end in segments:
            value = ins[at][begin:end, :].astype(f32)
            for ref in ins[at + 1 : at + len(arrays)]:
                value = value + ref[begin:end, :].astype(f32)
            total[first : first + end - begin, :] = value.astype(bf16)
            first += end - begin
            at += len(arrays)
        if first < rows:
            total[first:, :] = jnp.zeros((rows - first, width), bf16)
        for m in range(members):
            outs[m][...] = total[aligned(place_ref[0] ^ m, size), :]

    return call(
        body,
        "sum_split",
        [shape(size, width, dtype=bf16)] * members,
        [array for arrays, _, _ in segments for array in arrays],
        deps=deps,
        scalars=place.reshape(1),
        scratch=[pltpu.VMEM((rows, width), bf16)],
    )


def sum_all(arrays, dtype=bf16):
    def body(*refs):
        value = refs[0][...].astype(f32)
        for ref in refs[1:-1]:
            value = value + ref[...].astype(f32)
        refs[-1][...] = value.astype(dtype)

    return call(body, "sum_all", shape(*arrays[0].shape, dtype=dtype), arrays)


class CtxSum:
    def __init__(self, groups, *segments):
        self.index = lax.axis_index("ctx").astype(jnp.int32)
        self.groups = list(groups)
        self.segments = segments
        unit = 16
        for _, members in groups:
            unit *= members
        self.rows = -(-sum(end - begin for _, begin, end in segments) // unit) * unit

    def step(self, deps=()):
        if not self.groups:
            return
        first, members = self.groups.pop(0)
        place = (self.index >> first) & (members - 1)
        pieces = sum_split(self.segments, members, place, self.rows, deps)
        self.rows //= members
        arrays = [pieces[0]] + [swap(pieces[m], "ctx", m << first) for m in range(1, members)]
        self.segments = [(arrays, 0, self.rows)]

    def finish(self):
        while self.groups:
            self.step()
        return self.segments[0][0]


def stack_sums(first, second):
    sizes = [first[0].shape[0], second[0].shape[0]]

    def body(*refs):
        for begin, refs_of in ((0, refs[: len(first)]), (sizes[0], refs[len(first) : -1])):
            value = refs_of[0][...].astype(f32)
            for ref in refs_of[1:]:
                value = value + ref[...].astype(f32)
            refs[-1][begin : begin + value.shape[0], :] = value.astype(bf16)

    return call(
        body, "stack_sums", shape(sum(sizes), first[0].shape[1], dtype=bf16), [*first, *second]
    )


def place_gradients(gathered, vectors, f, shard, rows, size):
    piece = gathered.shape[0] // size
    columns = gathered.shape[1]
    below = piece - rows

    def body(f_ref, in_ref, v_ref, reduce_ref, expand_ref, output_ref, *refs):
        outs, ordered, small = refs[:-2], refs[-2], refs[-1]
        at = pl.program_id(0)
        reduce_ref[...] = in_ref[0, :rows, :].astype(f32)
        ordered[aligned(piece_of(at, size, 2), below), :] = in_ref[0, rows:, :]

        @pl.when(at == size - 1)
        def _():
            for unit, k in enumerate((0, 2, 1, 3)):
                expand_ref[:, aligned(f_ref[0] ^ k, columns)] = ordered[
                    unit * shard : (unit + 1) * shard, :
                ].astype(f32)
            output_ref[...] = ordered[4 * shard : 5 * shard, :].astype(f32)
            small[...] = v_ref[...].astype(f32)
            for k in range(6):
                outs[k][...] = small[k : k + 1, aligned(f_ref[0], shard)]
            outs[6][...] = small[pl.ds(8 + f_ref[0], 1), :]

    def whole(*sizes):
        return pl.BlockSpec(sizes, lambda p, s: (0, 0))

    return call(
        body,
        "place_gradients",
        [shape(size * rows, columns), shape(shard, 4 * columns), shape(shard, columns)]
        + [shape(1, shard)] * 6
        + [shape(1, columns)],
        [gathered.reshape(size, piece, columns), vectors],
        scalars=f.reshape(1),
        scratch=[pltpu.VMEM((size * below, columns), bf16), pltpu.VMEM((16, columns), f32)],
        limit=2 * vmem_limit,
        grid=(size,),
        in_specs=[pl.BlockSpec((1, piece, columns), lambda j, s: (j, 0, 0)), whole(16, columns)],
        out_specs=[
            pl.BlockSpec((rows, columns), lambda j, s: (piece_of(j, size), 0)),
            whole(shard, 4 * columns),
            whole(shard, columns),
        ]
        + [whole(1, shard)] * 6
        + [whole(1, columns)],
    )


def cast_feed(expand, reduce):
    shard, columns = expand.shape
    block = columns // 4

    def body(e_ref, r_ref, out_ref):
        at = pl.program_id(0)

        @pl.when(at < 4)
        def _():
            out_ref[...] = e_ref[...].astype(bf16)

        @pl.when(at >= 4)
        def _():
            out_ref[...] = r_ref[...].astype(bf16)

    return call(
        body,
        "cast_feed",
        shape(4 * shard + reduce.shape[0], block, dtype=bf16),
        [expand, reduce],
        grid=(8,),
        in_specs=[
            pl.BlockSpec((shard, block), lambda i: (0, jnp.minimum(i, 3))),
            pl.BlockSpec((reduce.shape[0] // 4, block), lambda i: (jnp.maximum(i - 4, 0), 0)),
        ],
        out_specs=pl.BlockSpec((shard, block), lambda i: (i, 0)),
    )


def cast_all(matrix, deps=()):
    rows, columns = matrix.shape
    tile = min(rows, 256)

    def body(in_ref, out_ref):
        out_ref[...] = in_ref[...].astype(bf16)

    spec = pl.BlockSpec((tile, columns), lambda i: (i, 0))
    return call(
        body,
        "cast_all",
        shape(rows, columns, dtype=bf16),
        [matrix],
        deps=deps,
        grid=(rows // tile,),
        in_specs=[spec],
        out_specs=spec,
    )


def reduce_gradient(activated, own, sibling, half, deps=()):
    rows, columns = activated.shape
    tokens, model = own.shape
    tile = columns // 4

    def body(h_ref, a_ref, d_ref, s_ref, out_ref):
        value = left_transposed(a_ref[:tokens, :], d_ref[...])
        out_ref[...] = (value + left_transposed(a_ref[tokens:, :], s_ref[...])).astype(bf16)

    whole = pl.BlockSpec((tokens, model), lambda i, s: (0, 0))
    return call(
        body,
        "reduce_gradient",
        shape(columns // 2, model, dtype=bf16),
        [activated, own, sibling],
        deps=deps,
        scalars=half.reshape(1),
        grid=(2,),
        in_specs=[pl.BlockSpec((rows, tile), lambda i, s: (0, 2 * i + s[0])), whole, whole],
        out_specs=pl.BlockSpec((tile, model), lambda i, s: (i, 0)),
    )


def expand_gradients(own, sibling, d_expanded, f, row_blocks, flip, shard, deps=()):
    tokens, model = own.shape
    columns = d_expanded.shape[1] // 2

    def body(f_ref, a_ref, b_ref, d_ref, out_ref):
        value = left_transposed(a_ref[...], d_ref[:tokens, :])
        out_ref[...] = (value + left_transposed(b_ref[...], d_ref[tokens:, :])).astype(bf16)

    def rows_map(i, s):
        return (0, s[0] ^ jnp.where(i < 2, row_blocks[0], row_blocks[1]))

    left = pl.BlockSpec((tokens, shard), rows_map)
    return call(
        body,
        "expand_gradients",
        shape(4 * shard, columns, dtype=bf16),
        [own, sibling, d_expanded],
        deps=deps,
        scalars=f.reshape(1),
        grid=(4,),
        in_specs=[left, left, pl.BlockSpec((2 * tokens, columns), lambda i, s: (0, (i % 2) ^ flip))],
        out_specs=pl.BlockSpec((shard, columns), lambda i, s: (i, 0)),
    )


def output_gradient(attended, d_attention, first_sums, second_sums, bias_sums, f, shard):
    model = d_attention.shape[1]
    tile = 256
    steps = model // tile

    def body(s_ref, a_ref, d_ref, first_ref, second_ref, bias_ref, keep_ref, send_ref, rows, small):
        step = pl.program_id(0)
        rows[aligned(step, tile), :] = left_transposed(a_ref[...], d_ref[...]).astype(bf16)

        @pl.when(step == steps - 1)
        def _():
            small[...] = jnp.zeros_like(small)
            small[0:3, :] = first_ref[0:3, :]
            small[3:6, :] = second_ref[0:3, :]
            for k in range(2):
                small[pl.ds(8 + (s_ref[0] ^ (2 * k)), 1), :] = bias_ref[
                    :, k * model : (k + 1) * model
                ]
            for out_ref, blocks in ((keep_ref, (0, 2)), (send_ref, (1, 3))):
                for k, block in enumerate(blocks):
                    out_ref[k * shard : (k + 1) * shard, :] = rows[
                        aligned(s_ref[0] ^ block, shard), :
                    ]
                out_ref[2 * shard :, :] = small[...].astype(bf16)

    total = 2 * shard + 16
    whole = pl.BlockSpec((total, model), lambda i, s: (0, 0))
    return call(
        body,
        "output_gradient",
        [shape(total, model, dtype=bf16)] * 2,
        [attended, d_attention, first_sums, second_sums, bias_sums],
        scalars=f.reshape(1),
        scratch=[pltpu.VMEM((model, model), bf16), pltpu.VMEM((16, model), f32)],
        grid=(steps,),
        in_specs=[pl.BlockSpec((attended.shape[0], tile), lambda i, s: (0, i))]
        + [
            pl.BlockSpec(array.shape, lambda i, s: (0, 0))
            for array in (d_attention, first_sums, second_sums, bias_sums)
        ],
        out_specs=[whole, whole],
    )


def add_parts(first, second, parts):
    width = first.shape[1]

    def body(a_ref, b_ref, *outs):
        for out_ref, ranges in zip(outs, parts):
            at = 0
            for begin, end in ranges:
                value = a_ref[begin:end, :].astype(f32) + b_ref[begin:end, :].astype(f32)
                out_ref[at : at + end - begin, :] = value.astype(bf16)
                at += end - begin

    return call(
        body,
        "add_parts",
        [shape(sum(e - b for b, e in ranges), width, dtype=bf16) for ranges in parts],
        [first, second],
    )


def projection_gradients(stream, d_all, f, shard):
    rows, width = d_all.shape
    model = stream.shape[1]
    tile = 512
    steps = rows // tile

    def body(f_ref, x_ref, d_ref, send_ref, keep_ref, total, sums, rounded):
        step = pl.program_id(0)

        @pl.when(step == 0)
        def _():
            total[...] = jnp.zeros_like(total)
            sums[...] = jnp.zeros_like(sums)

        d_value = d_ref[...]
        total[...] += left_transposed(x_ref[...], d_value)
        sums[...] += jnp.sum(d_value.astype(f32), axis=0, keepdims=True)

        @pl.when(step == steps - 1)
        def _():
            lane = lax.broadcasted_iota(jnp.int32, (1, width), 1)
            scale = jnp.where(lane < width // 3, query_scale, 1.0)
            rounded[...] = (total[...] * scale).astype(bf16)
            bias = jnp.broadcast_to(sums[...] * scale, (16, width)).astype(bf16)
            for out_ref, blocks in ((send_ref, (3, 1)), (keep_ref, (2, 0))):
                for k, block in enumerate(blocks):
                    out_ref[k * shard : (k + 1) * shard, :] = rounded[
                        aligned(f_ref[0] ^ block, shard), :
                    ]
                out_ref[2 * shard :, :] = bias

    out = shape(2 * shard + 16, width, dtype=bf16)
    whole = pl.BlockSpec((2 * shard + 16, width), lambda i, s: (0, 0))
    return call(
        body,
        "projection_gradients",
        [out, out],
        [stream, d_all],
        scalars=f.reshape(1),
        scratch=[
            pltpu.VMEM((model, width), f32),
            pltpu.VMEM((1, width), f32),
            pltpu.VMEM((model, width), bf16),
        ],
        grid=(steps,),
        in_specs=[
            pl.BlockSpec((tile, model), lambda i, s: (i, 0)),
            pl.BlockSpec((tile, width), lambda i, s: (i, 0)),
        ],
        out_specs=[whole, whole],
    )


def place_projections(pieces, scalars, rows, width, shard):
    count = len(pieces)
    if width % LANES:
        order = jnp.arange(count) ^ scalars[0]
        ordered = jnp.take(jnp.stack(pieces), order, axis=0)
        weights = jnp.transpose(ordered[:, :rows], (1, 0, 2)).astype(f32)
        biases = ordered[:, rows].astype(f32)
        return [
            weights[:, :, k * width : (k + 1) * width].reshape(rows, count * width)
            for k in range(3)
        ] + [
            lax.dynamic_slice_in_dim(
                biases[:, k * width : (k + 1) * width].reshape(1, -1), scalars[1] * shard, shard, 1
            )
            for k in (0, 2)
        ]

    def body(s_ref, *refs):
        outs, sums = refs[count:-1], refs[-1]
        for i in range(count):
            where = aligned(s_ref[0] ^ i, width)
            for k in range(3):
                cut = slice(k * width, (k + 1) * width)
                outs[k][:, where] = refs[i][:rows, cut].astype(f32)
                sums[k : k + 1, where] = refs[i][rows : rows + 16, cut].astype(f32)[0:1, :]
        for k, row in ((3, 0), (4, 2)):
            outs[k][...] = sums[row : row + 1, aligned(s_ref[1], shard)]

    return call(
        body,
        "place_projections",
        [shape(rows, count * width)] * 3 + [shape(1, shard)] * 2,
        pieces,
        scalars=scalars,
        scratch=[pltpu.VMEM((8, count * width), f32)],
    )


def project(blocks, first, weights, bias, query_docs, key_docs, own, heads, head_size, length, before, deps):
    tokens, model = blocks[0].shape
    width = heads * head_size
    shard = weights[0].shape[0]
    number = len(blocks)
    rows = number * tokens
    tile = 256
    per_block = tokens // tile
    start = first * per_block

    def body(own_ref, *refs):
        x_refs, w_refs = refs[:number], refs[number : number + 4]
        b_ref, qd_ref, kd_ref = refs[number + 4 : number + 7]
        q_ref, k_ref, v_ref, kt_ref, x_out = refs[-5:]
        for k in range(number):

            @pl.when(pl.program_id(0) // per_block == k)
            def _():
                x_out[...] = x_refs[k][...]

        product = b_ref[...]
        for k in range(4):
            product = product + matmul(x_out[:, aligned(own_ref[0] ^ k, shard)], w_refs[k][...])
        lane = lax.broadcasted_iota(jnp.int32, (tile, LANES - head_size), 1)
        ones = jnp.where(lane < 3, 1.0, 0.0).astype(f32)
        keys = product[:, width : 2 * width]
        for h in range(heads):
            cut = slice(h * head_size, (h + 1) * head_size)
            q_ref[h] = jnp.concatenate((product[:, :width][:, cut], qd_ref[...]), 1).astype(bf16)
            k_ref[h] = jnp.concatenate((keys[:, cut], kd_ref[...]), 1).astype(bf16)
            v_ref[h] = jnp.concatenate((product[:, 2 * width :][:, cut], ones), 1).astype(bf16)
        kt_ref[...] = jnp.transpose(keys).astype(bf16)

    out = shape(heads, length, LANES, dtype=bf16)
    out_spec = pl.BlockSpec((heads, tile, LANES), lambda i, s: (0, i + start, 0))
    extra_spec = pl.BlockSpec((tile, LANES - head_size), lambda i, s: (i + start, 0))
    old = list(before) if before is not None else []

    def block_map(k, i, s):
        return (jnp.clip(i - k * per_block, 0, per_block - 1), 0)

    operands = [*blocks, *weights, bias, query_docs, key_docs, *old]
    return call(
        body,
        "project",
        [out, out, out, shape(width, length, dtype=bf16), shape(length, model, dtype=bf16)],
        operands,
        scalars=own.reshape(1),
        deps=deps,
        aliases={1 + len(operands) - 5 + k: k for k in range(5)} if old else None,
        grid=(rows // tile,),
        in_specs=[pl.BlockSpec((tile, model), functools.partial(block_map, k)) for k in range(number)]
        + [pl.BlockSpec((shard, 3 * width), lambda i, s: (0, 0))] * 4
        + [pl.BlockSpec((1, 3 * width), lambda i, s: (0, 0)), extra_spec, extra_spec]
        + [pl.BlockSpec(memory_space=pl.ANY)] * len(old),
        out_specs=[
            out_spec,
            out_spec,
            out_spec,
            pl.BlockSpec((width, tile), lambda i, s: (0, i + start)),
            pl.BlockSpec((tile, model), lambda i, s: (i + start, 0)),
        ],
    )


def three_parts(value):
    high = value.astype(bf16).astype(f32)
    rest = value - high
    middle = rest.astype(bf16).astype(f32)
    return high, middle, rest - middle


def attend(queries, keys, values, group, number, tokens, head_size, docs, deps):
    heads, length, _ = keys.shape
    width = heads * head_size
    tile = 2 * tokens if length <= 4096 else 128
    per, span = max(1, tokens // tile), max(1, tile // tokens)
    rows = number * tokens
    chunk = min(length, 1024)

    def body(s_ref, q_ref, k_ref, v_ref, out_ref, wide_ref, back_ref):
        lane = lax.broadcasted_iota(jnp.int32, (tile, LANES), 1)
        for h in range(heads):
            query = q_ref[h]
            largest = summed = None
            for first in range(0, length, chunk):
                scores = right_transposed(query, k_ref[h, first : first + chunk, :])
                before = largest
                largest = jnp.max(scores, axis=1, keepdims=True)
                if before is not None:
                    largest = jnp.maximum(before, largest)
                    summed = summed * jnp.exp(before - largest)
                weights = jnp.exp(scores - largest).astype(bf16)
                part = matmul(weights, v_ref[h, first : first + chunk, :])
                summed = part if before is None else summed + part
            total = summed[:, head_size : head_size + 1]
            cut = slice(h * head_size, (h + 1) * head_size)
            attended = summed[:, :head_size] / total
            wide_ref[:, cut] = attended
            for b in range(span):
                where = aligned((b ^ s_ref[0]) & (span - 1), tile // span)
                out_ref[where, cut] = attended[b * tokens : (b + 1) * tokens].astype(bf16)
            parts = three_parts(-(largest + jnp.log(total)))
            back = query.astype(f32)
            for k in range(3):
                back = jnp.where(lane == head_size + docs + k, parts[k], back)
            back_ref[h] = back.astype(bf16)

    return call(
        body,
        "attend",
        [
            shape(rows, width, dtype=bf16),
            shape(rows, width),
            shape(heads, rows, LANES, dtype=bf16),
        ],
        [queries, keys, values],
        deps=deps,
        limit=40 * 1024 * 1024,
        scalars=group.reshape(1),
        grid=(rows // tile,),
        in_specs=[
            pl.BlockSpec((heads, tile, LANES), lambda i, s: (0, i, 0)),
            pl.BlockSpec((heads, length, LANES), lambda i, s: (0, 0, 0)),
            pl.BlockSpec((heads, length, LANES), lambda i, s: (0, 0, 0)),
        ],
        out_specs=[
            pl.BlockSpec((tile, width), lambda i, s: (((i // per) ^ (s[0] // span)) * per + i % per, 0)),
            pl.BlockSpec((tile, width), lambda i, s: (i, 0)),
            pl.BlockSpec((heads, tile, LANES), lambda i, s: (0, i, 0)),
        ],
    )


def attend_back(queries, douts, attended, keys, values, keys_t, head_size, tokens, group):
    heads, length, _ = keys.shape
    rows = attended.shape[0]
    width = heads * head_size
    tile = 2 * tokens if length <= 4096 else 128
    per, span = max(1, tokens // tile), max(1, tile // tokens)

    def body(s_ref, q_ref, d_ref, a_ref, k_ref, v_ref, kt_ref, dq_ref, dk_ref, dv_ref):
        @pl.when(pl.program_id(0) == 0)
        def _():
            dk_ref[...] = jnp.zeros_like(dk_ref)
            dv_ref[...] = jnp.zeros_like(dv_ref)

        lane = lax.broadcasted_iota(jnp.int32, (tile, LANES - head_size), 1)
        for h in range(heads):
            cut = slice(h * head_size, (h + 1) * head_size)
            dout = jnp.concatenate(
                [
                    d_ref[aligned((b ^ s_ref[0]) & (span - 1), tile // span), cut]
                    for b in range(span)
                ],
                axis=0,
            ).astype(f32)
            parts = three_parts(-jnp.sum(dout * a_ref[:, cut], axis=1, keepdims=True))
            extra = jnp.zeros((tile, LANES - head_size), f32)
            for k in range(3):
                extra = jnp.where(lane == k, parts[k], extra)
            dout = jnp.concatenate((dout, extra), axis=1).astype(bf16)
            query = q_ref[h]
            probabilities = jnp.exp(right_transposed(k_ref[h], query))
            grads = right_transposed(v_ref[h], dout)
            d_scores = (probabilities * grads).astype(bf16)
            dk_ref[:, cut] += matmul(d_scores, query)[:, :head_size]
            dv_ref[:, cut] += matmul(probabilities.astype(bf16), dout)[:, :head_size]
            dq_t = matmul(kt_ref[cut, :], d_scores)
            dq_ref[:, cut] = jnp.transpose(dq_t).astype(bf16)

    whole = pl.BlockSpec((length, width), lambda i, s: (0, 0))
    resident = pl.BlockSpec((heads, length, LANES), lambda i, s: (0, 0, 0))

    def dout_map(i, s):
        return (((i // per) ^ (s[0] // span)) * per + i % per, 0)

    in_specs = [
        pl.BlockSpec((heads, tile, LANES), lambda i, s: (0, i, 0)),
        pl.BlockSpec((tile, width), dout_map),
        pl.BlockSpec((tile, width), lambda i, s: (i, 0)),
        resident,
        resident,
        pl.BlockSpec((width, length), lambda i, s: (0, 0)),
    ]
    operands = [queries, douts, attended, keys, values, keys_t]
    return call(
        body,
        "attend_back",
        [shape(rows, width, dtype=bf16), shape(length, width), shape(length, width)],
        operands,
        scalars=group.reshape(1),
        limit=40 * 1024 * 1024 if length <= 4096 else 2 * vmem_limit,
        grid=(rows // tile,),
        in_specs=in_specs,
        out_specs=[pl.BlockSpec((tile, width), lambda i, s: (i, 0)), whole, whole],
    )


def head_grads(d_queries, d_key, d_value, tokens, number, group):
    width = d_key.shape[1]
    count = len(d_queries)
    rows = number * tokens

    def body(s_ref, *refs):
        dk_ref, dv_ref, all_ref, send_ref = refs[count:]
        first = 0
        for ref in refs[:count]:
            all_ref[first : first + ref.shape[0], :width] = ref[...]
            first += ref.shape[0]
        all_ref[:, width : 2 * width] = dk_ref[:rows, :].astype(bf16)
        all_ref[:, 2 * width :] = dv_ref[:rows, :].astype(bf16)
        for k in range(number):
            send_ref[aligned(s_ref[0] ^ k, tokens), :] = all_ref[k * tokens : (k + 1) * tokens, :]

    return call(
        body,
        "head_grads",
        [shape(rows, 3 * width, dtype=bf16)] * 2,
        [*d_queries, d_key, d_value],
        scalars=group.reshape(1),
    )


def lane_copy(value):
    return jnp.broadcast_to(value, (value.shape[0], LANES))


def attention_norm(received, weights, inputs, vectors, f, number):
    tokens, model = inputs.shape
    shard = weights[0].shape[0]
    width = received.shape[1]

    def body(f_ref, p_ref, *refs):
        w_refs = refs[:4]
        x_ref, v_ref = refs[4:6]
        normed_ref, rounded_ref, unit_ref, inverse_ref, all_ref, matrix = refs[6:]
        for k in range(4):
            matrix[aligned(f_ref[0] ^ k, shard), :] = w_refs[k][...]
        for j in range(number):
            all_ref[:, j * width : (j + 1) * width] = p_ref[j * tokens : (j + 1) * tokens, :]
        value = x_ref[...] + v_ref[0:1, :] + matmul(all_ref[...], matrix[...])
        average = jnp.mean(value, axis=-1, keepdims=True)
        centered = value - average
        inverse = lax.rsqrt(jnp.mean(centered * centered, axis=-1, keepdims=True) + epsilon)
        unit = centered * inverse
        normed = unit * v_ref[1:2, :] + v_ref[2:3, :]
        normed_ref[...] = normed
        rounded_ref[...] = normed.astype(bf16)
        unit_ref[...] = unit
        inverse_ref[...] = lane_copy(inverse)

    return call(
        body,
        "attention_norm",
        [
            shape(tokens, model),
            shape(tokens, model, dtype=bf16),
            shape(tokens, model),
            shape(tokens, LANES),
            shape(tokens, model, dtype=bf16),
        ],
        [received, *weights, inputs, vectors],
        scalars=f.reshape(1),
        scratch=[pltpu.VMEM((model, model), bf16)],
    )


def feed_specs(shard, model):
    tile = 2 * shard

    def block(t, s):
        return s[0] ^ (2 * (t // 2))

    specs = [
        pl.BlockSpec((shard, tile), lambda t, s, k=k: (8 * k + block(t, s), t % 2)) for k in range(4)
    ]
    specs.append(pl.BlockSpec((tile, model), lambda t, s: (4 * block(t, s) + 2 + t % 2, 0)))
    return specs, lambda t, s: 2 * block(t, s) + t % 2


def feed_forward(own, sibling, matrix, bias, f):
    tokens, model = own.shape
    shard = model // 4
    tile = 2 * shard

    def body(f_ref, a_ref, b_ref, *refs):
        w_refs, r_ref, bias_ref = refs[:4], refs[4], refs[5]
        act_ref, slope_ref, own_ref, other_ref, x_all = refs[6:]

        @pl.when(pl.program_id(0) == 0)
        def _():
            x_all[:tokens, :] = a_ref[...]
            x_all[tokens:, :] = b_ref[...]
            own_ref[...] = jnp.zeros_like(own_ref)
            other_ref[...] = jnp.zeros_like(other_ref)

        value = bias_ref[...]
        for k in range(4):
            value = value + matmul(x_all[:, k * shard : (k + 1) * shard], w_refs[k][...])
        below = 0.5 + 0.5 * lax.erf(value * 0.7071067811865476)
        density = 0.3989422804014327 * jnp.exp(-0.5 * value * value)
        activated = (value * below).astype(bf16)
        act_ref[...] = activated
        slope_ref[...] = (below + value * density).astype(bf16)
        own_ref[...] += matmul(activated[:tokens], r_ref[...])
        other_ref[...] += matmul(activated[tokens:], r_ref[...])

    specs, column = feed_specs(shard, model)
    wide = shape(2 * tokens, 4 * tile, dtype=bf16)
    whole = pl.BlockSpec((tokens, model), lambda t, s: (0, 0))
    return call(
        body,
        "feed_forward",
        [wide, wide, shape(tokens, model), shape(tokens, model)],
        [own, sibling, *[matrix] * 5, bias],
        scalars=f.reshape(1),
        limit=50 * 1024 * 1024,
        scratch=[pltpu.VMEM((2 * tokens, model), bf16)],
        grid=(4,),
        in_specs=[whole, whole, *specs, pl.BlockSpec((1, tile), lambda t, s: (0, column(t, s)))],
        out_specs=[pl.BlockSpec((2 * tokens, tile), lambda t, s: (0, t))] * 2 + [whole, whole],
    )


def second_norm(normed, own, received, vectors, cotangent):
    tokens, model = normed.shape
    tile = 64

    def body(n_ref, p_ref, r_ref, v_ref, c_ref, out_ref, d_ref, rounded_ref, sums_ref):
        value = n_ref[...] + p_ref[...] + r_ref[...] + v_ref[0:1, :]
        average = jnp.mean(value, axis=-1, keepdims=True)
        centered = value - average
        inverse = lax.rsqrt(jnp.mean(centered * centered, axis=-1, keepdims=True) + epsilon)
        unit = centered * inverse
        out_ref[...] = unit * v_ref[1:2, :] + v_ref[2:3, :]
        dy = c_ref[...]
        dz = dy * v_ref[1:2, :]
        mean_dz = jnp.mean(dz, axis=-1, keepdims=True)
        mean_dzz = jnp.mean(dz * unit, axis=-1, keepdims=True)
        result = inverse * (dz - mean_dz - unit * mean_dzz)
        d_ref[...] = result
        rounded = result.astype(bf16)
        rounded_ref[...] = rounded

        @pl.when(pl.program_id(0) == 0)
        def _():
            sums_ref[...] = jnp.zeros_like(sums_ref)

        sums_ref[0:1, :] += jnp.sum(dy * unit, axis=0, keepdims=True)
        sums_ref[1:2, :] += jnp.sum(dy, axis=0, keepdims=True)
        sums_ref[2:3, :] += jnp.sum(rounded.astype(f32), axis=0, keepdims=True)

    rows = pl.BlockSpec((tile, model), lambda i: (i, 0))
    fixed = pl.BlockSpec((8, model), lambda i: (0, 0))
    return call(
        body,
        "second_norm",
        [shape(tokens, model), shape(tokens, model), shape(tokens, model, dtype=bf16), shape(8, model)],
        [normed, own, received, vectors, cotangent],
        grid=(tokens // tile,),
        in_specs=[rows, rows, rows, fixed, rows],
        out_specs=[rows, rows, rows, fixed],
    )


def feed_back(own, sibling, slope, matrix, f):
    tokens, model = own.shape
    shard = model // 4
    tile = 2 * shard

    def body(f_ref, a_ref, b_ref, slope_ref, *refs):
        w_refs, r_ref = refs[:4], refs[4]
        de_ref, sums_ref, own_ref, other_ref, d_all = refs[5:]

        @pl.when(pl.program_id(0) == 0)
        def _():
            d_all[:tokens, :] = a_ref[...]
            d_all[tokens:, :] = b_ref[...]
            own_ref[...] = jnp.zeros_like(own_ref)
            other_ref[...] = jnp.zeros_like(other_ref)

        value = right_transposed(d_all[...], r_ref[...])
        rounded = (value * slope_ref[...].astype(f32)).astype(bf16)
        de_ref[...] = rounded
        sums_ref[...] = jnp.sum(rounded.astype(f32), axis=0, keepdims=True)
        for k in range(4):
            cut = slice(k * shard, (k + 1) * shard)
            own_ref[:, cut] += right_transposed(rounded[:tokens], w_refs[k][...])
            other_ref[:, cut] += right_transposed(rounded[tokens:], w_refs[k][...])

    specs, _ = feed_specs(shard, model)
    whole = pl.BlockSpec((tokens, model), lambda t, s: (0, 0))
    wide = pl.BlockSpec((2 * tokens, tile), lambda t, s: (0, t))
    return call(
        body,
        "feed_back",
        [
            shape(2 * tokens, 4 * tile, dtype=bf16),
            shape(1, 4 * tile),
            shape(tokens, model),
            shape(tokens, model),
        ],
        [own, sibling, slope, *[matrix] * 5],
        scalars=f.reshape(1),
        limit=50 * 1024 * 1024,
        scratch=[pltpu.VMEM((2 * tokens, model), bf16)],
        grid=(4,),
        in_specs=[whole, whole, wide, *specs],
        out_specs=[wide, pl.BlockSpec((1, tile), lambda t, s: (0, t)), whole, whole],
    )


def first_norm_back(d_second, own, received, unit, inverse, vectors, weights, f, number):
    tokens, model = d_second.shape
    shard = weights[0].shape[0]
    width = model // number

    def body(f_ref, d_ref, p_ref, r_ref, u_ref, i_ref, v_ref, *refs):
        w_refs = refs[:4]
        first_ref, rounded_ref, sums_ref, out_ref, matrix = refs[4:]
        for k in range(4):
            matrix[aligned(f_ref[0] ^ k, shard), :] = w_refs[k][...]
        dy = d_ref[...] + p_ref[...] + r_ref[...]
        unit_value = u_ref[...]
        dz = dy * v_ref[1:2, :]
        mean_dz = jnp.mean(dz, axis=-1, keepdims=True)
        mean_dzz = jnp.mean(dz * unit_value, axis=-1, keepdims=True)
        result = i_ref[:, 0:1] * (dz - mean_dz - unit_value * mean_dzz)
        first_ref[...] = result
        rounded = result.astype(bf16)
        rounded_ref[...] = rounded
        sums_ref[...] = jnp.zeros_like(sums_ref)
        sums_ref[0:1, :] = jnp.sum(dy * unit_value, axis=0, keepdims=True)
        sums_ref[1:2, :] = jnp.sum(dy, axis=0, keepdims=True)
        sums_ref[2:3, :] = jnp.sum(rounded.astype(f32), axis=0, keepdims=True)
        d_attended = right_transposed(rounded, matrix[...]).astype(bf16)
        for j in range(number):
            out_ref[j * tokens : (j + 1) * tokens, :] = d_attended[:, j * width : (j + 1) * width]

    return call(
        body,
        "first_norm_back",
        [
            shape(tokens, model),
            shape(tokens, model, dtype=bf16),
            shape(8, model),
            shape(number * tokens, width, dtype=bf16),
        ],
        [d_second, own, received, unit, inverse, vectors, *weights],
        scalars=f.reshape(1),
        scratch=[pltpu.VMEM((model, model), bf16)],
    )


def input_gradient(d_first, received, matrix, number):
    tokens, model = d_first.shape
    width = received.shape[1] // 3

    def body(d_ref, m_ref, r_ref, out_ref, ordered):
        for j in range(number):
            for k in range(3):
                ordered[:, k * model + j * width : k * model + (j + 1) * width] = r_ref[
                    j * tokens : (j + 1) * tokens, k * width : (k + 1) * width
                ]
        out_ref[...] = d_ref[...] + right_transposed(ordered[...], m_ref[...])

    return call(
        body,
        "input_gradient",
        shape(tokens, model),
        [d_first, matrix, received],
        scratch=[pltpu.VMEM((tokens, 3 * model), bf16)],
    )


def cast_projections(matrices, deps):
    rows, model = matrices[0].shape

    def body(q_ref, k_ref, v_ref, out_ref):
        out_ref[:, :model] = (q_ref[...] * query_scale).astype(bf16)
        out_ref[:, model : 2 * model] = k_ref[...].astype(bf16)
        out_ref[:, 2 * model :] = v_ref[...].astype(bf16)

    whole = pl.BlockSpec((rows, model), lambda: (0, 0))
    return call(
        body,
        "cast_projections",
        shape(rows, 3 * model, dtype=bf16),
        [*matrices],
        deps=deps,
        grid=(),
        in_specs=[whole] * 3,
        out_specs=pl.BlockSpec((rows, 3 * model), lambda: (0, 0)),
    )


def padded(vectors):
    return jnp.concatenate((jnp.stack(vectors), jnp.zeros((8 - len(vectors), vectors[0].shape[0]), f32)))


def per_device(
    hidden_in,
    starts,
    w_query,
    w_key,
    w_value,
    w_output,
    w_expand,
    w_reduce,
    bias_query,
    bias_value,
    bias_output,
    bias_expand,
    bias_reduce,
    attention_gain,
    attention_shift,
    feedforward_gain,
    feedforward_shift,
    cotangent,
):
    Order.last = ()
    tokens, model = hidden_in.shape[1:]
    head_size = model // HEADS
    ctx_size = lax.axis_size("ctx")
    length = tokens * ctx_size
    near = min(ctx_size, HEADS)
    copies = ctx_size // near
    heads = HEADS // near
    width = heads * head_size
    shard = w_query.shape[0]
    ff_block = w_reduce.shape[0]
    documents = starts.shape[1]
    c = lax.axis_index("ctx").astype(jnp.int32)
    f = lax.axis_index("fsdp").astype(jnp.int32)
    group = c & (near - 1)

    inputs = hidden_in[0]
    feed_matrix = lax.all_gather(cast_feed(w_expand, w_reduce), "fsdp", axis=0, tiled=True)
    blocks = gather_ctx(cast_all(inputs))

    own_columns = jnp.concatenate(
        [
            lax.dynamic_slice_in_dim(m, group * width, width, 1) * scale
            for m, scale in ((w_query, query_scale), (w_key, 1.0), (w_value, 1.0))
        ],
        axis=1,
    ).astype(bf16)

    def gather_rows(own):
        across = swap(own, "fsdp", 2)
        return [own, swap(own, "fsdp", 1), across, swap(across, "fsdp", 1)]

    projection_parts = gather_rows(own_columns)

    output_parts = gather_rows(cast_all(w_output, [blocks[1], blocks[2], blocks[4]]))

    all_projection = lax.all_gather(
        cast_projections((w_query, w_key, w_value), ()), "fsdp", axis=0, tiled=True
    )

    order = c ^ lax.iota(jnp.int32, ctx_size)
    positions = (order[:, None] * tokens + lax.iota(jnp.int32, tokens)[None, :]).reshape(-1)
    docs = jnp.sum((starts[0][None, :] <= positions[:, None]).astype(jnp.int32), axis=1) - 1
    lane = lax.iota(jnp.int32, LANES - head_size)[None, :]
    same = docs[:, None] == lane
    query_docs = jnp.where((lane < documents) & ~same, masked_value, 0.0).astype(f32)
    key_docs = jnp.where(same | ((lane >= documents) & (lane < documents + 3)), 1.0, 0.0).astype(f32)
    own_bias = jnp.concatenate(
        (
            lax.dynamic_slice_in_dim(bias_query * query_scale, group * width, width, 0),
            jnp.zeros((width,), f32),
            lax.dynamic_slice_in_dim(bias_value, group * width, width, 0),
        )
    ).reshape(1, -1)
    attention_vectors = padded((bias_output, attention_gain, attention_shift))
    feed_vectors = padded((bias_reduce, feedforward_gain, feedforward_shift))

    queries, keys, values, keys_t, stream = project(
        blocks,
        0,
        projection_parts,
        own_bias,
        query_docs,
        key_docs,
        f,
        heads,
        head_size,
        length,
        None,
        (),
    )

    out, wide, back = attend(
        queries, keys, values, group, near, tokens, head_size, documents, output_parts[1:]
    )
    received = exchange(out, near)
    normed, normed_r, first_unit, first_inverse, attended_r = attention_norm(
        received, output_parts, inputs, attention_vectors, f, near
    )

    sibling_normed = swap(normed_r, "fsdp", 1)
    activated_r, slope, partial, other = feed_forward(
        normed_r, sibling_normed, feed_matrix, bias_expand.reshape(1, -1), f
    )
    layer_out, d_second, d_reduced_r, second_sums = second_norm(
        normed, partial, swap(other, "fsdp", 1), feed_vectors, cotangent[0]
    )
    sibling_reduced = swap(d_reduced_r, "fsdp", 1)

    d_expanded_r, bias_expand_sum, partial, other = feed_back(
        d_reduced_r, sibling_reduced, slope, feed_matrix, f
    )
    other = swap(other, "fsdp", 1)

    expand_send = expand_gradients(normed_r, sibling_normed, d_expanded_r, f, (2, 3), 1, shard)
    expand_received = swap(expand_send, "fsdp", 2)
    d_first, d_attention_r, first_sums, d_attended = first_norm_back(
        d_second,
        partial,
        other,
        first_unit,
        first_inverse,
        attention_vectors,
        output_parts,
        f,
        near,
    )
    douts = exchange(d_attended, near)
    output_keep, output_send = output_gradient(
        attended_r, d_attention_r, first_sums, second_sums, bias_expand_sum, f, shard
    )
    output_received = swap(output_send, "fsdp", 1)
    low = c & 1
    reduce_send = reduce_gradient(activated_r, d_reduced_r, sibling_reduced, 1 - low, [douts])
    reduce_received = swap(reduce_send, "ctx", 1)

    rest = (2 * shard, 2 * shard + 16)
    d_query, d_key, d_value = attend_back(
        back, douts, wide, keys, values, keys_t, head_size, tokens, group
    )
    output_keep, output_send = add_parts(
        output_keep, output_received, [[(0, shard), rest], [(shard, 2 * shard), rest]]
    )
    output_received = swap(output_send, "fsdp", 2)
    expand_keep = expand_gradients(
        normed_r, sibling_normed, d_expanded_r, f, (0, 1), 0, shard
    )
    (expand_send,) = add_parts(expand_keep, expand_received, [[(2 * shard, 4 * shard)]])
    expand_other = swap(expand_send, "fsdp", 1)
    count = ctx_size
    while count > near:
        count //= 2
        received = [
            swap(d[count * tokens :].astype(bf16), "ctx", count).astype(f32) for d in (d_key, d_value)
        ]
        d_key = d_key[: count * tokens] + received[0]
        d_value = d_value[: count * tokens] + received[1]
    d_all, d_send = head_grads([d_query], d_key, d_value, tokens, near, group)
    d_mine = exchange(d_send, near)

    send, keep = projection_gradients(stream, d_all, f, shard)
    received = swap(send, "fsdp", 1)
    cut = ff_block // 2
    reduce_keep = reduce_gradient(activated_r, d_reduced_r, sibling_reduced, low)
    reduce_keep, reduce_send = add_parts(
        reduce_keep, reduce_received, [[(0, cut)], [(cut, 2 * cut)]]
    )
    reduce_received = swap(reduce_send, "fsdp", 2)
    send, keep = add_parts(keep, received, [[(0, shard), rest], [(shard, 2 * shard), rest]])
    received = swap(send, "fsdp", 2)
    expander = CtxSum(
        ctx_groups(2),
        ([expand_keep, expand_received], 0, 2 * shard),
        ([expand_other], 0, 2 * shard),
        ([output_keep, output_received], 0, shard),
    )
    expander.step()
    mine = sum_all([keep, received])
    count = ctx_size
    while count > near:
        count //= 2
        mine = sum_all([mine, swap(mine, "ctx", count)])
    reducer = CtxSum(ctx_groups()[1:], ([reduce_keep, reduce_received], 0, cut))
    reducer.step([d_mine])
    expander.step()
    reducer.step()
    input_grad = input_gradient(d_first, d_mine, all_projection, near)
    reduced, expanded = reducer.finish(), expander.finish()
    gathered = lax.all_gather(stack_sums(reduced, expanded), "ctx", axis=0, tiled=True)
    (vectors,) = add_parts(output_keep, output_received, [[(shard, shard + 16)]])
    for bit, _ in ctx_groups():
        vectors = sum_all([vectors, swap(vectors, "ctx", 1 << bit)])
    grad_query, grad_key, grad_value, grad_bias_query, grad_bias_value = place_projections(
        gather_small(mine, near), jnp.stack((group, f)), shard, width, shard
    )
    grad_w_reduce, grad_w_expand, grad_w_output, *small = place_gradients(
        gathered, vectors, f, shard, reduced[0].shape[0], ctx_size
    )
    (
        grad_bias_query,
        grad_bias_value,
        grad_att_gain,
        grad_att_shift,
        grad_bias_output,
        grad_ff_gain,
        grad_ff_shift,
        grad_bias_reduce,
        grad_bias_expand,
    ) = [v.reshape(-1) for v in (grad_bias_query, grad_bias_value, *small)]

    return (
        layer_out[None],
        input_grad[None],
        grad_query,
        grad_key,
        grad_value,
        grad_w_output,
        grad_w_expand,
        grad_w_reduce,
        grad_bias_query,
        grad_bias_value,
        grad_bias_output,
        grad_bias_expand,
        grad_bias_reduce,
        grad_att_gain,
        grad_att_shift,
        grad_ff_gain,
        grad_ff_shift,
    )


def solution(mesh):
    rows = P("fsdp", None)
    activations = P("fsdp", "ctx", None)
    return jax.shard_map(
        per_device,
        mesh=mesh,
        in_specs=(activations,) + (rows,) * 7 + (P(),) * 9 + (activations,),
        out_specs=(activations, activations) + (rows,) * 6 + (P("fsdp"),) * 9,
        check_vma=False,
    )
```

```python
import functools

import jax
import jax.numpy as jnp
from jax import lax
from jax.experimental import pallas as pl
from jax.experimental.pallas import tpu as pltpu
from jax.sharding import PartitionSpec as P

HEADS = 16
LANES = 128
epsilon = 1e-05
masked_value = -1e30
query_scale = 0.125
bf16 = jnp.bfloat16
f32 = jnp.float32
vmem_limit = 28 * 1024 * 1024


def matmul(left, right):
    return jnp.dot(left, right, preferred_element_type=f32)


def left_transposed(left, right):
    return lax.dot_general(left, right, (((0,), (0,)), ((), ())), preferred_element_type=f32)


def right_transposed(left, right):
    return lax.dot_general(left, right, (((1,), (1,)), ((), ())), preferred_element_type=f32)


def swap(array, axis, mask):
    size = lax.axis_size(axis)
    return lax.ppermute(array, axis, [(i, i ^ mask) for i in range(size)])


def shape(*sizes, dtype=f32):
    return jax.ShapeDtypeStruct(sizes, dtype)


class Order:
    last = ()


def call(
    body, name, out_shape, operands, scalars=None, scratch=(), aliases=None, deps=(), limit=vmem_limit, **grid
):
    count = 0 if scalars is None else 1
    several = isinstance(out_shape, (list, tuple))
    if not grid:
        whole = pl.BlockSpec(memory_space=pltpu.VMEM)
        grid = dict(
            grid=(),
            in_specs=[whole] * len(operands),
            out_specs=[whole] * len(out_shape) if several else whole,
        )
    extra = [*Order.last, *deps]
    first = count + len(operands)
    grid["in_specs"] = list(grid["in_specs"]) + [pl.BlockSpec(memory_space=pl.ANY)] * len(extra)

    def ordered(*refs):
        body(*refs[:first], *refs[first + len(extra) :])

    result = pl.pallas_call(
        ordered,
        out_shape=out_shape,
        grid_spec=pltpu.PrefetchScalarGridSpec(
            num_scalar_prefetch=count, scratch_shapes=list(scratch), **grid
        ),
        input_output_aliases=aliases or {},
        compiler_params=pltpu.CompilerParams(vmem_limit_bytes=limit),
        cost_estimate=pl.CostEstimate(flops=1, bytes_accessed=1, transcendentals=0),
        name=name,
    )(*([] if scalars is None else [scalars]), *operands, *extra)
    Order.last = (result[0] if several else result,)
    return result


def aligned(index, size):
    return pl.ds(pl.multiple_of(index * size, size), size)


def gather_ctx(own):
    size = lax.axis_size("ctx")
    masks = [1 << i for i in range(size.bit_length() - 1)]
    blocks = {0: own}
    for mask in reversed(masks[1:]):
        for index in list(blocks):
            blocks[index | mask] = swap(blocks[index], "ctx", mask)
    for index in list(blocks):
        if index != 2:
            blocks[index | 1] = swap(blocks[index], "ctx", 1)
    blocks[3] = swap(blocks[1], "ctx", 2)
    return [blocks[i] for i in range(len(blocks))]


def gather_small(own, number):
    blocks = {0: own}
    for index in range(2, number, 2):
        blocks[index] = swap(own, "ctx", index)
    for index in list(blocks):
        blocks[index | 1] = swap(blocks[index], "ctx", 1)
    return [blocks[i] for i in range(number)]


def exchange(array, number):
    size = lax.axis_size("ctx")
    if number == size:
        return lax.all_to_all(array, "ctx", 0, 0, tiled=True)
    rows = array.shape[0] // number
    own = lax.axis_index("ctx").astype(jnp.int32) & (number - 1)
    result = jnp.zeros_like(array)
    for i in range(number):
        block = lax.dynamic_slice_in_dim(array, (own ^ i) * rows, rows, 0)
        block = block if i == 0 else swap(block, "ctx", i)
        result = lax.dynamic_update_slice_in_dim(result, block, (own ^ i) * rows, 0)
    return result


def ctx_groups(together=1):
    bits = lax.axis_size("ctx").bit_length() - 1
    groups, first = [(0, 2)], 1
    while first < bits:
        count = min(together, bits - first)
        groups.append((first, 1 << count))
        first += count
    return groups


def piece_of(index, size, together=1):
    bits = size.bit_length() - 1
    piece, first, count = 0, 0, 1
    while first < bits:
        piece = (piece << count) | ((index >> first) & ((1 << count) - 1))
        first += count
        count = min(together, bits - first)
    return piece


def sum_split(segments, members, place, rows, deps):
    width = segments[0][0][0].shape[1]
    size = rows // members
    number = sum(len(arrays) for arrays, _, _ in segments)

    def body(place_ref, *refs):
        ins, outs, total = refs[:number], refs[number:-1], refs[-1]
        first = at = 0
        for arrays, begin, end in segments:
            value = ins[at][begin:end, :].astype(f32)
            for ref in ins[at + 1 : at + len(arrays)]:
                value = value + ref[begin:end, :].astype(f32)
            total[first : first + end - begin, :] = value.astype(bf16)
            first += end - begin
            at += len(arrays)
        if first < rows:
            total[first:, :] = jnp.zeros((rows - first, width), bf16)
        for m in range(members):
            outs[m][...] = total[aligned(place_ref[0] ^ m, size), :]

    return call(
        body,
        "sum_split",
        [shape(size, width, dtype=bf16)] * members,
        [array for arrays, _, _ in segments for array in arrays],
        deps=deps,
        scalars=place.reshape(1),
        scratch=[pltpu.VMEM((rows, width), bf16)],
    )


def sum_all(arrays, dtype=bf16):
    def body(*refs):
        value = refs[0][...].astype(f32)
        for ref in refs[1:-1]:
            value = value + ref[...].astype(f32)
        refs[-1][...] = value.astype(dtype)

    return call(body, "sum_all", shape(*arrays[0].shape, dtype=dtype), arrays)


class CtxSum:
    def __init__(self, groups, *segments):
        self.index = lax.axis_index("ctx").astype(jnp.int32)
        self.groups = list(groups)
        self.segments = segments
        unit = 16
        for _, members in groups:
            unit *= members
        self.rows = -(-sum(end - begin for _, begin, end in segments) // unit) * unit

    def step(self, deps=()):
        if not self.groups:
            return
        first, members = self.groups.pop(0)
        place = (self.index >> first) & (members - 1)
        pieces = sum_split(self.segments, members, place, self.rows, deps)
        self.rows //= members
        arrays = [pieces[0]] + [swap(pieces[m], "ctx", m << first) for m in range(1, members)]
        self.segments = [(arrays, 0, self.rows)]

    def finish(self):
        while self.groups:
            self.step()
        return self.segments[0][0]


def stack_sums(first, second):
    sizes = [first[0].shape[0], second[0].shape[0]]

    def body(*refs):
        for begin, refs_of in ((0, refs[: len(first)]), (sizes[0], refs[len(first) : -1])):
            value = refs_of[0][...].astype(f32)
            for ref in refs_of[1:]:
                value = value + ref[...].astype(f32)
            refs[-1][begin : begin + value.shape[0], :] = value.astype(bf16)

    return call(
        body, "stack_sums", shape(sum(sizes), first[0].shape[1], dtype=bf16), [*first, *second]
    )


def place_gradients(gathered, vectors, f, shard, rows, size):
    piece = gathered.shape[0] // size
    columns = gathered.shape[1]
    below = piece - rows

    def body(f_ref, in_ref, v_ref, reduce_ref, expand_ref, output_ref, *refs):
        outs, ordered, small = refs[:-2], refs[-2], refs[-1]
        at = pl.program_id(0)
        reduce_ref[...] = in_ref[0, :rows, :].astype(f32)
        ordered[aligned(piece_of(at, size, 2), below), :] = in_ref[0, rows:, :]

        @pl.when(at == size - 1)
        def _():
            for unit, k in enumerate((0, 2, 1, 3)):
                expand_ref[:, aligned(f_ref[0] ^ k, columns)] = ordered[
                    unit * shard : (unit + 1) * shard, :
                ].astype(f32)
            output_ref[...] = ordered[4 * shard : 5 * shard, :].astype(f32)
            small[...] = v_ref[...].astype(f32)
            for k in range(6):
                outs[k][...] = small[k : k + 1, aligned(f_ref[0], shard)]
            outs[6][...] = small[pl.ds(8 + f_ref[0], 1), :]

    def whole(*sizes):
        return pl.BlockSpec(sizes, lambda p, s: (0, 0))

    return call(
        body,
        "place_gradients",
        [shape(size * rows, columns), shape(shard, 4 * columns), shape(shard, columns)]
        + [shape(1, shard)] * 6
        + [shape(1, columns)],
        [gathered.reshape(size, piece, columns), vectors],
        scalars=f.reshape(1),
        scratch=[pltpu.VMEM((size * below, columns), bf16), pltpu.VMEM((16, columns), f32)],
        limit=2 * vmem_limit,
        grid=(size,),
        in_specs=[pl.BlockSpec((1, piece, columns), lambda j, s: (j, 0, 0)), whole(16, columns)],
        out_specs=[
            pl.BlockSpec((rows, columns), lambda j, s: (piece_of(j, size), 0)),
            whole(shard, 4 * columns),
            whole(shard, columns),
        ]
        + [whole(1, shard)] * 6
        + [whole(1, columns)],
    )


def cast_feed(expand, reduce):
    shard, columns = expand.shape
    block = columns // 4

    def body(e_ref, r_ref, out_ref):
        at = pl.program_id(0)

        @pl.when(at < 4)
        def _():
            out_ref[...] = e_ref[...].astype(bf16)

        @pl.when(at >= 4)
        def _():
            out_ref[...] = r_ref[...].astype(bf16)

    return call(
        body,
        "cast_feed",
        shape(4 * shard + reduce.shape[0], block, dtype=bf16),
        [expand, reduce],
        grid=(8,),
        in_specs=[
            pl.BlockSpec((shard, block), lambda i: (0, jnp.minimum(i, 3))),
            pl.BlockSpec((reduce.shape[0] // 4, block), lambda i: (jnp.maximum(i - 4, 0), 0)),
        ],
        out_specs=pl.BlockSpec((shard, block), lambda i: (i, 0)),
    )


def cast_all(matrix, deps=()):
    rows, columns = matrix.shape
    tile = min(rows, 256)

    def body(in_ref, out_ref):
        out_ref[...] = in_ref[...].astype(bf16)

    spec = pl.BlockSpec((tile, columns), lambda i: (i, 0))
    return call(
        body,
        "cast_all",
        shape(rows, columns, dtype=bf16),
        [matrix],
        deps=deps,
        grid=(rows // tile,),
        in_specs=[spec],
        out_specs=spec,
    )


def reduce_gradient(activated, own, sibling, half, deps=()):
    rows, columns = activated.shape
    tokens, model = own.shape
    tile = columns // 4

    def body(h_ref, a_ref, d_ref, s_ref, out_ref):
        value = left_transposed(a_ref[:tokens, :], d_ref[...])
        out_ref[...] = (value + left_transposed(a_ref[tokens:, :], s_ref[...])).astype(bf16)

    whole = pl.BlockSpec((tokens, model), lambda i, s: (0, 0))
    return call(
        body,
        "reduce_gradient",
        shape(columns // 2, model, dtype=bf16),
        [activated, own, sibling],
        deps=deps,
        scalars=half.reshape(1),
        grid=(2,),
        in_specs=[pl.BlockSpec((rows, tile), lambda i, s: (0, 2 * i + s[0])), whole, whole],
        out_specs=pl.BlockSpec((tile, model), lambda i, s: (i, 0)),
    )


def expand_gradients(own, sibling, d_expanded, f, row_blocks, flip, shard, deps=()):
    tokens, model = own.shape
    columns = d_expanded.shape[1] // 2

    def body(f_ref, a_ref, b_ref, d_ref, out_ref):
        value = left_transposed(a_ref[...], d_ref[:tokens, :])
        out_ref[...] = (value + left_transposed(b_ref[...], d_ref[tokens:, :])).astype(bf16)

    def rows_map(i, s):
        return (0, s[0] ^ jnp.where(i < 2, row_blocks[0], row_blocks[1]))

    left = pl.BlockSpec((tokens, shard), rows_map)
    return call(
        body,
        "expand_gradients",
        shape(4 * shard, columns, dtype=bf16),
        [own, sibling, d_expanded],
        deps=deps,
        scalars=f.reshape(1),
        grid=(4,),
        in_specs=[left, left, pl.BlockSpec((2 * tokens, columns), lambda i, s: (0, (i % 2) ^ flip))],
        out_specs=pl.BlockSpec((shard, columns), lambda i, s: (i, 0)),
    )


def output_gradient(attended, d_attention, first_sums, second_sums, bias_sums, f, shard):
    model = d_attention.shape[1]
    tile = 256
    steps = model // tile

    def body(s_ref, a_ref, d_ref, first_ref, second_ref, bias_ref, keep_ref, send_ref, rows, small):
        step = pl.program_id(0)
        rows[aligned(step, tile), :] = left_transposed(a_ref[...], d_ref[...]).astype(bf16)

        @pl.when(step == steps - 1)
        def _():
            small[...] = jnp.zeros_like(small)
            small[0:3, :] = first_ref[0:3, :]
            small[3:6, :] = second_ref[0:3, :]
            for k in range(2):
                small[pl.ds(8 + (s_ref[0] ^ (2 * k)), 1), :] = bias_ref[
                    :, k * model : (k + 1) * model
                ]
            for out_ref, blocks in ((keep_ref, (0, 2)), (send_ref, (1, 3))):
                for k, block in enumerate(blocks):
                    out_ref[k * shard : (k + 1) * shard, :] = rows[
                        aligned(s_ref[0] ^ block, shard), :
                    ]
                out_ref[2 * shard :, :] = small[...].astype(bf16)

    total = 2 * shard + 16
    whole = pl.BlockSpec((total, model), lambda i, s: (0, 0))
    return call(
        body,
        "output_gradient",
        [shape(total, model, dtype=bf16)] * 2,
        [attended, d_attention, first_sums, second_sums, bias_sums],
        scalars=f.reshape(1),
        scratch=[pltpu.VMEM((model, model), bf16), pltpu.VMEM((16, model), f32)],
        grid=(steps,),
        in_specs=[pl.BlockSpec((attended.shape[0], tile), lambda i, s: (0, i))]
        + [
            pl.BlockSpec(array.shape, lambda i, s: (0, 0))
            for array in (d_attention, first_sums, second_sums, bias_sums)
        ],
        out_specs=[whole, whole],
    )


def add_parts(first, second, parts):
    width = first.shape[1]

    def body(a_ref, b_ref, *outs):
        for out_ref, ranges in zip(outs, parts):
            at = 0
            for begin, end in ranges:
                value = a_ref[begin:end, :].astype(f32) + b_ref[begin:end, :].astype(f32)
                out_ref[at : at + end - begin, :] = value.astype(bf16)
                at += end - begin

    return call(
        body,
        "add_parts",
        [shape(sum(e - b for b, e in ranges), width, dtype=bf16) for ranges in parts],
        [first, second],
    )


def projection_gradients(stream, d_all, f, shard):
    rows, width = d_all.shape
    model = stream.shape[1]
    tile = 512
    steps = rows // tile

    def body(f_ref, x_ref, d_ref, send_ref, keep_ref, total, sums, rounded):
        step = pl.program_id(0)

        @pl.when(step == 0)
        def _():
            total[...] = jnp.zeros_like(total)
            sums[...] = jnp.zeros_like(sums)

        d_value = d_ref[...]
        total[...] += left_transposed(x_ref[...], d_value)
        sums[...] += jnp.sum(d_value.astype(f32), axis=0, keepdims=True)

        @pl.when(step == steps - 1)
        def _():
            lane = lax.broadcasted_iota(jnp.int32, (1, width), 1)
            scale = jnp.where(lane < width // 3, query_scale, 1.0)
            rounded[...] = (total[...] * scale).astype(bf16)
            bias = jnp.broadcast_to(sums[...] * scale, (16, width)).astype(bf16)
            for out_ref, blocks in ((send_ref, (3, 1)), (keep_ref, (2, 0))):
                for k, block in enumerate(blocks):
                    out_ref[k * shard : (k + 1) * shard, :] = rounded[
                        aligned(f_ref[0] ^ block, shard), :
                    ]
                out_ref[2 * shard :, :] = bias

    out = shape(2 * shard + 16, width, dtype=bf16)
    whole = pl.BlockSpec((2 * shard + 16, width), lambda i, s: (0, 0))
    return call(
        body,
        "projection_gradients",
        [out, out],
        [stream, d_all],
        scalars=f.reshape(1),
        scratch=[
            pltpu.VMEM((model, width), f32),
            pltpu.VMEM((1, width), f32),
            pltpu.VMEM((model, width), bf16),
        ],
        grid=(steps,),
        in_specs=[
            pl.BlockSpec((tile, model), lambda i, s: (i, 0)),
            pl.BlockSpec((tile, width), lambda i, s: (i, 0)),
        ],
        out_specs=[whole, whole],
    )


def place_projections(pieces, scalars, rows, width, shard):
    count = len(pieces)
    if width % LANES:
        order = jnp.arange(count) ^ scalars[0]
        ordered = jnp.take(jnp.stack(pieces), order, axis=0)
        weights = jnp.transpose(ordered[:, :rows], (1, 0, 2)).astype(f32)
        biases = ordered[:, rows].astype(f32)
        return [
            weights[:, :, k * width : (k + 1) * width].reshape(rows, count * width)
            for k in range(3)
        ] + [
            lax.dynamic_slice_in_dim(
                biases[:, k * width : (k + 1) * width].reshape(1, -1), scalars[1] * shard, shard, 1
            )
            for k in (0, 2)
        ]

    def body(s_ref, *refs):
        outs, sums = refs[count:-1], refs[-1]
        for i in range(count):
            where = aligned(s_ref[0] ^ i, width)
            for k in range(3):
                cut = slice(k * width, (k + 1) * width)
                outs[k][:, where] = refs[i][:rows, cut].astype(f32)
                sums[k : k + 1, where] = refs[i][rows : rows + 16, cut].astype(f32)[0:1, :]
        for k, row in ((3, 0), (4, 2)):
            outs[k][...] = sums[row : row + 1, aligned(s_ref[1], shard)]

    return call(
        body,
        "place_projections",
        [shape(rows, count * width)] * 3 + [shape(1, shard)] * 2,
        pieces,
        scalars=scalars,
        scratch=[pltpu.VMEM((8, count * width), f32)],
    )


def project(blocks, first, weights, bias, query_docs, key_docs, own, heads, head_size, length, before, deps):
    tokens, model = blocks[0].shape
    width = heads * head_size
    shard = weights[0].shape[0]
    number = len(blocks)
    rows = number * tokens
    tile = 256
    per_block = tokens // tile
    start = first * per_block

    def body(own_ref, *refs):
        x_refs, w_refs = refs[:number], refs[number : number + 4]
        b_ref, qd_ref, kd_ref = refs[number + 4 : number + 7]
        q_ref, k_ref, v_ref, kt_ref, x_out = refs[-5:]
        for k in range(number):

            @pl.when(pl.program_id(0) // per_block == k)
            def _():
                x_out[...] = x_refs[k][...]

        product = b_ref[...]
        for k in range(4):
            product = product + matmul(x_out[:, aligned(own_ref[0] ^ k, shard)], w_refs[k][...])
        lane = lax.broadcasted_iota(jnp.int32, (tile, LANES - head_size), 1)
        ones = jnp.where(lane < 3, 1.0, 0.0).astype(f32)
        keys = product[:, width : 2 * width]
        for h in range(heads):
            cut = slice(h * head_size, (h + 1) * head_size)
            q_ref[h] = jnp.concatenate((product[:, :width][:, cut], qd_ref[...]), 1).astype(bf16)
            k_ref[h] = jnp.concatenate((keys[:, cut], kd_ref[...]), 1).astype(bf16)
            v_ref[h] = jnp.concatenate((product[:, 2 * width :][:, cut], ones), 1).astype(bf16)
        kt_ref[...] = jnp.transpose(keys).astype(bf16)

    out = shape(heads, length, LANES, dtype=bf16)
    out_spec = pl.BlockSpec((heads, tile, LANES), lambda i, s: (0, i + start, 0))
    extra_spec = pl.BlockSpec((tile, LANES - head_size), lambda i, s: (i + start, 0))
    old = list(before) if before is not None else []

    def block_map(k, i, s):
        return (jnp.clip(i - k * per_block, 0, per_block - 1), 0)

    operands = [*blocks, *weights, bias, query_docs, key_docs, *old]
    return call(
        body,
        "project",
        [out, out, out, shape(width, length, dtype=bf16), shape(length, model, dtype=bf16)],
        operands,
        scalars=own.reshape(1),
        deps=deps,
        aliases={1 + len(operands) - 5 + k: k for k in range(5)} if old else None,
        grid=(rows // tile,),
        in_specs=[pl.BlockSpec((tile, model), functools.partial(block_map, k)) for k in range(number)]
        + [pl.BlockSpec((shard, 3 * width), lambda i, s: (0, 0))] * 4
        + [pl.BlockSpec((1, 3 * width), lambda i, s: (0, 0)), extra_spec, extra_spec]
        + [pl.BlockSpec(memory_space=pl.ANY)] * len(old),
        out_specs=[
            out_spec,
            out_spec,
            out_spec,
            pl.BlockSpec((width, tile), lambda i, s: (0, i + start)),
            pl.BlockSpec((tile, model), lambda i, s: (i + start, 0)),
        ],
    )


def three_parts(value):
    high = value.astype(bf16).astype(f32)
    rest = value - high
    middle = rest.astype(bf16).astype(f32)
    return high, middle, rest - middle


def attend(queries, keys, values, group, number, tokens, head_size, docs, deps):
    heads, length, _ = keys.shape
    width = heads * head_size
    tile = 2 * tokens if length <= 4096 else 128
    per, span = max(1, tokens // tile), max(1, tile // tokens)
    rows = number * tokens
    chunk = min(length, 1024)

    def body(s_ref, q_ref, k_ref, v_ref, out_ref, wide_ref, back_ref):
        lane = lax.broadcasted_iota(jnp.int32, (tile, LANES), 1)
        for h in range(heads):
            query = q_ref[h]
            largest = summed = None
            for first in range(0, length, chunk):
                scores = right_transposed(query, k_ref[h, first : first + chunk, :])
                before = largest
                largest = jnp.max(scores, axis=1, keepdims=True)
                if before is not None:
                    largest = jnp.maximum(before, largest)
                    summed = summed * jnp.exp(before - largest)
                weights = jnp.exp(scores - largest).astype(bf16)
                part = matmul(weights, v_ref[h, first : first + chunk, :])
                summed = part if before is None else summed + part
            total = summed[:, head_size : head_size + 1]
            cut = slice(h * head_size, (h + 1) * head_size)
            attended = summed[:, :head_size] / total
            wide_ref[:, cut] = attended
            for b in range(span):
                where = aligned((b ^ s_ref[0]) & (span - 1), tile // span)
                out_ref[where, cut] = attended[b * tokens : (b + 1) * tokens].astype(bf16)
            parts = three_parts(-(largest + jnp.log(total)))
            back = query.astype(f32)
            for k in range(3):
                back = jnp.where(lane == head_size + docs + k, parts[k], back)
            back_ref[h] = back.astype(bf16)

    return call(
        body,
        "attend",
        [
            shape(rows, width, dtype=bf16),
            shape(rows, width),
            shape(heads, rows, LANES, dtype=bf16),
        ],
        [queries, keys, values],
        deps=deps,
        limit=40 * 1024 * 1024,
        scalars=group.reshape(1),
        grid=(rows // tile,),
        in_specs=[
            pl.BlockSpec((heads, tile, LANES), lambda i, s: (0, i, 0)),
            pl.BlockSpec((heads, length, LANES), lambda i, s: (0, 0, 0)),
            pl.BlockSpec((heads, length, LANES), lambda i, s: (0, 0, 0)),
        ],
        out_specs=[
            pl.BlockSpec((tile, width), lambda i, s: (((i // per) ^ (s[0] // span)) * per + i % per, 0)),
            pl.BlockSpec((tile, width), lambda i, s: (i, 0)),
            pl.BlockSpec((heads, tile, LANES), lambda i, s: (0, i, 0)),
        ],
    )


def attend_back(queries, douts, attended, keys, values, keys_t, head_size, tokens, group):
    heads, length, _ = keys.shape
    rows = attended.shape[0]
    width = heads * head_size
    tile = 2 * tokens if length <= 4096 else 128
    per, span = max(1, tokens // tile), max(1, tile // tokens)

    def body(s_ref, q_ref, d_ref, a_ref, k_ref, v_ref, kt_ref, dq_ref, dk_ref, dv_ref):
        @pl.when(pl.program_id(0) == 0)
        def _():
            dk_ref[...] = jnp.zeros_like(dk_ref)
            dv_ref[...] = jnp.zeros_like(dv_ref)

        lane = lax.broadcasted_iota(jnp.int32, (tile, LANES - head_size), 1)
        for h in range(heads):
            cut = slice(h * head_size, (h + 1) * head_size)
            dout = jnp.concatenate(
                [
                    d_ref[aligned((b ^ s_ref[0]) & (span - 1), tile // span), cut]
                    for b in range(span)
                ],
                axis=0,
            ).astype(f32)
            parts = three_parts(-jnp.sum(dout * a_ref[:, cut], axis=1, keepdims=True))
            extra = jnp.zeros((tile, LANES - head_size), f32)
            for k in range(3):
                extra = jnp.where(lane == k, parts[k], extra)
            dout = jnp.concatenate((dout, extra), axis=1).astype(bf16)
            query = q_ref[h]
            probabilities = jnp.exp(right_transposed(k_ref[h], query))
            grads = right_transposed(v_ref[h], dout)
            d_scores = (probabilities * grads).astype(bf16)
            dk_ref[:, cut] += matmul(d_scores, query)[:, :head_size]
            dv_ref[:, cut] += matmul(probabilities.astype(bf16), dout)[:, :head_size]
            dq_t = matmul(kt_ref[cut, :], d_scores)
            dq_ref[:, cut] = jnp.transpose(dq_t).astype(bf16)

    whole = pl.BlockSpec((length, width), lambda i, s: (0, 0))
    resident = pl.BlockSpec((heads, length, LANES), lambda i, s: (0, 0, 0))

    def dout_map(i, s):
        return (((i // per) ^ (s[0] // span)) * per + i % per, 0)

    in_specs = [
        pl.BlockSpec((heads, tile, LANES), lambda i, s: (0, i, 0)),
        pl.BlockSpec((tile, width), dout_map),
        pl.BlockSpec((tile, width), lambda i, s: (i, 0)),
        resident,
        resident,
        pl.BlockSpec((width, length), lambda i, s: (0, 0)),
    ]
    operands = [queries, douts, attended, keys, values, keys_t]
    return call(
        body,
        "attend_back",
        [shape(rows, width, dtype=bf16), shape(length, width), shape(length, width)],
        operands,
        scalars=group.reshape(1),
        limit=40 * 1024 * 1024 if length <= 4096 else 2 * vmem_limit,
        grid=(rows // tile,),
        in_specs=in_specs,
        out_specs=[pl.BlockSpec((tile, width), lambda i, s: (i, 0)), whole, whole],
    )


def head_grads(d_queries, d_key, d_value, tokens, number, group):
    width = d_key.shape[1]
    count = len(d_queries)
    rows = number * tokens

    def body(s_ref, *refs):
        dk_ref, dv_ref, all_ref, send_ref = refs[count:]
        first = 0
        for ref in refs[:count]:
            all_ref[first : first + ref.shape[0], :width] = ref[...]
            first += ref.shape[0]
        all_ref[:, width : 2 * width] = dk_ref[:rows, :].astype(bf16)
        all_ref[:, 2 * width :] = dv_ref[:rows, :].astype(bf16)
        for k in range(number):
            send_ref[aligned(s_ref[0] ^ k, tokens), :] = all_ref[k * tokens : (k + 1) * tokens, :]

    return call(
        body,
        "head_grads",
        [shape(rows, 3 * width, dtype=bf16)] * 2,
        [*d_queries, d_key, d_value],
        scalars=group.reshape(1),
    )


def lane_copy(value):
    return jnp.broadcast_to(value, (value.shape[0], LANES))


def attention_norm(received, weights, inputs, vectors, f, number):
    tokens, model = inputs.shape
    shard = weights[0].shape[0]
    width = received.shape[1]

    def body(f_ref, p_ref, *refs):
        w_refs = refs[:4]
        x_ref, v_ref = refs[4:6]
        normed_ref, rounded_ref, unit_ref, inverse_ref, all_ref, matrix = refs[6:]
        for k in range(4):
            matrix[aligned(f_ref[0] ^ k, shard), :] = w_refs[k][...]
        for j in range(number):
            all_ref[:, j * width : (j + 1) * width] = p_ref[j * tokens : (j + 1) * tokens, :]
        value = x_ref[...] + v_ref[0:1, :] + matmul(all_ref[...], matrix[...])
        average = jnp.mean(value, axis=-1, keepdims=True)
        centered = value - average
        inverse = lax.rsqrt(jnp.mean(centered * centered, axis=-1, keepdims=True) + epsilon)
        unit = centered * inverse
        normed = unit * v_ref[1:2, :] + v_ref[2:3, :]
        normed_ref[...] = normed
        rounded_ref[...] = normed.astype(bf16)
        unit_ref[...] = unit
        inverse_ref[...] = lane_copy(inverse)

    return call(
        body,
        "attention_norm",
        [
            shape(tokens, model),
            shape(tokens, model, dtype=bf16),
            shape(tokens, model),
            shape(tokens, LANES),
            shape(tokens, model, dtype=bf16),
        ],
        [received, *weights, inputs, vectors],
        scalars=f.reshape(1),
        scratch=[pltpu.VMEM((model, model), bf16)],
    )


def feed_specs(shard, model):
    tile = 2 * shard

    def block(t, s):
        return s[0] ^ (2 * (t // 2))

    specs = [
        pl.BlockSpec((shard, tile), lambda t, s, k=k: (8 * k + block(t, s), t % 2)) for k in range(4)
    ]
    specs.append(pl.BlockSpec((tile, model), lambda t, s: (4 * block(t, s) + 2 + t % 2, 0)))
    return specs, lambda t, s: 2 * block(t, s) + t % 2


def feed_forward(own, sibling, matrix, bias, f):
    tokens, model = own.shape
    shard = model // 4
    tile = 2 * shard

    def body(f_ref, a_ref, b_ref, *refs):
        w_refs, r_ref, bias_ref = refs[:4], refs[4], refs[5]
        act_ref, slope_ref, own_ref, other_ref, x_all = refs[6:]

        @pl.when(pl.program_id(0) == 0)
        def _():
            x_all[:tokens, :] = a_ref[...]
            x_all[tokens:, :] = b_ref[...]
            own_ref[...] = jnp.zeros_like(own_ref)
            other_ref[...] = jnp.zeros_like(other_ref)

        value = bias_ref[...]
        for k in range(4):
            value = value + matmul(x_all[:, k * shard : (k + 1) * shard], w_refs[k][...])
        below = 0.5 + 0.5 * lax.erf(value * 0.7071067811865476)
        density = 0.3989422804014327 * jnp.exp(-0.5 * value * value)
        activated = (value * below).astype(bf16)
        act_ref[...] = activated
        slope_ref[...] = (below + value * density).astype(bf16)
        own_ref[...] += matmul(activated[:tokens], r_ref[...])
        other_ref[...] += matmul(activated[tokens:], r_ref[...])

    specs, column = feed_specs(shard, model)
    wide = shape(2 * tokens, 4 * tile, dtype=bf16)
    whole = pl.BlockSpec((tokens, model), lambda t, s: (0, 0))
    return call(
        body,
        "feed_forward",
        [wide, wide, shape(tokens, model), shape(tokens, model)],
        [own, sibling, *[matrix] * 5, bias],
        scalars=f.reshape(1),
        limit=50 * 1024 * 1024,
        scratch=[pltpu.VMEM((2 * tokens, model), bf16)],
        grid=(4,),
        in_specs=[whole, whole, *specs, pl.BlockSpec((1, tile), lambda t, s: (0, column(t, s)))],
        out_specs=[pl.BlockSpec((2 * tokens, tile), lambda t, s: (0, t))] * 2 + [whole, whole],
    )


def second_norm(normed, own, received, vectors, cotangent):
    tokens, model = normed.shape
    tile = 64

    def body(n_ref, p_ref, r_ref, v_ref, c_ref, out_ref, d_ref, rounded_ref, sums_ref):
        value = n_ref[...] + p_ref[...] + r_ref[...] + v_ref[0:1, :]
        average = jnp.mean(value, axis=-1, keepdims=True)
        centered = value - average
        inverse = lax.rsqrt(jnp.mean(centered * centered, axis=-1, keepdims=True) + epsilon)
        unit = centered * inverse
        out_ref[...] = unit * v_ref[1:2, :] + v_ref[2:3, :]
        dy = c_ref[...]
        dz = dy * v_ref[1:2, :]
        mean_dz = jnp.mean(dz, axis=-1, keepdims=True)
        mean_dzz = jnp.mean(dz * unit, axis=-1, keepdims=True)
        result = inverse * (dz - mean_dz - unit * mean_dzz)
        d_ref[...] = result
        rounded = result.astype(bf16)
        rounded_ref[...] = rounded

        @pl.when(pl.program_id(0) == 0)
        def _():
            sums_ref[...] = jnp.zeros_like(sums_ref)

        sums_ref[0:1, :] += jnp.sum(dy * unit, axis=0, keepdims=True)
        sums_ref[1:2, :] += jnp.sum(dy, axis=0, keepdims=True)
        sums_ref[2:3, :] += jnp.sum(rounded.astype(f32), axis=0, keepdims=True)

    rows = pl.BlockSpec((tile, model), lambda i: (i, 0))
    fixed = pl.BlockSpec((8, model), lambda i: (0, 0))
    return call(
        body,
        "second_norm",
        [shape(tokens, model), shape(tokens, model), shape(tokens, model, dtype=bf16), shape(8, model)],
        [normed, own, received, vectors, cotangent],
        grid=(tokens // tile,),
        in_specs=[rows, rows, rows, fixed, rows],
        out_specs=[rows, rows, rows, fixed],
    )


def feed_back(own, sibling, slope, matrix, f):
    tokens, model = own.shape
    shard = model // 4
    tile = 2 * shard

    def body(f_ref, a_ref, b_ref, slope_ref, *refs):
        w_refs, r_ref = refs[:4], refs[4]
        de_ref, sums_ref, own_ref, other_ref, d_all = refs[5:]

        @pl.when(pl.program_id(0) == 0)
        def _():
            d_all[:tokens, :] = a_ref[...]
            d_all[tokens:, :] = b_ref[...]
            own_ref[...] = jnp.zeros_like(own_ref)
            other_ref[...] = jnp.zeros_like(other_ref)

        value = right_transposed(d_all[...], r_ref[...])
        rounded = (value * slope_ref[...].astype(f32)).astype(bf16)
        de_ref[...] = rounded
        sums_ref[...] = jnp.sum(rounded.astype(f32), axis=0, keepdims=True)
        for k in range(4):
            cut = slice(k * shard, (k + 1) * shard)
            own_ref[:, cut] += right_transposed(rounded[:tokens], w_refs[k][...])
            other_ref[:, cut] += right_transposed(rounded[tokens:], w_refs[k][...])

    specs, _ = feed_specs(shard, model)
    whole = pl.BlockSpec((tokens, model), lambda t, s: (0, 0))
    wide = pl.BlockSpec((2 * tokens, tile), lambda t, s: (0, t))
    return call(
        body,
        "feed_back",
        [
            shape(2 * tokens, 4 * tile, dtype=bf16),
            shape(1, 4 * tile),
            shape(tokens, model),
            shape(tokens, model),
        ],
        [own, sibling, slope, *[matrix] * 5],
        scalars=f.reshape(1),
        limit=50 * 1024 * 1024,
        scratch=[pltpu.VMEM((2 * tokens, model), bf16)],
        grid=(4,),
        in_specs=[whole, whole, wide, *specs],
        out_specs=[wide, pl.BlockSpec((1, tile), lambda t, s: (0, t)), whole, whole],
    )


def first_norm_back(d_second, own, received, unit, inverse, vectors, weights, f, number):
    tokens, model = d_second.shape
    shard = weights[0].shape[0]
    width = model // number

    def body(f_ref, d_ref, p_ref, r_ref, u_ref, i_ref, v_ref, *refs):
        w_refs = refs[:4]
        first_ref, rounded_ref, sums_ref, out_ref, matrix = refs[4:]
        for k in range(4):
            matrix[aligned(f_ref[0] ^ k, shard), :] = w_refs[k][...]
        dy = d_ref[...] + p_ref[...] + r_ref[...]
        unit_value = u_ref[...]
        dz = dy * v_ref[1:2, :]
        mean_dz = jnp.mean(dz, axis=-1, keepdims=True)
        mean_dzz = jnp.mean(dz * unit_value, axis=-1, keepdims=True)
        result = i_ref[:, 0:1] * (dz - mean_dz - unit_value * mean_dzz)
        first_ref[...] = result
        rounded = result.astype(bf16)
        rounded_ref[...] = rounded
        sums_ref[...] = jnp.zeros_like(sums_ref)
        sums_ref[0:1, :] = jnp.sum(dy * unit_value, axis=0, keepdims=True)
        sums_ref[1:2, :] = jnp.sum(dy, axis=0, keepdims=True)
        sums_ref[2:3, :] = jnp.sum(rounded.astype(f32), axis=0, keepdims=True)
        d_attended = right_transposed(rounded, matrix[...]).astype(bf16)
        for j in range(number):
            out_ref[j * tokens : (j + 1) * tokens, :] = d_attended[:, j * width : (j + 1) * width]

    return call(
        body,
        "first_norm_back",
        [
            shape(tokens, model),
            shape(tokens, model, dtype=bf16),
            shape(8, model),
            shape(number * tokens, width, dtype=bf16),
        ],
        [d_second, own, received, unit, inverse, vectors, *weights],
        scalars=f.reshape(1),
        scratch=[pltpu.VMEM((model, model), bf16)],
    )


def input_gradient(d_first, received, matrix, number):
    tokens, model = d_first.shape
    width = received.shape[1] // 3

    def body(d_ref, m_ref, r_ref, out_ref, ordered):
        for j in range(number):
            for k in range(3):
                ordered[:, k * model + j * width : k * model + (j + 1) * width] = r_ref[
                    j * tokens : (j + 1) * tokens, k * width : (k + 1) * width
                ]
        out_ref[...] = d_ref[...] + right_transposed(ordered[...], m_ref[...])

    return call(
        body,
        "input_gradient",
        shape(tokens, model),
        [d_first, matrix, received],
        scratch=[pltpu.VMEM((tokens, 3 * model), bf16)],
    )


def cast_projections(matrices, deps):
    rows, model = matrices[0].shape

    def body(q_ref, k_ref, v_ref, out_ref):
        out_ref[:, :model] = (q_ref[...] * query_scale).astype(bf16)
        out_ref[:, model : 2 * model] = k_ref[...].astype(bf16)
        out_ref[:, 2 * model :] = v_ref[...].astype(bf16)

    whole = pl.BlockSpec((rows, model), lambda: (0, 0))
    return call(
        body,
        "cast_projections",
        shape(rows, 3 * model, dtype=bf16),
        [*matrices],
        deps=deps,
        grid=(),
        in_specs=[whole] * 3,
        out_specs=pl.BlockSpec((rows, 3 * model), lambda: (0, 0)),
    )


def padded(vectors):
    return jnp.concatenate((jnp.stack(vectors), jnp.zeros((8 - len(vectors), vectors[0].shape[0]), f32)))


def per_device(
    hidden_in,
    starts,
    w_query,
    w_key,
    w_value,
    w_output,
    w_expand,
    w_reduce,
    bias_query,
    bias_value,
    bias_output,
    bias_expand,
    bias_reduce,
    attention_gain,
    attention_shift,
    feedforward_gain,
    feedforward_shift,
    cotangent,
):
    Order.last = ()
    tokens, model = hidden_in.shape[1:]
    head_size = model // HEADS
    ctx_size = lax.axis_size("ctx")
    length = tokens * ctx_size
    near = min(ctx_size, HEADS)
    copies = ctx_size // near
    heads = HEADS // near
    width = heads * head_size
    shard = w_query.shape[0]
    ff_block = w_reduce.shape[0]
    documents = starts.shape[1]
    c = lax.axis_index("ctx").astype(jnp.int32)
    f = lax.axis_index("fsdp").astype(jnp.int32)
    group = c & (near - 1)

    inputs = hidden_in[0]
    feed_matrix = lax.all_gather(cast_feed(w_expand, w_reduce), "fsdp", axis=0, tiled=True)
    blocks = gather_ctx(cast_all(inputs))

    own_columns = jnp.concatenate(
        [
            lax.dynamic_slice_in_dim(m, group * width, width, 1) * scale
            for m, scale in ((w_query, query_scale), (w_key, 1.0), (w_value, 1.0))
        ],
        axis=1,
    ).astype(bf16)

    def gather_rows(own):
        across = swap(own, "fsdp", 2)
        return [own, swap(own, "fsdp", 1), across, swap(across, "fsdp", 1)]

    projection_parts = gather_rows(own_columns)

    output_parts = gather_rows(cast_all(w_output, [blocks[1], blocks[2], blocks[4]]))

    all_projection = lax.all_gather(
        cast_projections((w_query, w_key, w_value), ()), "fsdp", axis=0, tiled=True
    )

    order = c ^ lax.iota(jnp.int32, ctx_size)
    positions = (order[:, None] * tokens + lax.iota(jnp.int32, tokens)[None, :]).reshape(-1)
    docs = jnp.sum((starts[0][None, :] <= positions[:, None]).astype(jnp.int32), axis=1) - 1
    lane = lax.iota(jnp.int32, LANES - head_size)[None, :]
    same = docs[:, None] == lane
    query_docs = jnp.where((lane < documents) & ~same, masked_value, 0.0).astype(f32)
    key_docs = jnp.where(same | ((lane >= documents) & (lane < documents + 3)), 1.0, 0.0).astype(f32)
    own_bias = jnp.concatenate(
        (
            lax.dynamic_slice_in_dim(bias_query * query_scale, group * width, width, 0),
            jnp.zeros((width,), f32),
            lax.dynamic_slice_in_dim(bias_value, group * width, width, 0),
        )
    ).reshape(1, -1)
    attention_vectors = padded((bias_output, attention_gain, attention_shift))
    feed_vectors = padded((bias_reduce, feedforward_gain, feedforward_shift))

    queries, keys, values, keys_t, stream = project(
        blocks,
        0,
        projection_parts,
        own_bias,
        query_docs,
        key_docs,
        f,
        heads,
        head_size,
        length,
        None,
        (),
    )

    out, wide, back = attend(
        queries, keys, values, group, near, tokens, head_size, documents, output_parts[1:]
    )
    received = exchange(out, near)
    normed, normed_r, first_unit, first_inverse, attended_r = attention_norm(
        received, output_parts, inputs, attention_vectors, f, near
    )

    sibling_normed = swap(normed_r, "fsdp", 1)
    activated_r, slope, partial, other = feed_forward(
        normed_r, sibling_normed, feed_matrix, bias_expand.reshape(1, -1), f
    )
    layer_out, d_second, d_reduced_r, second_sums = second_norm(
        normed, partial, swap(other, "fsdp", 1), feed_vectors, cotangent[0]
    )
    sibling_reduced = swap(d_reduced_r, "fsdp", 1)

    d_expanded_r, bias_expand_sum, partial, other = feed_back(
        d_reduced_r, sibling_reduced, slope, feed_matrix, f
    )
    other = swap(other, "fsdp", 1)

    expand_send = expand_gradients(normed_r, sibling_normed, d_expanded_r, f, (2, 3), 1, shard)
    expand_received = swap(expand_send, "fsdp", 2)
    d_first, d_attention_r, first_sums, d_attended = first_norm_back(
        d_second,
        partial,
        other,
        first_unit,
        first_inverse,
        attention_vectors,
        output_parts,
        f,
        near,
    )
    douts = exchange(d_attended, near)
    output_keep, output_send = output_gradient(
        attended_r, d_attention_r, first_sums, second_sums, bias_expand_sum, f, shard
    )
    output_received = swap(output_send, "fsdp", 1)
    low = c & 1
    reduce_send = reduce_gradient(activated_r, d_reduced_r, sibling_reduced, 1 - low, [douts])
    reduce_received = swap(reduce_send, "ctx", 1)

    rest = (2 * shard, 2 * shard + 16)
    d_query, d_key, d_value = attend_back(
        back, douts, wide, keys, values, keys_t, head_size, tokens, group
    )
    count = ctx_size
    while count > near:
        count //= 2
        received = [
            swap(d[count * tokens :].astype(bf16), "ctx", count).astype(f32) for d in (d_key, d_value)
        ]
        d_key = d_key[: count * tokens] + received[0]
        d_value = d_value[: count * tokens] + received[1]
    d_all, d_send = head_grads([d_query], d_key, d_value, tokens, near, group)
    d_mine = exchange(d_send, near)
    output_keep, output_send = add_parts(
        output_keep, output_received, [[(0, shard), rest], [(shard, 2 * shard), rest]]
    )
    output_received = swap(output_send, "fsdp", 2)
    expand_keep = expand_gradients(
        normed_r, sibling_normed, d_expanded_r, f, (0, 1), 0, shard
    )
    (expand_send,) = add_parts(expand_keep, expand_received, [[(2 * shard, 4 * shard)]])
    expand_other = swap(expand_send, "fsdp", 1)

    send, keep = projection_gradients(stream, d_all, f, shard)
    received = swap(send, "fsdp", 1)
    cut = ff_block // 2
    reduce_keep = reduce_gradient(activated_r, d_reduced_r, sibling_reduced, low)
    reduce_keep, reduce_send = add_parts(
        reduce_keep, reduce_received, [[(0, cut)], [(cut, 2 * cut)]]
    )
    reduce_received = swap(reduce_send, "fsdp", 2)
    send, keep = add_parts(keep, received, [[(0, shard), rest], [(shard, 2 * shard), rest]])
    received = swap(send, "fsdp", 2)
    expander = CtxSum(
        ctx_groups(2),
        ([expand_keep, expand_received], 0, 2 * shard),
        ([expand_other], 0, 2 * shard),
        ([output_keep, output_received], 0, shard),
    )
    expander.step()
    mine = sum_all([keep, received])
    count = ctx_size
    while count > near:
        count //= 2
        mine = sum_all([mine, swap(mine, "ctx", count)])
    reducer = CtxSum(ctx_groups()[1:], ([reduce_keep, reduce_received], 0, cut))
    reducer.step([d_mine])
    expander.step()
    reducer.step()
    input_grad = input_gradient(d_first, d_mine, all_projection, near)
    reduced, expanded = reducer.finish(), expander.finish()
    gathered = lax.all_gather(stack_sums(reduced, expanded), "ctx", axis=0, tiled=True)
    (vectors,) = add_parts(output_keep, output_received, [[(shard, shard + 16)]])
    for bit, _ in ctx_groups():
        vectors = sum_all([vectors, swap(vectors, "ctx", 1 << bit)])
    grad_query, grad_key, grad_value, grad_bias_query, grad_bias_value = place_projections(
        gather_small(mine, near), jnp.stack((group, f)), shard, width, shard
    )
    grad_w_reduce, grad_w_expand, grad_w_output, *small = place_gradients(
        gathered, vectors, f, shard, reduced[0].shape[0], ctx_size
    )
    (
        grad_bias_query,
        grad_bias_value,
        grad_att_gain,
        grad_att_shift,
        grad_bias_output,
        grad_ff_gain,
        grad_ff_shift,
        grad_bias_reduce,
        grad_bias_expand,
    ) = [v.reshape(-1) for v in (grad_bias_query, grad_bias_value, *small)]

    return (
        layer_out[None],
        input_grad[None],
        grad_query,
        grad_key,
        grad_value,
        grad_w_output,
        grad_w_expand,
        grad_w_reduce,
        grad_bias_query,
        grad_bias_value,
        grad_bias_output,
        grad_bias_expand,
        grad_bias_reduce,
        grad_att_gain,
        grad_att_shift,
        grad_ff_gain,
        grad_ff_shift,
    )


def solution(mesh):
    rows = P("fsdp", None)
    activations = P("fsdp", "ctx", None)
    return jax.shard_map(
        per_device,
        mesh=mesh,
        in_specs=(activations,) + (rows,) * 7 + (P(),) * 9 + (activations,),
        out_specs=(activations, activations) + (rows,) * 6 + (P("fsdp"),) * 9,
        check_vma=False,
    )
```
